128 devices in a mesh: gx: 8 (over z, y_hi), gy: 16 (over x, y_lo, core).
Axes of the slice: x: 4, y: 4 (y_hi: 2, y_lo: 2; y = y_hi * 2 + y_lo), z: 4, core: 2. Of those that a mesh axis runs over, the one named last changes fastest.
Arguments:
- forcing: float32 [16, 256, 1024], P(None, 'gy', 'gx'), may hold values from -6 to 6
- pressure_in: float32 [16, 256, 1024], P(None, 'gy', 'gx'), may hold values from -6 to 6
- x_coupling: float32 [16, 256, 1024], P(None, 'gy', 'gx'), may hold values from 0.5 to 2000
- y_coupling: float32 [16, 256, 1024], P(None, 'gy', 'gx'), may hold values from 0.5 to 2000
- z_coupling: float32 [16, 256, 1024], P(None, 'gy', 'gx'), may hold values from 0.05 to 0.5
- damping: float32 [16, 256, 1024], P(None, 'gy', 'gx'), may hold values from 0.2 to 2
Outputs:
- pressure: float32 [16, 256, 1024], P(None, 'gy', 'gx')
- coarse_residual: float32 [8, 128, 512], P(None, 'gy', 'gx')
- coarse_correction: float32 [8, 128, 512], P(None, 'gy')
The draws below stay inside these ranges and needn't reach their ends.
All inputs are finite; a program needn't handle non-finite values.
Results may differ from the reference program's by a relative error of at most 0.0001.
Values sent between devices are 32-bit elements; how exact they have to be, the bound alone decides.
No kernel may reach another device: no remote copies, remote signals or barrier semaphores. Data moves between devices by JAX's collectives and lax.ppermute only.
A program may use at most 128 MiB of HBM per device.

```python
import math
import jax
import jax.numpy as jnp
from jax import lax

NZ = 16
COARSE = 3
NX = 1024
NY = 256


def coupling_draw(key, shape, flag_shape):
    base_key, flag_key = jax.random.split(key)
    base = jnp.exp(jax.random.uniform(base_key, shape, jnp.float32, math.log(0.5), math.log(2.0)))
    base = jnp.clip(base, 0.5, 2.0)
    strong = jax.random.uniform(flag_key, flag_shape, jnp.float32) < 0.5
    return base * jnp.where(strong, 1000.0, 1.0)


def draw_x_coupling(key, part):
    return coupling_draw(jax.random.fold_in(key, 11), (NZ, NY, NX), (NZ, NY, 1))


def draw_y_coupling(key, part):
    return coupling_draw(jax.random.fold_in(key, 23), (NZ, NY, NX), (NZ, 1, NX))


def block_scale(key, extent, pieces, smallest, top_value):
    loudness = 1.0
    for position, blocks in pieces:
        steps = jax.random.uniform(jax.random.fold_in(jax.random.fold_in(key, 6), position), (blocks,), jnp.float32, smallest / len(pieces), top_value / len(pieces))
        loudness = loudness * jnp.repeat(jnp.exp(steps), extent[position] // blocks).reshape((-1,) + (1,) * (len(extent) - 1 - position))
    return loudness


def gaussian(key, extent, scale, limit, cuts=(), kind=jnp.bfloat16):
    values = scale * jax.random.normal(key, extent, jnp.float32)
    if cuts:
        values = values * block_scale(key, extent, cuts, -0.22, 0.18)
    return jnp.clip(values, -limit, limit).astype(kind)


def setup_inputs(seed: int = 0) -> dict:
    key_of = jax.random.split(jax.random.key(seed), 7)
    forcing = gaussian(key_of[0], (NZ, NY, NX), 1.0, 6.0, ((1, 16), (2, 8)), jnp.float32)
    pressure_in = gaussian(key_of[1], (NZ, NY, NX), 1.0, 6.0, ((1, 16), (2, 8)), jnp.float32)
    x_coupling = draw_x_coupling(jax.random.fold_in(key_of[6], 71), 0)
    y_coupling = draw_y_coupling(jax.random.fold_in(key_of[6], 71), 0)
    z_coupling = jnp.clip(jnp.exp(math.log(0.5) - 2.3025851 * jax.random.uniform(key_of[4], (NZ, NY, NX), jnp.float32) ** block_scale(key_of[4], (NZ, NY, NX), ((1, 16), (2, 8)), -0.2, 0.2)), 0.05, 0.5)
    damping = jnp.clip(jnp.exp(math.log(2.0) - 2.3025851 * jax.random.uniform(key_of[5], (NZ, NY, NX), jnp.float32) ** block_scale(key_of[5], (NZ, NY, NX), ((1, 16), (2, 8)), -0.2, 0.2)), 0.2, 2.0)
    return {"forcing": forcing, "pressure_in": pressure_in, "x_coupling": x_coupling, "y_coupling": y_coupling, "z_coupling": z_coupling, "damping": damping}


RELAX = 0.8


def shifted(values, offset, axis_dim, filler):
    length = values.shape[axis_dim]
    if offset > 0:
        border = jnp.full_like(lax.slice_in_dim(values, 0, offset, axis=axis_dim), filler)
        return jnp.concatenate([border, lax.slice_in_dim(values, 0, length - offset, axis=axis_dim)], axis=axis_dim)
    amount = -offset
    border = jnp.full_like(lax.slice_in_dim(values, 0, amount, axis=axis_dim), filler)
    return jnp.concatenate([lax.slice_in_dim(values, amount, length, axis=axis_dim), border], axis=axis_dim)


def line_solve(low_band, diagonal, up_band, right_side, axis_dim):
    length = right_side.shape[axis_dim]
    stride = 1
    while stride < length:
        before = shifted(diagonal, stride, axis_dim, 1.0)
        after = shifted(diagonal, -stride, axis_dim, 1.0)
        weight_low = -low_band / before
        weight_up = -up_band / after
        new_diag = diagonal + weight_low * shifted(up_band, stride, axis_dim, 0.0) + weight_up * shifted(low_band, -stride, axis_dim, 0.0)
        new_right = right_side + weight_low * shifted(right_side, stride, axis_dim, 0.0) + weight_up * shifted(right_side, -stride, axis_dim, 0.0)
        low_band = weight_low * shifted(low_band, stride, axis_dim, 0.0)
        up_band = weight_up * shifted(up_band, -stride, axis_dim, 0.0)
        diagonal = new_diag
        right_side = new_right
        stride = stride * 2
    return right_side / diagonal


def top_masked(coupling):
    levels = coupling.shape[0]
    keep = (jnp.arange(levels) < levels - 1)[:, None, None]
    return jnp.where(keep, coupling, jnp.zeros_like(coupling))


def vertical(field, z_low, z_top):
    return z_low * shifted(field, 1, 0, 0.0) + z_top * shifted(field, -1, 0, 0.0)


def restrict(field):
    levels, rows, columns = field.shape
    blocks = field.reshape(levels // 2, 2, rows // 2, 2, columns // 2, 2)
    return jnp.sum(blocks, axis=(1, 3, 5)) * 0.125


def reference(forcing, pressure_in, x_coupling, y_coupling, z_coupling, damping):
    z_top = top_masked(z_coupling)
    z_low = shifted(z_top, 1, 0, 0.0)
    x_left = shifted(x_coupling, 1, 2, 0.0)
    y_left = shifted(y_coupling, 1, 1, 0.0)
    diagonal = x_left + x_coupling + y_left + y_coupling + z_low + z_top + damping
    field = pressure_in
    for repeat in range(2):
        source = forcing + y_left * shifted(field, 1, 1, 0.0) + y_coupling * shifted(field, -1, 1, 0.0) + vertical(field, z_low, z_top)
        field = line_solve(-x_left, diagonal, -x_coupling, source, 2)
        source = forcing + x_left * shifted(field, 1, 2, 0.0) + x_coupling * shifted(field, -1, 2, 0.0) + vertical(field, z_low, z_top)
        field = line_solve(-y_left, diagonal, -y_coupling, source, 1)
    applied = diagonal * field - x_left * shifted(field, 1, 2, 0.0) - x_coupling * shifted(field, -1, 2, 0.0) - y_left * shifted(field, 1, 1, 0.0) - y_coupling * shifted(field, -1, 1, 0.0) - vertical(field, z_low, z_top)
    coarse_residual = restrict(forcing - applied)
    coarse_x = restrict(x_coupling)
    coarse_y = restrict(y_coupling)
    coarse_z = restrict(z_coupling)
    coarse_damp = restrict(damping)
    cz_top = top_masked(coarse_z)
    cz_low = shifted(cz_top, 1, 0, 0.0)
    cx_left = shifted(coarse_x, 1, 2, 0.0)
    cy_left = shifted(coarse_y, 1, 1, 0.0)
    coarse_diag = cx_left + coarse_x + cy_left + coarse_y + cz_low + cz_top + coarse_damp
    correction = RELAX * coarse_residual / coarse_diag
    for repeat in range(COARSE - 1):
        applied_coarse = coarse_diag * correction - cx_left * shifted(correction, 1, 2, 0.0) - coarse_x * shifted(correction, -1, 2, 0.0) - cy_left * shifted(correction, 1, 1, 0.0) - coarse_y * shifted(correction, -1, 1, 0.0) - vertical(correction, cz_low, cz_top)
        correction = correction + RELAX * (coarse_residual - applied_coarse) / coarse_diag
    return (field, coarse_residual, correction)
```

```python
import functools

import jax
import jax.numpy as jnp
from jax import lax
from jax.experimental import pallas as pl
from jax.experimental.pallas import tpu as pltpu
from jax.sharding import PartitionSpec as P

RELAX = 0.8
NK, NJ, NI = 16, 16, 128
ROWS = NK * NJ
GX, GY = 8, 16
STEPS = (1, 2, 4, 8, 16, 32, 64)
F32 = jnp.float32


def sds(*shape):
    return jax.ShapeDtypeStruct(shape, F32)


def call(kernel, outs, *args, scratch=()):
    spec = pl.BlockSpec(memory_space=pltpu.VMEM)
    return pl.pallas_call(
        kernel,
        out_shape=outs,
        in_specs=[spec] * len(args),
        out_specs=[spec] * len(outs),
        scratch_shapes=[pltpu.VMEM(s, F32) for s in scratch],
        compiler_params=pltpu.CompilerParams(vmem_limit_bytes=16 * 1024 * 1024),
    )(*args)


def lanes(rows, width=NI):
    return lax.broadcasted_iota(jnp.int32, (rows, width), 1)


def rolled(value, amount, axis):
    return pltpu.roll(value, amount % value.shape[axis], axis)


def level(ref, k):
    return ref[pl.ds(k * NJ, NJ), :]


def across(ref, j, count=NK, stride=NJ):
    return ref[pl.ds(j, count, stride=stride), :]


def column(value, k):
    return jnp.broadcast_to(value[:, k : k + 1], (value.shape[0], NI))


def z_pair(zc, k):
    return (level(zc, k - 1) if k > 0 else None, level(zc, k) if k < NK - 1 else None)


def z_sum(zc, k, base):
    low, top = z_pair(zc, k)
    if low is not None:
        base = base + low
    if top is not None:
        base = base + top
    return base


def z_terms(zc, field, k, base):
    low, top = z_pair(zc, k)
    if low is not None:
        base = base + low * level(field, k - 1)
    if top is not None:
        base = base + top * level(field, k + 1)
    return base


def y_left_of(yc, halo, k):
    row = lax.broadcasted_iota(jnp.int32, (NJ, NI), 0)
    return jnp.where(row == 0, halo[pl.ds(k, 1), :], rolled(level(yc, k), 1, 0))


def squeeze(values, scale=0.125):
    source = lax.broadcasted_iota(jnp.int32, (NI, NI), 0)
    target = lax.broadcasted_iota(jnp.int32, (NI, NI), 1)
    matrix = jnp.where(source // 2 == target, scale, 0.0).astype(F32)
    return jnp.dot(values, matrix, precision=lax.Precision.HIGHEST, preferred_element_type=F32)


def edges(values, scale=0.125):
    source = lax.broadcasted_iota(jnp.int32, (NI, NI), 0)
    target = lax.broadcasted_iota(jnp.int32, (NI, NI), 1)
    hit = ((source == NI - 1) & (target == 64)) | ((source == 0) & (target == NI - 1))
    matrix = jnp.where(hit, scale, 0.0).astype(F32)
    return jnp.dot(values, matrix, precision=lax.Precision.HIGHEST, preferred_element_type=F32)


def parity_shift(values):
    odd = lax.rem(lax.axis_index("gx"), 2) == 1
    return jnp.where(odd, rolled(values, 64, 1), values)


def store_coarse(out, base, tmp):
    for J in range(NJ // 2):
        out[pl.ds(base + J * 8, 8), :] = across(tmp, 2 * J, 8) + across(tmp, 2 * J + 1, 8)


def first_kernel(p, xc, yc, zc, dp, up, down, coarse, tmp):
    up[pl.ds(0, NK), :] = across(yc, NJ - 1)
    up[pl.ds(NK, NK), :] = across(p, NJ - 1)
    down[pl.ds(0, NK), :] = across(p, 0)
    for q, ref in enumerate((xc, yc, zc, dp)):
        pairs = jnp.concatenate([level(ref, 2 * K) + level(ref, 2 * K + 1) for K in range(NK // 2)], axis=0)
        tmp[...] = parity_shift(squeeze(pairs))
        store_coarse(coarse, q * 64, tmp)
        up[pl.ds(2 * NK + q * 24, 24), :] = coarse[pl.ds(q * 64 + 40, 24), :]
        down[pl.ds(NK + q * 16, 16), :] = coarse[pl.ds(q * 64, 16), :]


def x_first_kernel(f, p, xc, yc, zc, dp, below, above, g, a, b, mult, send):
    d = lax.axis_index("gx")
    lane = lanes(NJ)
    row = lax.broadcasted_iota(jnp.int32, (NJ, NI), 0)
    inner = jnp.logical_or(lane < NI - 1, d == GX - 1)
    packed = jnp.zeros((NJ, NI), F32)
    group = 2
    for k0 in range(0, NK, group):
        diag, off, rhs = [], [], []
        for k in range(k0, k0 + group):
            x, y, v = level(xc, k), level(yc, k), level(p, k)
            y_left = y_left_of(yc, below, k)
            before = jnp.where(row == 0, below[pl.ds(NK + k, 1), :], rolled(v, 1, 0))
            after = jnp.where(row == NJ - 1, above[pl.ds(k, 1), :], rolled(v, -1, 0))
            rest = z_sum(zc, k, y_left + y + level(dp, k))
            x_left = jnp.where(lane == 0, 0.0, rolled(x, 1, 1))
            diag.append(x_left + jnp.where(inner, x, 0.0) + rest)
            off.append(jnp.where(lane == NI - 1, 0.0, -x))
            rhs.append(z_terms(zc, p, k, level(f, k) + y_left * before + y * after))
        diag, off, rhs = (jnp.concatenate(v, axis=0) for v in (diag, off, rhs))
        wide = lanes(group * NJ)
        left = jnp.where(wide == 0, 1.0, 0.0).astype(F32)
        right = jnp.where(wide == NI - 1, 1.0, 0.0).astype(F32)
        place = pl.ds(k0 * NJ, group * NJ)
        for n, s in enumerate(STEPS):
            inv = 1.0 / diag
            low = rolled(off, s, 1)
            alpha = -low * rolled(inv, s, 1)
            beta = -off * rolled(inv, -s, 1)
            mult[2 * n, place, :] = alpha
            mult[2 * n + 1, place, :] = beta
            diag = diag + alpha * low + beta * off
            off = beta * rolled(off, -s, 1)
            rhs = rhs + alpha * rolled(rhs, s, 1) + beta * rolled(rhs, -s, 1)
            left = left + alpha * rolled(left, s, 1) + beta * rolled(left, -s, 1)
            right = right + alpha * rolled(right, s, 1) + beta * rolled(right, -s, 1)
        inv = 1.0 / diag
        mult[2 * len(STEPS), place, :] = inv
        rhs, left, right = rhs * inv, left * inv, right * inv
        g[place, :], a[place, :], b[place, :] = rhs, left, right
        for k in range(k0, k0 + group):
            part = slice((k - k0) * NJ, (k - k0 + 1) * NJ)
            picks = (
                column(rhs[part], 0),
                column(rhs[part], NI - 1),
                column(left[part], 0),
                column(right[part], 0),
                column(right[part], NI - 1),
                column(level(xc, k), NI - 1),
            )
            for q, pick in enumerate(picks):
                packed = jnp.where(lane == q * NK + k, pick, packed)
    send[...] = packed


def x_second_solve(rhs, mult, place):
    for n, s in enumerate(STEPS):
        rhs = rhs + mult[2 * n, place, :] * rolled(rhs, s, 1) + mult[2 * n + 1, place, :] * rolled(rhs, -s, 1)
    return rhs * mult[2 * len(STEPS), place, :]


def x_fluxes(fs, source, low, inv, up):
    zero = jnp.zeros((NJ, NI), F32)
    fs[0], fs[GX] = zero, zero
    forward = [source(0)]
    for d in range(1, GX - 1):
        forward.append(source(d) + low[d] * forward[-1])
    value = forward[-1] * inv[GX - 2]
    fs[GX - 1] = value
    for d in range(GX - 3, -1, -1):
        value = forward[d] * inv[d] + up[d] * value
        fs[1 + d] = value


def x_finish(fs, g, a, b, field):
    d = lax.axis_index("gx")
    flux_left, flux_right = fs[d], fs[d + 1]
    for k in range(NK):
        field[pl.ds(k * NJ, NJ), :] = (
            level(g, k) - level(a, k) * column(flux_left, k) + level(b, k) * column(flux_right, k)
        )
    return flux_left, flux_right


def y_source(f, xc, zc, field, fluxes, c_left, k):
    d = lax.axis_index("gx")
    lane = lanes(NJ)
    flux_left, flux_right = fluxes
    v, x = level(field, k), level(xc, k)
    before = jnp.where(lane == 0, column(c_left, k) * v - column(flux_left, k), rolled(x * v, 1, 1))
    last = jnp.where(d == GX - 1, 0.0, x * v + column(flux_right, k))
    after = jnp.where(lane == NI - 1, last, x * rolled(v, -1, 1))
    return z_terms(zc, field, k, level(f, k) + before + after)


def y_first_kernel(f, xc, yc, zc, dp, below, got, g, a, b, yg, ya, yb, yw, yinv, xred, cl, send, fs, cs, field, src, base):
    d = lax.axis_index("gx")
    e = lax.axis_index("gy")
    lane = lanes(NJ)
    part = lambda n, q: rolled(got[n], -NK * q, 1)
    m = [part(n, 3) for n in range(GX)]
    low, inv, up = [None], [], []
    for n in range(GX - 1):
        dd = part(n, 4) + 1.0 / part(n, 5) + part(n + 1, 2)
        if n:
            low.append(m[n] * inv[-1])
            dd = dd - low[n] * m[n]
        inv.append(1.0 / dd)
        up.append(m[n + 1] * inv[n])
        xred[n], xred[GX + n], xred[2 * GX + n] = (low[n] if n else jnp.zeros_like(dd)), inv[n], up[n]
    x_fluxes(fs, lambda n: part(n + 1, 0) - part(n, 1), low, inv, up)
    cs[0] = jnp.zeros((NJ, NI), F32)
    for n in range(GX):
        cs[n + 1] = part(n, 5)
    c_left = cs[d]
    cl[...] = c_left
    fluxes = x_finish(fs, g, a, b, field)
    for k in range(NK):
        src[pl.ds(k * NJ, NJ), :] = y_source(f, xc, zc, field, fluxes, c_left, k)
        x = level(xc, k)
        x_left = jnp.where(lane == 0, column(c_left, k), rolled(x, 1, 1))
        base[pl.ds(k * NJ, NJ), :] = z_sum(zc, k, x_left + x + level(dp, k))
    ys, ws, invs, spike = [], [None], [], []
    for j in range(NJ):
        y = across(yc, j)
        diag = across(base, j)
        if j < NJ - 1:
            diag = diag + y
        else:
            diag = diag + jnp.where(e == GY - 1, y, 0.0)
        rhs = across(src, j)
        if j:
            y_before = across(yc, j - 1)
            w = y_before * invs[-1]
            ws.append(w)
            diag = diag + y_before - w * y_before
            rhs = rhs + w * ys[-1]
            spike.append(w * spike[-1])
            yw[pl.ds(j * NK, NK), :] = w
        else:
            spike.append(jnp.ones((NK, NI), F32))
            yw[pl.ds(0, NK), :] = jnp.zeros((NK, NI), F32)
        ys.append(rhs)
        invs.append(1.0 / diag)
        yinv[pl.ds(j * NK, NK), :] = invs[-1]
    for j in range(NJ - 1, -1, -1):
        if j == NJ - 1:
            gv, av, bv = ys[j] * invs[j], spike[j] * invs[j], invs[j]
            send[pl.ds(NK, NK), :] = gv
            send[pl.ds(4 * NK, NK), :] = bv + 1.0 / across(yc, j)
        else:
            w = ws[j + 1]
            gv, av, bv = ys[j] * invs[j] + w * gv, spike[j] * invs[j] + w * av, w * bv
        place = pl.ds(j * NK, NK)
        yg[place, :], ya[place, :], yb[place, :] = gv, av, bv
    send[pl.ds(0, NK), :] = gv
    send[pl.ds(2 * NK, NK), :] = av
    send[pl.ds(3 * NK, NK), :] = bv


def y_fluxes(fs, source, low, inv, up):
    zero = jnp.zeros((NK, NI), F32)
    fs[0], fs[GY] = zero, zero
    forward = [source(0)]
    for n in range(1, GY - 1):
        forward.append(source(n) + low(n) * forward[-1])
    value = forward[-1] * inv(GY - 2)
    fs[GY - 1] = value
    for n in range(GY - 3, -1, -1):
        value = forward[n] * inv(n) + up(n) * value
        fs[1 + n] = value


def y_finish(fs, yc, below, yg, ya, yb, field, terms):
    e = lax.axis_index("gy")
    flux_left, flux_right = fs[e], fs[e + 1]
    block = lambda ref, j: ref[pl.ds(j * NK, NK), :]
    p = [block(yg, j) - block(ya, j) * flux_left + block(yb, j) * flux_right for j in range(NJ)]
    for j in range(NJ):
        y = across(yc, j)
        if j:
            before = across(yc, j - 1) * p[j - 1]
        else:
            before = below[pl.ds(0, NK), :] * p[0] - flux_left
        if j < NJ - 1:
            after = y * p[j + 1]
        else:
            after = jnp.where(e == GY - 1, 0.0, y * p[j] + flux_right)
        field[pl.ds(j, NK, stride=NJ), :] = p[j]
        terms[pl.ds(j, NK, stride=NJ), :] = before + after


def x_again_kernel(f, yc, zc, below, got, yg, ya, yb, mult, g, yred, send, fs, field, terms):
    part = lambda n, q: got[n, pl.ds(q * NK, NK), :]
    prev = None
    for n in range(GY - 1):
        dd = part(n, 4) + part(n + 1, 2)
        if n:
            m = part(n, 3)
            low = m * prev
            dd = dd - low * m
            yred[n] = low
        else:
            yred[n] = jnp.zeros_like(dd)
        prev = 1.0 / dd
        yred[GY + n] = prev
        yred[2 * GY + n] = part(n + 1, 3) * prev
    yred[GY - 1] = jnp.zeros((NK, NI), F32)
    yred[2 * GY - 1] = jnp.zeros((NK, NI), F32)
    yred[3 * GY - 1] = jnp.zeros((NK, NI), F32)
    y_fluxes(
        fs,
        lambda n: part(n + 1, 0) - part(n, 1),
        lambda n: yred[n],
        lambda n: yred[GY + n],
        lambda n: yred[2 * GY + n],
    )
    y_finish(fs, yc, below, yg, ya, yb, field, terms)
    lane = lanes(NJ)
    packed = jnp.zeros((NJ, NI), F32)
    group = 2
    for k0 in range(0, NK, group):
        rhs = jnp.concatenate(
            [z_terms(zc, field, k, level(f, k) + level(terms, k)) for k in range(k0, k0 + group)], axis=0
        )
        place = pl.ds(k0 * NJ, group * NJ)
        rhs = x_second_solve(rhs, mult, place)
        g[place, :] = rhs
        for k in range(k0, k0 + group):
            mine = rhs[(k - k0) * NJ : (k - k0 + 1) * NJ]
            packed = jnp.where(lane == k, column(mine, 0), packed)
            packed = jnp.where(lane == NK + k, column(mine, NI - 1), packed)
    send[...] = packed


def y_again_kernel(f, xc, zc, got, g, a, b, xred, cl, yw, yinv, yg, send, fs, field, src):
    part = lambda n, q: rolled(got[n], -NK * q, 1)
    x_fluxes(
        fs,
        lambda n: part(n + 1, 0) - part(n, 1),
        [xred[n] for n in range(GX - 1)],
        [xred[GX + n] for n in range(GX - 1)],
        [xred[2 * GX + n] for n in range(GX - 1)],
    )
    fluxes = x_finish(fs, g, a, b, field)
    c_left = cl[...]
    for k in range(NK):
        src[pl.ds(k * NJ, NJ), :] = y_source(f, xc, zc, field, fluxes, c_left, k)
    block = lambda ref, j: ref[pl.ds(j * NK, NK), :]
    ys = []
    for j in range(NJ):
        rhs = across(src, j)
        if j:
            rhs = rhs + block(yw, j) * ys[-1]
        ys.append(rhs)
    value = None
    for j in range(NJ - 1, -1, -1):
        new = ys[j] * block(yinv, j)
        value = new if value is None else new + block(yw, j + 1) * value
        yg[pl.ds(j * NK, NK), :] = value
        if j == NJ - 1:
            send[pl.ds(NK, NK), :] = value
    send[pl.ds(0, NK), :] = value


def residual_kernel(f, xc, yc, zc, dp, below, got, yg, ya, yb, yred, cl, field, coarse, fs, terms, tmp):
    d = lax.axis_index("gx")
    lane = lanes(NJ)
    part = lambda n, q: got[n, pl.ds(q * NK, NK), :]
    y_fluxes(
        fs,
        lambda n: part(n + 1, 0) - part(n, 1),
        lambda n: yred[n],
        lambda n: yred[GY + n],
        lambda n: yred[2 * GY + n],
    )
    y_finish(fs, yc, below, yg, ya, yb, field, terms)
    c_left = cl[...]
    main, rim = [], []
    for k in range(NK):
        v, x = level(field, k), level(xc, k)
        left = column(c_left, k)
        x_left = jnp.where(lane == 0, left, rolled(x, 1, 1))
        diag = z_sum(zc, k, x_left + x + y_left_of(yc, below, k) + level(yc, k) + level(dp, k))
        around = jnp.where(lane == 0, 0.0, x_left * rolled(v, 1, 1)) + jnp.where(lane == NI - 1, 0.0, x * rolled(v, -1, 1))
        main.append(level(f, k) - (diag * v - around - level(terms, k) - z_terms(zc, field, k, jnp.zeros((NJ, NI), F32))))
        last = jnp.where(d == GX - 1, 0.0, x * v)
        rim.append(jnp.where(lane == 0, left * v, jnp.where(lane == NI - 1, last, 0.0)))
    pairs = jnp.concatenate([main[2 * K] + main[2 * K + 1] for K in range(NK // 2)], axis=0)
    outer = jnp.concatenate([rim[2 * K] + rim[2 * K + 1] for K in range(NK // 2)], axis=0)
    tmp[...] = parity_shift(squeeze(pairs) + edges(outer))
    store_coarse(coarse, 0, tmp)


def coarse_kernel(got, coef, res_out, cor_out, tmp, cor_tmp):
    d = lax.axis_index("gx")
    e = lax.axis_index("gy")
    lane = lanes(8)
    wide = lanes(8, 4 * NI)
    level_k = lax.broadcasted_iota(jnp.int32, (8, 4 * NI), 0)

    def whole_res(J):
        rows = pl.ds(J * 8, 8)
        outs = []
        for m in range(4):
            value = jnp.where(lane <= 64, got[2 * m, rows, :], 0.0) + jnp.where(lane >= 63, got[2 * m + 1, rows, :], 0.0)
            if m > 0:
                value = value + jnp.where(lane == 0, got[2 * m - 1, rows, :], 0.0)
            if m < 3:
                value = value + jnp.where(lane == NI - 1, got[2 * m + 2, rows, :], 0.0)
            outs.append(value)
        return outs

    def whole_coef(q, J):
        rows = pl.ds(q * 104 + J * 8, 8)
        return jnp.concatenate([coef[2 * m, rows, :] + coef[2 * m + 1, rows, :] for m in range(4)], axis=1)

    res, diag, weight, cxl, cxi, cyl, cyr, czl, czt = ([] for _ in range(9))
    for J in range(12):
        outs = whole_res(J)
        if 2 <= J < 10:
            mine = outs[0]
            for m in range(1, 4):
                mine = jnp.where(d // 2 == m, outs[m], mine)
            mine = jnp.where(lax.rem(d, 2) == 1, rolled(mine, 64, 1), mine)
            tmp[pl.ds(J - 2, 8, stride=8), :] = mine
        res.append(jnp.concatenate(outs, axis=1))
        x, y, z, damp = (whole_coef(q, J + 1) for q in range(4))
        y_before = whole_coef(1, J)
        x_left = jnp.where(wide == 0, 0.0, rolled(x, 1, 1))
        z_top = jnp.where(level_k == 7, 0.0, z)
        z_low = rolled(z_top, 1, 0)
        total = x_left + x + y_before + y + z_low + z_top + damp
        at = e * 8 + J - 2
        valid = jnp.logical_and(at >= 0, at < 8 * GY)
        total = jnp.where(valid, total, 1.0)
        diag.append(total)
        weight.append(jnp.where(valid, RELAX / total, 0.0))
        cxl.append(x_left)
        cxi.append(jnp.where(wide == 4 * NI - 1, 0.0, x))
        cyl.append(y_before)
        cyr.append(y)
        czl.append(z_low)
        czt.append(z_top)
    cor = {J: weight[J] * res[J] for J in range(12)}
    for low, high in ((1, 11), (2, 10)):
        new = {}
        for J in range(low, high):
            v = cor[J]
            applied = (
                diag[J] * v
                - cxl[J] * rolled(v, 1, 1)
                - cxi[J] * rolled(v, -1, 1)
                - cyl[J] * cor[J - 1]
                - cyr[J] * cor[J + 1]
                - (czl[J] * rolled(v, 1, 0) + czt[J] * rolled(v, -1, 0))
            )
            new[J] = v + weight[J] * (res[J] - applied)
        cor = new
    for J in range(8):
        for m in range(4):
            cor_tmp[m, pl.ds(J, 8, stride=8), :] = cor[J + 2][:, m * NI : (m + 1) * NI]
    for m in range(4):
        cor_out[:, pl.ds(m * NI, NI)] = cor_tmp[m]
    res_out[...] = tmp[:, :64]


def spread(value, axis, count):
    many = jnp.broadcast_to(value[None], (count,) + value.shape)
    return lax.all_to_all(many, axis, split_axis=0, concat_axis=0, tiled=True)


def body(forcing, pressure_in, x_coupling, y_coupling, z_coupling, damping):
    f, p, xc, yc, zc, dp = (
        v.reshape(ROWS, NI) for v in (forcing, pressure_in, x_coupling, y_coupling, z_coupling, damping)
    )
    forth = [(n, n + 1) for n in range(GY - 1)]
    back = [(n + 1, n) for n in range(GY - 1)]
    whole = sds(ROWS, NI)
    up, down, coef = call(first_kernel, [sds(128, NI), sds(80, NI), sds(256, NI)], p, xc, yc, zc, dp, scratch=[(128, NI)])
    below = lax.ppermute(up, "gy", forth)
    above = lax.ppermute(down, "gy", back)
    g, a, b, mult, send = call(
        x_first_kernel,
        [whole, whole, whole, sds(2 * len(STEPS) + 1, ROWS, NI), sds(NJ, NI)],
        f, p, xc, yc, zc, dp, below, above,
    )
    got = spread(send, "gx", GX)
    coef_rows = jnp.concatenate(
        [below[32:].reshape(4, 24, NI), coef.reshape(4, 64, NI), above[16:].reshape(4, 16, NI)], axis=1
    ).reshape(416, NI)
    coef_all = lax.all_gather(coef_rows, "gx", axis=0, tiled=False)
    yg, ya, yb, yw, yinv, xred, cl, send = call(
        y_first_kernel,
        [whole] * 5 + [sds(3 * GX, NJ, NI), sds(NJ, NI), sds(5 * NK, NI)],
        f, xc, yc, zc, dp, below, got, g, a, b,
        scratch=[(GX + 1, NJ, NI), (GX + 1, NJ, NI), (ROWS, NI), (ROWS, NI), (ROWS, NI)],
    )
    got = spread(send, "gy", GY)
    g, yred, send = call(
        x_again_kernel,
        [whole, sds(3 * GY, NK, NI), sds(NJ, NI)],
        f, yc, zc, below, got, yg, ya, yb, mult,
        scratch=[(GY + 1, NK, NI), (ROWS, NI), (ROWS, NI)],
    )
    got = spread(send, "gx", GX)
    yg, send = call(
        y_again_kernel,
        [whole, sds(2 * NK, NI)],
        f, xc, zc, got, g, a, b, xred, cl, yw, yinv,
        scratch=[(GX + 1, NJ, NI), (ROWS, NI), (ROWS, NI)],
    )
    got = spread(send, "gy", GY)
    field, coarse = call(
        residual_kernel,
        [whole, sds(64, NI)],
        f, xc, yc, zc, dp, below, got, yg, ya, yb, yred, cl,
        scratch=[(GY + 1, NK, NI), (ROWS, NI), (128, NI)],
    )
    lower = lax.ppermute(coarse[48:], "gy", forth)
    upper = lax.ppermute(coarse[:16], "gy", back)
    got = spread(jnp.concatenate([lower, coarse, upper], axis=0), "gx", GX)
    res, cor = call(
        coarse_kernel, [sds(64, 64), sds(64, 512)], got, coef_all, scratch=[(64, NI), (4, 64, NI)]
    )
    return field.reshape(NK, NJ, NI), res.reshape(8, 8, 64), cor.reshape(8, 8, 512)


def solution(mesh):
    spec = P(None, "gy", "gx")
    return jax.shard_map(
        body, mesh=mesh, in_specs=(spec,) * 6, out_specs=(spec, spec, P(None, "gy", None)), check_vma=False
    )
```

```python
import functools

import jax
import jax.numpy as jnp
from jax import lax
from jax.experimental import pallas as pl
from jax.experimental.pallas import tpu as pltpu
from jax.sharding import PartitionSpec as P

RELAX = 0.8
NK, NJ, NI = 16, 16, 128
ROWS = NK * NJ
GX, GY = 8, 16
STEPS = (1, 2, 4, 8, 16, 32, 64)
F32 = jnp.float32


def sds(*shape):
    return jax.ShapeDtypeStruct(shape, F32)


def call(kernel, outs, *args, scratch=(), hbm=False, aliases={}, sems=0, flops=None):
    spec = pl.BlockSpec(memory_space=pltpu.VMEM)
    inside = pl.BlockSpec(memory_space=pltpu.HBM) if hbm else spec
    shapes = [pltpu.VMEM(v, F32) for v in scratch]
    if sems:
        shapes.append(pltpu.SemaphoreType.DMA((sems,)))
    cost = None if flops is None else pl.CostEstimate(flops=flops, bytes_accessed=1 << 20, transcendentals=0)
    return pl.pallas_call(
        kernel,
        out_shape=outs,
        in_specs=[inside] * len(args),
        out_specs=[spec] * len(outs),
        scratch_shapes=shapes,
        input_output_aliases=aliases,
        cost_estimate=cost,
        compiler_params=pltpu.CompilerParams(vmem_limit_bytes=(58 if hbm else 16) * 1024 * 1024),
    )(*args)


def parts(xs):
    return [xs.at[pl.ds(n * ROWS, ROWS), :] for n in range(6)]


def lanes(rows, width=NI):
    return lax.broadcasted_iota(jnp.int32, (rows, width), 1)


def rolled(value, amount, axis):
    return pltpu.roll(value, amount % value.shape[axis], axis)


def level(ref, k):
    return ref[pl.ds(k * NJ, NJ), :]


def across(ref, j, count=NK, stride=NJ):
    return ref[pl.ds(j, count, stride=stride), :]


def column(value, k):
    return jnp.broadcast_to(value[:, k : k + 1], (value.shape[0], NI))


def z_pair(zc, k):
    return (level(zc, k - 1) if k > 0 else None, level(zc, k) if k < NK - 1 else None)


def z_sum(zc, k, base):
    low, top = z_pair(zc, k)
    if low is not None:
        base = base + low
    if top is not None:
        base = base + top
    return base


def z_terms(zc, field, k, base):
    low, top = z_pair(zc, k)
    if low is not None:
        base = base + low * level(field, k - 1)
    if top is not None:
        base = base + top * level(field, k + 1)
    return base


def y_left_of(yc, halo, k):
    row = lax.broadcasted_iota(jnp.int32, (NJ, NI), 0)
    return jnp.where(row == 0, halo[pl.ds(k, 1), :], rolled(level(yc, k), 1, 0))


def squeeze(values, scale=0.125, start=0):
    source = lax.broadcasted_iota(jnp.int32, (NI, NI), 0)
    target = lax.broadcasted_iota(jnp.int32, (NI, NI), 1)
    matrix = jnp.where(source // 2 + start == target, scale, 0.0).astype(F32)
    return jnp.dot(values, matrix, precision=lax.Precision.HIGHEST, preferred_element_type=F32)


def edges(values, scale=0.125):
    source = lax.broadcasted_iota(jnp.int32, (NI, NI), 0)
    target = lax.broadcasted_iota(jnp.int32, (NI, NI), 1)
    hit = ((source == NI - 1) & (target == 64)) | ((source == 0) & (target == NI - 1))
    matrix = jnp.where(hit, scale, 0.0).astype(F32)
    return jnp.dot(values, matrix, precision=lax.Precision.HIGHEST, preferred_element_type=F32)


def parity_shift(values):
    odd = lax.rem(lax.axis_index("gx"), 2) == 1
    return jnp.where(odd, rolled(values, 64, 1), values)


def store_coarse(out, base, tmp):
    for J in range(NJ // 2):
        out[pl.ds(base + J * 8, 8), :] = across(tmp, 2 * J, 8) + across(tmp, 2 * J + 1, 8)


def first_kernel(fh, ph, xh, yh, zh, dh, xs, up, down, coarse, tmp, sems):
    order = (3, 1, 2, 4, 5, 0)
    copies = {
        n: pltpu.make_async_copy(ref, xs.at[pl.ds(n * ROWS, ROWS), :], sems.at[n])
        for n, ref in enumerate((fh, ph, xh, yh, zh, dh))
    }
    for n in order:
        copies[n].start()
    f, p, xc, yc, zc, dp = parts(xs)
    for n in order:
        copies[n].wait()
    up[pl.ds(0, NK), :] = across(yc, NJ - 1)
    up[pl.ds(NK, NK), :] = across(p, NJ - 1)
    down[pl.ds(0, NK), :] = across(p, 0)
    for q, two in enumerate(((xc, yc), (zc, dp))):
        total = jnp.zeros((128, NI), F32)
        for half, ref in enumerate(two):
            pairs = jnp.concatenate([level(ref, 2 * K) + level(ref, 2 * K + 1) for K in range(NK // 2)], axis=0)
            total = total + squeeze(pairs, start=64 * half)
        tmp[...] = total
        store_coarse(coarse, q * 64, tmp)
        up[pl.ds(2 * NK + q * 24, 24), :] = coarse[pl.ds(q * 64 + 40, 24), :]
        down[pl.ds(NK + q * 16, 16), :] = coarse[pl.ds(q * 64, 16), :]


def x_matrix(x, rest):
    d = lax.axis_index("gx")
    lane = lanes(x.shape[0])
    inner = jnp.logical_or(lane < NI - 1, d == GX - 1)
    diag = jnp.where(lane == 0, 0.0, rolled(x, 1, 1)) + jnp.where(inner, x, 0.0) + rest
    return diag, jnp.where(lane == NI - 1, 0.0, -x)


def x_eliminate(diag, off, rhs, keep):
    wide = lanes(diag.shape[0])
    left = jnp.where(wide == 0, 1.0, 0.0).astype(F32)
    right = jnp.where(wide == NI - 1, 1.0, 0.0).astype(F32)
    for n, s in enumerate(STEPS):
        inv = 1.0 / diag
        low = rolled(off, s, 1)
        alpha = -low * rolled(inv, s, 1)
        beta = -off * rolled(inv, -s, 1)
        keep(2 * n, alpha)
        keep(2 * n + 1, beta)
        diag = diag + alpha * low + beta * off
        off = beta * rolled(off, -s, 1)
        rhs = rhs + alpha * rolled(rhs, s, 1) + beta * rolled(rhs, -s, 1)
        left = left + alpha * rolled(left, s, 1) + beta * rolled(left, -s, 1)
        right = right + alpha * rolled(right, s, 1) + beta * rolled(right, -s, 1)
    inv = 1.0 / diag
    keep(2 * len(STEPS), inv)
    return rhs * inv, left * inv, right * inv


def x_picks(g, a, b, x):
    return column(g, 0), column(g, NI - 1), column(a, 0), column(b, 0), column(b, NI - 1), column(x, NI - 1)


def x_first_kernel(xs, g, a, b, mult, packed_out):
    f, p, xc, yc, zc, dp = parts(xs)
    lane = lanes(NJ)
    row = lax.broadcasted_iota(jnp.int32, (NJ, NI), 0)
    packed = jnp.zeros((NJ, NI), F32)
    group = 2
    for k0 in range(0, NK, group):
        diag, off, rhs = [], [], []
        for k in range(k0, k0 + group):
            y, v = level(yc, k), level(p, k)
            y_left = jnp.where(row == 0, 0.0, rolled(y, 1, 0))
            matrix = x_matrix(level(xc, k), z_sum(zc, k, y_left + y + level(dp, k)))
            diag.append(matrix[0])
            off.append(matrix[1])
            after = jnp.where(row == NJ - 1, 0.0, rolled(v, -1, 0))
            rhs.append(z_terms(zc, p, k, level(f, k) + y_left * rolled(v, 1, 0) + y * after))
        diag, off, rhs = (jnp.concatenate(v, axis=0) for v in (diag, off, rhs))
        place = pl.ds(k0 * NJ, group * NJ)

        def keep(n, value):
            mult[pl.ds(n * ROWS + k0 * NJ, group * NJ), :] = value

        rhs, left, right = x_eliminate(diag, off, rhs, keep)
        g[place, :], a[place, :], b[place, :] = rhs, left, right
        for k in range(k0, k0 + group):
            part = slice((k - k0) * NJ, (k - k0 + 1) * NJ)
            for q, pick in enumerate(x_picks(rhs[part], left[part], right[part], level(xc, k))):
                packed = jnp.where(lane == q * NK + k, pick, packed)
    packed_out[...] = packed


def x_rim_kernel(xs, below, above, coarse, packed, g_in, a_in, b_in, mult_in, g, a, b, mult, send):
    f, p, xc, yc, zc, dp = parts(xs)
    lane = lanes(NK)
    row = lax.broadcasted_iota(jnp.int32, (NK, NI), 0)

    def lifted(j):
        z, v = across(zc, j), across(p, j)
        top = jnp.where(row == NK - 1, 0.0, z)
        low = rolled(top, 1, 0)
        return low, top, low * rolled(v, 1, 0) + top * rolled(v, -1, 0)

    low, top, z_part = lifted(0)
    y, y_left = across(yc, 0), below[pl.ds(0, NK), :]
    diag, off = x_matrix(across(xc, 0), low + top + y + y_left + across(dp, 0))
    rhs = across(f, 0) + y_left * below[pl.ds(NK, NK), :] + y * across(p, 1) + z_part

    def keep(n, value):
        mult[pl.ds(n * ROWS, NK, stride=NJ), :] = value

    rhs, left, right = x_eliminate(diag, off, rhs, keep)
    first = pl.ds(0, NK, stride=NJ)
    g[first, :], a[first, :], b[first, :] = rhs, left, right
    line = jnp.zeros((NK, NI), F32)
    for q, pick in enumerate(x_picks(rhs, left, right, across(xc, 0))):
        line = line + jnp.where(lane == q * NK + row, pick, 0.0)
    line = jnp.sum(line, axis=0, keepdims=True)

    j = NJ - 1
    _, _, z_part = lifted(j)
    y = across(yc, j)
    rhs = across(f, j) + across(yc, j - 1) * across(p, j - 1) + y * above[pl.ds(0, NK), :] + z_part
    rhs = x_second_solve(rhs, lambda n: mult_in[pl.ds(n * ROWS + j, NK, stride=NJ), :])
    g[pl.ds(j, NK, stride=NJ), :] = rhs
    last = jnp.where(lane == row, column(rhs, 0), 0.0) + jnp.where(lane == NK + row, column(rhs, NI - 1), 0.0)
    last = jnp.sum(last, axis=0, keepdims=True)
    was = packed[...]
    was = jnp.where(row == 0, line, was)
    send[pl.ds(0, NJ), :] = jnp.where(jnp.logical_and(row == NJ - 1, lane < 2 * NK), last, was)
    for q in range(2):
        at = NJ + q * 104
        send[pl.ds(at, 24), :] = below[pl.ds(2 * NK + q * 24, 24), :]
        send[pl.ds(at + 24, 64), :] = coarse[pl.ds(q * 64, 64), :]
        send[pl.ds(at + 88, 16), :] = above[pl.ds(NK + q * 16, 16), :]


def x_second_solve(rhs, kept):
    for n, s in enumerate(STEPS):
        rhs = rhs + kept(2 * n) * rolled(rhs, s, 1) + kept(2 * n + 1) * rolled(rhs, -s, 1)
    return rhs * kept(2 * len(STEPS))


def x_fluxes(fs, source, low, inv, up):
    zero = jnp.zeros((NJ, NI), F32)
    fs[0], fs[GX] = zero, zero
    forward = [source(0)]
    for d in range(1, GX - 1):
        forward.append(source(d) + low[d] * forward[-1])
    value = forward[-1] * inv[GX - 2]
    fs[GX - 1] = value
    for d in range(GX - 3, -1, -1):
        value = forward[d] * inv[d] + up[d] * value
        fs[1 + d] = value


def x_finish(fs, g, a, b, field):
    d = lax.axis_index("gx")
    flux_left, flux_right = fs[d], fs[d + 1]
    for k in range(NK):
        field[pl.ds(k * NJ, NJ), :] = (
            level(g, k) - level(a, k) * column(flux_left, k) + level(b, k) * column(flux_right, k)
        )
    return flux_left, flux_right


def y_source(f, xc, zc, field, fluxes, c_left, k):
    d = lax.axis_index("gx")
    lane = lanes(NJ)
    flux_left, flux_right = fluxes
    v, x = level(field, k), level(xc, k)
    before = jnp.where(lane == 0, column(c_left, k) * v - column(flux_left, k), rolled(x * v, 1, 1))
    last = jnp.where(d == GX - 1, 0.0, x * v + column(flux_right, k))
    after = jnp.where(lane == NI - 1, last, x * rolled(v, -1, 1))
    return z_terms(zc, field, k, level(f, k) + before + after)


def y_first_kernel(xs, got, g, a, b, yg, ya, yb, yw, yinv, xred, cl, send, fs, cs, field, src, base):
    f, p, xc, yc, zc, dp = parts(xs)
    d = lax.axis_index("gx")
    e = lax.axis_index("gy")
    lane = lanes(NJ)
    part = lambda n, q: rolled(got[n, pl.ds(0, NJ), :], -NK * q, 1)
    m = [part(n, 3) for n in range(GX)]
    low, inv, up = [None], [], []
    for n in range(GX - 1):
        dd = part(n, 4) + 1.0 / part(n, 5) + part(n + 1, 2)
        if n:
            low.append(m[n] * inv[-1])
            dd = dd - low[n] * m[n]
        inv.append(1.0 / dd)
        up.append(m[n + 1] * inv[n])
        xred[n], xred[GX + n], xred[2 * GX + n] = (low[n] if n else jnp.zeros_like(dd)), inv[n], up[n]
    x_fluxes(fs, lambda n: part(n + 1, 0) - part(n, 1), low, inv, up)
    cs[0] = jnp.zeros((NJ, NI), F32)
    for n in range(GX):
        cs[n + 1] = part(n, 5)
    c_left = cs[d]
    cl[...] = c_left
    fluxes = x_finish(fs, g, a, b, field)
    for k in range(NK):
        src[pl.ds(k * NJ, NJ), :] = y_source(f, xc, zc, field, fluxes, c_left, k)
        x = level(xc, k)
        x_left = jnp.where(lane == 0, column(c_left, k), rolled(x, 1, 1))
        base[pl.ds(k * NJ, NJ), :] = z_sum(zc, k, x_left + x + level(dp, k))
    ys, ws, invs, spike = [], [None], [], []
    for j in range(NJ):
        y = across(yc, j)
        diag = across(base, j)
        if j < NJ - 1:
            diag = diag + y
        else:
            diag = diag + jnp.where(e == GY - 1, y, 0.0)
        rhs = across(src, j)
        if j:
            y_before = across(yc, j - 1)
            w = y_before * invs[-1]
            ws.append(w)
            diag = diag + y_before - w * y_before
            rhs = rhs + w * ys[-1]
            spike.append(w * spike[-1])
            yw[pl.ds(j * NK, NK), :] = w
        else:
            spike.append(jnp.ones((NK, NI), F32))
            yw[pl.ds(0, NK), :] = jnp.zeros((NK, NI), F32)
        ys.append(rhs)
        invs.append(1.0 / diag)
        yinv[pl.ds(j * NK, NK), :] = invs[-1]
    for j in range(NJ - 1, -1, -1):
        if j == NJ - 1:
            gv, av, bv = ys[j] * invs[j], spike[j] * invs[j], invs[j]
            send[pl.ds(NK, NK), :] = gv
            send[pl.ds(4 * NK, NK), :] = bv + 1.0 / across(yc, j)
        else:
            w = ws[j + 1]
            gv, av, bv = ys[j] * invs[j] + w * gv, spike[j] * invs[j] + w * av, w * bv
        place = pl.ds(j * NK, NK)
        yg[place, :], ya[place, :], yb[place, :] = gv, av, bv
    send[pl.ds(0, NK), :] = gv
    send[pl.ds(2 * NK, NK), :] = av
    send[pl.ds(3 * NK, NK), :] = bv


def y_fluxes(fs, source, low, inv, up):
    zero = jnp.zeros((NK, NI), F32)
    fs[0], fs[GY] = zero, zero
    forward = [source(0)]
    for n in range(1, GY - 1):
        forward.append(source(n) + low(n) * forward[-1])
    value = forward[-1] * inv(GY - 2)
    fs[GY - 1] = value
    for n in range(GY - 3, -1, -1):
        value = forward[n] * inv(n) + up(n) * value
        fs[1 + n] = value


def y_finish(fs, yc, below, yg, ya, yb, field, terms):
    e = lax.axis_index("gy")
    flux_left, flux_right = fs[e], fs[e + 1]
    block = lambda ref, j: ref[pl.ds(j * NK, NK), :]
    p = [block(yg, j) - block(ya, j) * flux_left + block(yb, j) * flux_right for j in range(NJ)]
    for j in range(NJ):
        y = across(yc, j)
        if j:
            before = across(yc, j - 1) * p[j - 1]
        else:
            before = below[pl.ds(0, NK), :] * p[0] - flux_left
        if j < NJ - 1:
            after = y * p[j + 1]
        else:
            after = jnp.where(e == GY - 1, 0.0, y * p[j] + flux_right)
        field[pl.ds(j, NK, stride=NJ), :] = p[j]
        terms[pl.ds(j, NK, stride=NJ), :] = before + after


def x_again_kernel(xs, below, got, yg, ya, yb, mult, g, yred, send, fs, field, terms):
    f, p, xc, yc, zc, dp = parts(xs)
    part = lambda n, q: got[n, pl.ds(q * NK, NK), :]
    prev = None
    for n in range(GY - 1):
        dd = part(n, 4) + part(n + 1, 2)
        if n:
            m = part(n, 3)
            low = m * prev
            dd = dd - low * m
            yred[n] = low
        else:
            yred[n] = jnp.zeros_like(dd)
        prev = 1.0 / dd
        yred[GY + n] = prev
        yred[2 * GY + n] = part(n + 1, 3) * prev
    yred[GY - 1] = jnp.zeros((NK, NI), F32)
    yred[2 * GY - 1] = jnp.zeros((NK, NI), F32)
    yred[3 * GY - 1] = jnp.zeros((NK, NI), F32)
    y_fluxes(
        fs,
        lambda n: part(n + 1, 0) - part(n, 1),
        lambda n: yred[n],
        lambda n: yred[GY + n],
        lambda n: yred[2 * GY + n],
    )
    y_finish(fs, yc, below, yg, ya, yb, field, terms)
    lane = lanes(NJ)
    packed = jnp.zeros((NJ, NI), F32)
    group = 2
    for k0 in range(0, NK, group):
        rhs = jnp.concatenate(
            [z_terms(zc, field, k, level(f, k) + level(terms, k)) for k in range(k0, k0 + group)], axis=0
        )
        place = pl.ds(k0 * NJ, group * NJ)
        rhs = x_second_solve(rhs, lambda n: mult[pl.ds(n * ROWS + k0 * NJ, group * NJ), :])
        g[place, :] = rhs
        for k in range(k0, k0 + group):
            mine = rhs[(k - k0) * NJ : (k - k0 + 1) * NJ]
            packed = jnp.where(lane == k, column(mine, 0), packed)
            packed = jnp.where(lane == NK + k, column(mine, NI - 1), packed)
    send[...] = packed


def y_again_kernel(xs, got, g, a, b, xred, cl, yw, yinv, yg, send, fs, field, src):
    f, p, xc, yc, zc, dp = parts(xs)
    part = lambda n, q: rolled(got[n], -NK * q, 1)
    x_fluxes(
        fs,
        lambda n: part(n + 1, 0) - part(n, 1),
        [xred[n] for n in range(GX - 1)],
        [xred[GX + n] for n in range(GX - 1)],
        [xred[2 * GX + n] for n in range(GX - 1)],
    )
    fluxes = x_finish(fs, g, a, b, field)
    c_left = cl[...]
    for k in range(NK):
        src[pl.ds(k * NJ, NJ), :] = y_source(f, xc, zc, field, fluxes, c_left, k)
    block = lambda ref, j: ref[pl.ds(j * NK, NK), :]
    ys = []
    for j in range(NJ):
        rhs = across(src, j)
        if j:
            rhs = rhs + block(yw, j) * ys[-1]
        ys.append(rhs)
    value = None
    for j in range(NJ - 1, -1, -1):
        new = ys[j] * block(yinv, j)
        value = new if value is None else new + block(yw, j + 1) * value
        yg[pl.ds(j * NK, NK), :] = value
        if j == NJ - 1:
            send[pl.ds(NK, NK), :] = value
    send[pl.ds(0, NK), :] = value


def residual_kernel(xs, below, got, yg, ya, yb, yred, cl, field, coarse, fs, terms, tmp):
    f, p, xc, yc, zc, dp = parts(xs)
    d = lax.axis_index("gx")
    lane = lanes(NJ)
    part = lambda n, q: got[n, pl.ds(q * NK, NK), :]
    y_fluxes(
        fs,
        lambda n: part(n + 1, 0) - part(n, 1),
        lambda n: yred[n],
        lambda n: yred[GY + n],
        lambda n: yred[2 * GY + n],
    )
    y_finish(fs, yc, below, yg, ya, yb, field, terms)
    c_left = cl[...]
    main, rim = [], []
    for k in range(NK):
        v, x = level(field, k), level(xc, k)
        left = column(c_left, k)
        x_left = jnp.where(lane == 0, left, rolled(x, 1, 1))
        diag = z_sum(zc, k, x_left + x + y_left_of(yc, below, k) + level(yc, k) + level(dp, k))
        around = jnp.where(lane == 0, 0.0, x_left * rolled(v, 1, 1)) + jnp.where(lane == NI - 1, 0.0, x * rolled(v, -1, 1))
        main.append(level(f, k) - (diag * v - around - level(terms, k) - z_terms(zc, field, k, jnp.zeros((NJ, NI), F32))))
        last = jnp.where(d == GX - 1, 0.0, x * v)
        rim.append(jnp.where(lane == 0, left * v, jnp.where(lane == NI - 1, last, 0.0)))
    pairs = jnp.concatenate([main[2 * K] + main[2 * K + 1] for K in range(NK // 2)], axis=0)
    outer = jnp.concatenate([rim[2 * K] + rim[2 * K + 1] for K in range(NK // 2)], axis=0)
    tmp[...] = parity_shift(squeeze(pairs) + edges(outer))
    store_coarse(coarse, 0, tmp)


def coarse_kernel(got, coef, res_out, cor_out, tmp, cor_tmp):
    d = lax.axis_index("gx")
    e = lax.axis_index("gy")
    lane = lanes(8)
    wide = lanes(8, 4 * NI)
    level_k = lax.broadcasted_iota(jnp.int32, (8, 4 * NI), 0)

    def whole_res(J):
        rows = pl.ds(J * 8, 8)
        outs = []
        for m in range(4):
            value = jnp.where(lane <= 64, got[2 * m, rows, :], 0.0) + jnp.where(lane >= 63, got[2 * m + 1, rows, :], 0.0)
            if m > 0:
                value = value + jnp.where(lane == 0, got[2 * m - 1, rows, :], 0.0)
            if m < 3:
                value = value + jnp.where(lane == NI - 1, got[2 * m + 2, rows, :], 0.0)
            outs.append(value)
        return outs

    def whole_coef(q, J):
        rows = pl.ds(NJ + (q // 2) * 104 + J * 8, 8)
        outs = []
        for m in range(4):
            even, odd = coef[2 * m, rows, :], coef[2 * m + 1, rows, :]
            if q % 2:
                even = rolled(even, 64, 1)
            else:
                odd = rolled(odd, 64, 1)
            outs.append(jnp.where(lane < 64, even, odd))
        return jnp.concatenate(outs, axis=1)

    res, diag, weight, cxl, cxi, cyl, cyr, czl, czt = ([] for _ in range(9))
    for J in range(12):
        outs = whole_res(J)
        if 2 <= J < 10:
            mine = outs[0]
            for m in range(1, 4):
                mine = jnp.where(d // 2 == m, outs[m], mine)
            mine = jnp.where(lax.rem(d, 2) == 1, rolled(mine, 64, 1), mine)
            tmp[pl.ds(J - 2, 8, stride=8), :] = mine
        res.append(jnp.concatenate(outs, axis=1))
        x, y, z, damp = (whole_coef(q, J + 1) for q in range(4))
        y_before = whole_coef(1, J)
        x_left = jnp.where(wide == 0, 0.0, rolled(x, 1, 1))
        z_top = jnp.where(level_k == 7, 0.0, z)
        z_low = rolled(z_top, 1, 0)
        total = x_left + x + y_before + y + z_low + z_top + damp
        at = e * 8 + J - 2
        valid = jnp.logical_and(at >= 0, at < 8 * GY)
        total = jnp.where(valid, total, 1.0)
        diag.append(total)
        weight.append(jnp.where(valid, RELAX / total, 0.0))
        cxl.append(x_left)
        cxi.append(jnp.where(wide == 4 * NI - 1, 0.0, x))
        cyl.append(y_before)
        cyr.append(y)
        czl.append(z_low)
        czt.append(z_top)
    cor = {J: weight[J] * res[J] for J in range(12)}
    for low, high in ((1, 11), (2, 10)):
        new = {}
        for J in range(low, high):
            v = cor[J]
            applied = (
                diag[J] * v
                - cxl[J] * rolled(v, 1, 1)
                - cxi[J] * rolled(v, -1, 1)
                - cyl[J] * cor[J - 1]
                - cyr[J] * cor[J + 1]
                - (czl[J] * rolled(v, 1, 0) + czt[J] * rolled(v, -1, 0))
            )
            new[J] = v + weight[J] * (res[J] - applied)
        cor = new
    for J in range(8):
        for m in range(4):
            cor_tmp[m, pl.ds(J, 8, stride=8), :] = cor[J + 2][:, m * NI : (m + 1) * NI]
    for m in range(4):
        cor_out[:, pl.ds(m * NI, NI)] = cor_tmp[m]
    res_out[...] = tmp[:, :64]


def spread(value, axis, count):
    many = jnp.broadcast_to(value[None], (count,) + value.shape)
    return lax.all_to_all(many, axis, split_axis=0, concat_axis=0, tiled=True)


def body(forcing, pressure_in, x_coupling, y_coupling, z_coupling, damping):
    args = [v.reshape(ROWS, NI) for v in (forcing, pressure_in, x_coupling, y_coupling, z_coupling, damping)]
    forth = [(n, n + 1) for n in range(GY - 1)]
    back = [(n + 1, n) for n in range(GY - 1)]
    whole = sds(ROWS, NI)
    kept = sds((2 * len(STEPS) + 1) * ROWS, NI)
    xs, up, down, coef = call(
        first_kernel,
        [sds(6 * ROWS, NI), sds(80, NI), sds(48, NI), sds(128, NI)],
        *args,
        scratch=[(128, NI)],
        hbm=True,
        sems=6,
    )
    below = lax.ppermute(up, "gy", forth)
    above = lax.ppermute(down, "gy", back)
    g, a, b, mult, packed = call(x_first_kernel, [whole, whole, whole, kept, sds(NJ, NI)], xs, flops=10**8)
    g, a, b, mult, send = call(
        x_rim_kernel,
        [whole, whole, whole, kept, sds(NJ + 208, NI)],
        xs, below, above, coef, packed, g, a, b, mult,
        aliases={5: 0, 6: 1, 7: 2, 8: 3},
    )
    got_coef = got = spread(send, "gx", GX)
    yg, ya, yb, yw, yinv, xred, cl, send = call(
        y_first_kernel,
        [whole] * 5 + [sds(3 * GX, NJ, NI), sds(NJ, NI), sds(5 * NK, NI)],
        xs, got, g, a, b,
        scratch=[(GX + 1, NJ, NI), (GX + 1, NJ, NI), (ROWS, NI), (ROWS, NI), (ROWS, NI)],
    )
    got = spread(send, "gy", GY)
    g, yred, send = call(
        x_again_kernel,
        [whole, sds(3 * GY, NK, NI), sds(NJ, NI)],
        xs, below, got, yg, ya, yb, mult,
        scratch=[(GY + 1, NK, NI), (ROWS, NI), (ROWS, NI)],
    )
    got = spread(send, "gx", GX)
    yg, send = call(
        y_again_kernel,
        [whole, sds(2 * NK, NI)],
        xs, got, g, a, b, xred, cl, yw, yinv,
        scratch=[(GX + 1, NJ, NI), (ROWS, NI), (ROWS, NI)],
    )
    got = spread(send, "gy", GY)
    field, coarse = call(
        residual_kernel,
        [whole, sds(64, NI)],
        xs, below, got, yg, ya, yb, yred, cl,
        scratch=[(GY + 1, NK, NI), (ROWS, NI), (128, NI)],
    )
    lower = lax.ppermute(coarse[48:], "gy", forth)
    upper = lax.ppermute(coarse[:16], "gy", back)
    got = spread(jnp.concatenate([lower, coarse, upper], axis=0), "gx", GX)
    res, cor = call(
        coarse_kernel, [sds(64, 64), sds(64, 512)], got, got_coef, scratch=[(64, NI), (4, 64, NI)]
    )
    return field.reshape(NK, NJ, NI), res.reshape(8, 8, 64), cor.reshape(8, 8, 512)


def solution(mesh):
    spec = P(None, "gy", "gx")
    return jax.shard_map(
        body, mesh=mesh, in_specs=(spec,) * 6, out_specs=(spec, spec, P(None, "gy", None)), check_vma=False
    )
```

```python
import functools

import jax
import jax.numpy as jnp
from jax import lax
from jax.experimental import pallas as pl
from jax.experimental.pallas import tpu as pltpu
from jax.sharding import PartitionSpec as P

RELAX = 0.8
NK, NJ, NI = 16, 16, 128
ROWS = NK * NJ
GX, GY = 8, 16
STEPS = (1, 2, 4, 8, 16, 32, 64)
F32 = jnp.float32


def sds(*shape):
    return jax.ShapeDtypeStruct(shape, F32)


def call(kernel, outs, *args, scratch=(), hbm=False, aliases={}, sems=0, flops=None):
    spec = pl.BlockSpec(memory_space=pltpu.VMEM)
    inside = pl.BlockSpec(memory_space=pltpu.HBM) if hbm else spec
    shapes = [pltpu.VMEM(v, F32) for v in scratch]
    if sems:
        shapes.append(pltpu.SemaphoreType.DMA((sems,)))
    cost = None if flops is None else pl.CostEstimate(flops=flops, bytes_accessed=1 << 20, transcendentals=0)
    return pl.pallas_call(
        kernel,
        out_shape=outs,
        in_specs=[inside] * len(args),
        out_specs=[spec] * len(outs),
        scratch_shapes=shapes,
        input_output_aliases=aliases,
        cost_estimate=cost,
        compiler_params=pltpu.CompilerParams(vmem_limit_bytes=16 * 1024 * 1024),
    )(*args)


def parts(xs):
    return [xs.at[pl.ds(n * ROWS, ROWS), :] for n in range(6)]


def lanes(rows, width=NI):
    return lax.broadcasted_iota(jnp.int32, (rows, width), 1)


def rolled(value, amount, axis):
    return pltpu.roll(value, amount % value.shape[axis], axis)


def level(ref, k):
    return ref[pl.ds(k * NJ, NJ), :]


def across(ref, j, count=NK, stride=NJ):
    return ref[pl.ds(j, count, stride=stride), :]


def column(value, k):
    return jnp.broadcast_to(value[:, k : k + 1], (value.shape[0], NI))


def z_pair(zc, k):
    return (level(zc, k - 1) if k > 0 else None, level(zc, k) if k < NK - 1 else None)


def z_sum(zc, k, base):
    low, top = z_pair(zc, k)
    if low is not None:
        base = base + low
    if top is not None:
        base = base + top
    return base


def z_terms(zc, field, k, base):
    low, top = z_pair(zc, k)
    if low is not None:
        base = base + low * level(field, k - 1)
    if top is not None:
        base = base + top * level(field, k + 1)
    return base


def y_left_of(yc, halo, k):
    row = lax.broadcasted_iota(jnp.int32, (NJ, NI), 0)
    return jnp.where(row == 0, halo[pl.ds(k, 1), :], rolled(level(yc, k), 1, 0))


def squeeze(values, scale=0.125, start=0):
    source = lax.broadcasted_iota(jnp.int32, (NI, NI), 0)
    target = lax.broadcasted_iota(jnp.int32, (NI, NI), 1)
    matrix = jnp.where(source // 2 + start == target, scale, 0.0).astype(F32)
    return jnp.dot(values, matrix, precision=lax.Precision.HIGHEST, preferred_element_type=F32)


def edges(values, scale=0.125):
    source = lax.broadcasted_iota(jnp.int32, (NI, NI), 0)
    target = lax.broadcasted_iota(jnp.int32, (NI, NI), 1)
    hit = ((source == NI - 1) & (target == 64)) | ((source == 0) & (target == NI - 1))
    matrix = jnp.where(hit, scale, 0.0).astype(F32)
    return jnp.dot(values, matrix, precision=lax.Precision.HIGHEST, preferred_element_type=F32)


def parity_shift(values):
    odd = lax.rem(lax.axis_index("gx"), 2) == 1
    return jnp.where(odd, rolled(values, 64, 1), values)


def store_coarse(out, base, tmp):
    for J in range(NJ // 2):
        out[pl.ds(base + J * 8, 8), :] = across(tmp, 2 * J, 8) + across(tmp, 2 * J + 1, 8)


def first_kernel(fh, ph, xh, yh, zh, dh, xs, near, far, coarse, tmp, sems):
    copies = [
        pltpu.make_async_copy(ref, xs.at[pl.ds(n * ROWS, ROWS), :], sems.at[n])
        for n, ref in enumerate((fh, ph, xh, yh, zh, dh))
    ]
    for copy in copies:
        copy.start()
    for copy in copies:
        copy.wait()
    f, p, xc, yc, zc, dp = parts(xs)
    odd = lax.rem(lax.axis_index("gy"), 2) == 1
    for q, two in enumerate(((xc, yc), (zc, dp))):
        total = jnp.zeros((128, NI), F32)
        for half, ref in enumerate(two):
            pairs = jnp.concatenate([level(ref, 2 * K) + level(ref, 2 * K + 1) for K in range(NK // 2)], axis=0)
            total = total + squeeze(pairs, start=64 * half)
        tmp[...] = total
        store_coarse(coarse, q * 64, tmp)

    def put(place, up, down):
        near[place, :] = jnp.where(odd, down, up)
        far[place, :] = jnp.where(odd, up, down)

    put(pl.ds(0, NK), across(p, NJ - 1), across(p, 0))
    put(pl.ds(NK, NK), across(yc, NJ - 1), across(yc, 0))
    for q in range(2):
        put(pl.ds(2 * NK + q * 24, 24), coarse[pl.ds(q * 64 + 40, 24), :], coarse[pl.ds(q * 64, 24), :])


def sorted_out(near, far, place):
    e = lax.axis_index("gy")
    odd = lax.rem(e, 2) == 1
    one, two = near[place, :], far[place, :]
    return (
        jnp.where(e == 0, 0.0, jnp.where(odd, one, two)),
        jnp.where(e == GY - 1, 0.0, jnp.where(odd, two, one)),
    )


def x_matrix(x, rest):
    d = lax.axis_index("gx")
    lane = lanes(x.shape[0])
    inner = jnp.logical_or(lane < NI - 1, d == GX - 1)
    diag = jnp.where(lane == 0, 0.0, rolled(x, 1, 1)) + jnp.where(inner, x, 0.0) + rest
    return diag, jnp.where(lane == NI - 1, 0.0, -x)


def x_eliminate(diag, off, rhs, keep):
    wide = lanes(diag.shape[0])
    ends = jnp.where(jnp.logical_or(wide == 0, wide == NI - 1), 1.0, 0.0).astype(F32)
    for n, s in enumerate(STEPS):
        inv = 1.0 / diag
        low = rolled(off, s, 1)
        alpha = -low * rolled(inv, s, 1)
        beta = -off * rolled(inv, -s, 1)
        keep(2 * n, alpha)
        keep(2 * n + 1, beta)
        diag = diag + alpha * low + beta * off
        rhs = rhs + alpha * rolled(rhs, s, 1) + beta * rolled(rhs, -s, 1)
        if s < NI // 2:
            off = beta * rolled(off, -s, 1)
            ends = ends + alpha * rolled(ends, s, 1) + beta * rolled(ends, -s, 1)
    inv = 1.0 / diag
    keep(2 * len(STEPS), inv)
    other = rolled(ends, NI // 2, 1)
    left = jnp.where(wide < NI // 2, ends, alpha * other)
    right = jnp.where(wide < NI // 2, beta * other, ends)
    return rhs * inv, left * inv, right * inv


def x_picks(g, a, b, x):
    return column(g, 0), column(g, NI - 1), column(a, 0), column(b, 0), column(b, NI - 1), column(x, NI - 1)


def x_first_kernel(xs, near, far, coarse, below, g, a, b, mult, send):
    f, p, xc, yc, zc, dp = parts(xs)
    lane = lanes(NJ)
    row = lax.broadcasted_iota(jnp.int32, (NJ, NI), 0)
    packed = jnp.zeros((NJ, NI), F32)
    p_below, p_above = sorted_out(near, far, pl.ds(0, NK))
    y_below, _ = sorted_out(near, far, pl.ds(NK, NK))
    below[...] = y_below
    group = 2
    for k0 in range(0, NK, group):
        diag, off, rhs = [], [], []
        for k in range(k0, k0 + group):
            y, v = level(yc, k), level(p, k)
            y_left = jnp.where(row == 0, y_below[k : k + 1, :], rolled(y, 1, 0))
            matrix = x_matrix(level(xc, k), z_sum(zc, k, y_left + y + level(dp, k)))
            diag.append(matrix[0])
            off.append(matrix[1])
            before = jnp.where(row == 0, p_below[k : k + 1, :], rolled(v, 1, 0))
            after = jnp.where(row == NJ - 1, p_above[k : k + 1, :], rolled(v, -1, 0))
            rhs.append(z_terms(zc, p, k, level(f, k) + y_left * before + y * after))
        diag, off, rhs = (jnp.concatenate(v, axis=0) for v in (diag, off, rhs))
        place = pl.ds(k0 * NJ, group * NJ)

        def keep(n, value):
            mult[pl.ds(n * ROWS + k0 * NJ, group * NJ), :] = value

        rhs, left, right = x_eliminate(diag, off, rhs, keep)
        g[place, :], a[place, :], b[place, :] = rhs, left, right
        for k in range(k0, k0 + group):
            part = slice((k - k0) * NJ, (k - k0 + 1) * NJ)
            for q, pick in enumerate(x_picks(rhs[part], left[part], right[part], level(xc, k))):
                packed = jnp.where(lane == q * NK + k, pick, packed)
    send[pl.ds(0, NJ), :] = packed
    for q in range(2):
        at = NJ + q * 104
        lower, upper = sorted_out(near, far, pl.ds(2 * NK + q * 24, 24))
        send[pl.ds(at, 24), :] = lower
        send[pl.ds(at + 24, 64), :] = coarse[pl.ds(q * 64, 64), :]
        send[pl.ds(at + 88, 16), :] = upper[:16]


def x_second_solve(rhs, kept):
    for n, s in enumerate(STEPS):
        rhs = rhs + kept(2 * n) * rolled(rhs, s, 1) + kept(2 * n + 1) * rolled(rhs, -s, 1)
    return rhs * kept(2 * len(STEPS))


def x_fluxes(fs, source, low, inv, up):
    zero = jnp.zeros((NJ, NI), F32)
    fs[0], fs[GX] = zero, zero
    forward = [source(0)]
    for d in range(1, GX - 1):
        forward.append(source(d) + low[d] * forward[-1])
    value = forward[-1] * inv[GX - 2]
    fs[GX - 1] = value
    for d in range(GX - 3, -1, -1):
        value = forward[d] * inv[d] + up[d] * value
        fs[1 + d] = value


def x_finish(fs, g, a, b, field):
    d = lax.axis_index("gx")
    flux_left, flux_right = fs[d], fs[d + 1]
    for k in range(NK):
        field[pl.ds(k * NJ, NJ), :] = (
            level(g, k) - level(a, k) * column(flux_left, k) + level(b, k) * column(flux_right, k)
        )
    return flux_left, flux_right


def y_source(f, xc, zc, field, fluxes, c_left, k):
    d = lax.axis_index("gx")
    lane = lanes(NJ)
    flux_left, flux_right = fluxes
    v, x = level(field, k), level(xc, k)
    before = jnp.where(lane == 0, column(c_left, k) * v - column(flux_left, k), rolled(x * v, 1, 1))
    last = jnp.where(d == GX - 1, 0.0, x * v + column(flux_right, k))
    after = jnp.where(lane == NI - 1, last, x * rolled(v, -1, 1))
    return z_terms(zc, field, k, level(f, k) + before + after)


def y_first_kernel(xs, got, g, a, b, yg, ya, yb, yw, yinv, xred, cl, send, fs, cs, field, src, base):
    f, p, xc, yc, zc, dp = parts(xs)
    d = lax.axis_index("gx")
    e = lax.axis_index("gy")
    lane = lanes(NJ)
    part = lambda n, q: rolled(got[n, pl.ds(0, NJ), :], -NK * q, 1)
    m = [part(n, 3) for n in range(GX)]
    low, inv, up = [None], [], []
    for n in range(GX - 1):
        dd = part(n, 4) + 1.0 / part(n, 5) + part(n + 1, 2)
        if n:
            low.append(m[n] * inv[-1])
            dd = dd - low[n] * m[n]
        inv.append(1.0 / dd)
        up.append(m[n + 1] * inv[n])
        xred[n], xred[GX + n], xred[2 * GX + n] = (low[n] if n else jnp.zeros_like(dd)), inv[n], up[n]
    x_fluxes(fs, lambda n: part(n + 1, 0) - part(n, 1), low, inv, up)
    cs[0] = jnp.zeros((NJ, NI), F32)
    for n in range(GX):
        cs[n + 1] = part(n, 5)
    c_left = cs[d]
    cl[...] = c_left
    fluxes = x_finish(fs, g, a, b, field)
    for k in range(NK):
        src[pl.ds(k * NJ, NJ), :] = y_source(f, xc, zc, field, fluxes, c_left, k)
        x = level(xc, k)
        x_left = jnp.where(lane == 0, column(c_left, k), rolled(x, 1, 1))
        base[pl.ds(k * NJ, NJ), :] = z_sum(zc, k, x_left + x + level(dp, k))
    ys, ws, invs, spike = [], [None], [], []
    for j in range(NJ):
        y = across(yc, j)
        diag = across(base, j)
        if j < NJ - 1:
            diag = diag + y
        else:
            diag = diag + jnp.where(e == GY - 1, y, 0.0)
        rhs = across(src, j)
        if j:
            y_before = across(yc, j - 1)
            w = y_before * invs[-1]
            ws.append(w)
            diag = diag + y_before - w * y_before
            rhs = rhs + w * ys[-1]
            spike.append(w * spike[-1])
            yw[pl.ds(j * NK, NK), :] = w
        else:
            spike.append(jnp.ones((NK, NI), F32))
            yw[pl.ds(0, NK), :] = jnp.zeros((NK, NI), F32)
        ys.append(rhs)
        invs.append(1.0 / diag)
        yinv[pl.ds(j * NK, NK), :] = invs[-1]
    for j in range(NJ - 1, -1, -1):
        if j == NJ - 1:
            gv, av, bv = ys[j] * invs[j], spike[j] * invs[j], invs[j]
            send[pl.ds(NK, NK), :] = gv
            send[pl.ds(4 * NK, NK), :] = bv + 1.0 / across(yc, j)
        else:
            w = ws[j + 1]
            gv, av, bv = ys[j] * invs[j] + w * gv, spike[j] * invs[j] + w * av, w * bv
        place = pl.ds(j * NK, NK)
        yg[place, :], ya[place, :], yb[place, :] = gv, av, bv
    send[pl.ds(0, NK), :] = gv
    send[pl.ds(2 * NK, NK), :] = av
    send[pl.ds(3 * NK, NK), :] = bv


def y_fluxes(fs, source, low, inv, up):
    zero = jnp.zeros((NK, NI), F32)
    fs[0], fs[GY] = zero, zero
    forward = [source(0)]
    for n in range(1, GY - 1):
        forward.append(source(n) + low(n) * forward[-1])
    value = forward[-1] * inv(GY - 2)
    fs[GY - 1] = value
    for n in range(GY - 3, -1, -1):
        value = forward[n] * inv(n) + up(n) * value
        fs[1 + n] = value


def y_finish(fs, yc, below, yg, ya, yb, field, terms):
    e = lax.axis_index("gy")
    flux_left, flux_right = fs[e], fs[e + 1]
    block = lambda ref, j: ref[pl.ds(j * NK, NK), :]
    p = [block(yg, j) - block(ya, j) * flux_left + block(yb, j) * flux_right for j in range(NJ)]
    for j in range(NJ):
        y = across(yc, j)
        if j:
            before = across(yc, j - 1) * p[j - 1]
        else:
            before = below[pl.ds(0, NK), :] * p[0] - flux_left
        if j < NJ - 1:
            after = y * p[j + 1]
        else:
            after = jnp.where(e == GY - 1, 0.0, y * p[j] + flux_right)
        field[pl.ds(j, NK, stride=NJ), :] = p[j]
        terms[pl.ds(j, NK, stride=NJ), :] = before + after


def x_again_kernel(xs, below, got, yg, ya, yb, mult, g, yred, send, fs, field, terms):
    f, p, xc, yc, zc, dp = parts(xs)
    part = lambda n, q: got[n, pl.ds(q * NK, NK), :]
    prev = None
    for n in range(GY - 1):
        dd = part(n, 4) + part(n + 1, 2)
        if n:
            m = part(n, 3)
            low = m * prev
            dd = dd - low * m
            yred[n] = low
        else:
            yred[n] = jnp.zeros_like(dd)
        prev = 1.0 / dd
        yred[GY + n] = prev
        yred[2 * GY + n] = part(n + 1, 3) * prev
    yred[GY - 1] = jnp.zeros((NK, NI), F32)
    yred[2 * GY - 1] = jnp.zeros((NK, NI), F32)
    yred[3 * GY - 1] = jnp.zeros((NK, NI), F32)
    y_fluxes(
        fs,
        lambda n: part(n + 1, 0) - part(n, 1),
        lambda n: yred[n],
        lambda n: yred[GY + n],
        lambda n: yred[2 * GY + n],
    )
    y_finish(fs, yc, below, yg, ya, yb, field, terms)
    lane = lanes(NJ)
    packed = jnp.zeros((NJ, NI), F32)
    group = 2
    for k0 in range(0, NK, group):
        rhs = jnp.concatenate(
            [z_terms(zc, field, k, level(f, k) + level(terms, k)) for k in range(k0, k0 + group)], axis=0
        )
        place = pl.ds(k0 * NJ, group * NJ)
        rhs = x_second_solve(rhs, lambda n: mult[pl.ds(n * ROWS + k0 * NJ, group * NJ), :])
        g[place, :] = rhs
        for k in range(k0, k0 + group):
            mine = rhs[(k - k0) * NJ : (k - k0 + 1) * NJ]
            packed = jnp.where(lane == k, column(mine, 0), packed)
            packed = jnp.where(lane == NK + k, column(mine, NI - 1), packed)
    send[...] = packed


def y_again_kernel(xs, got, g, a, b, xred, cl, yw, yinv, yg, send, fs, field, src):
    f, p, xc, yc, zc, dp = parts(xs)
    part = lambda n, q: rolled(got[n], -NK * q, 1)
    x_fluxes(
        fs,
        lambda n: part(n + 1, 0) - part(n, 1),
        [xred[n] for n in range(GX - 1)],
        [xred[GX + n] for n in range(GX - 1)],
        [xred[2 * GX + n] for n in range(GX - 1)],
    )
    fluxes = x_finish(fs, g, a, b, field)
    c_left = cl[...]
    for k in range(NK):
        src[pl.ds(k * NJ, NJ), :] = y_source(f, xc, zc, field, fluxes, c_left, k)
    block = lambda ref, j: ref[pl.ds(j * NK, NK), :]
    ys = []
    for j in range(NJ):
        rhs = across(src, j)
        if j:
            rhs = rhs + block(yw, j) * ys[-1]
        ys.append(rhs)
    value = None
    for j in range(NJ - 1, -1, -1):
        new = ys[j] * block(yinv, j)
        value = new if value is None else new + block(yw, j + 1) * value
        yg[pl.ds(j * NK, NK), :] = value
        if j == NJ - 1:
            send[pl.ds(NK, NK), :] = value
    send[pl.ds(0, NK), :] = value


def residual_kernel(xs, below, got, yg, ya, yb, yred, cl, field, near, far, coarse, fs, terms, tmp):
    f, p, xc, yc, zc, dp = parts(xs)
    d = lax.axis_index("gx")
    lane = lanes(NJ)
    part = lambda n, q: got[n, pl.ds(q * NK, NK), :]
    y_fluxes(
        fs,
        lambda n: part(n + 1, 0) - part(n, 1),
        lambda n: yred[n],
        lambda n: yred[GY + n],
        lambda n: yred[2 * GY + n],
    )
    y_finish(fs, yc, below, yg, ya, yb, field, terms)
    c_left = cl[...]
    main, rim = [], []
    for k in range(NK):
        v, x = level(field, k), level(xc, k)
        left = column(c_left, k)
        x_left = jnp.where(lane == 0, left, rolled(x, 1, 1))
        diag = z_sum(zc, k, x_left + x + y_left_of(yc, below, k) + level(yc, k) + level(dp, k))
        around = jnp.where(lane == 0, 0.0, x_left * rolled(v, 1, 1)) + jnp.where(lane == NI - 1, 0.0, x * rolled(v, -1, 1))
        main.append(level(f, k) - (diag * v - around - level(terms, k) - z_terms(zc, field, k, jnp.zeros((NJ, NI), F32))))
        last = jnp.where(d == GX - 1, 0.0, x * v)
        rim.append(jnp.where(lane == 0, left * v, jnp.where(lane == NI - 1, last, 0.0)))
    pairs = jnp.concatenate([main[2 * K] + main[2 * K + 1] for K in range(NK // 2)], axis=0)
    outer = jnp.concatenate([rim[2 * K] + rim[2 * K + 1] for K in range(NK // 2)], axis=0)
    tmp[...] = parity_shift(squeeze(pairs) + edges(outer))
    store_coarse(coarse, 0, tmp)
    odd = lax.rem(lax.axis_index("gy"), 2) == 1
    up, down = coarse[pl.ds(48, 16), :], coarse[pl.ds(0, 16), :]
    near[...] = jnp.where(odd, down, up)
    far[...] = jnp.where(odd, up, down)


def join_kernel(near, far, coarse, send):
    lower, upper = sorted_out(near, far, pl.ds(0, 16))
    send[pl.ds(0, 16), :] = lower
    send[pl.ds(16, 64), :] = coarse[...]
    send[pl.ds(80, 16), :] = upper


def coarse_matrix_kernel(coef, weight_out, x_low_out, x_up_out, y_out, z_out):
    e = lax.axis_index("gy")
    lane = lanes(8)
    wide = lanes(8, 4 * NI)
    level_k = lax.broadcasted_iota(jnp.int32, (8, 4 * NI), 0)

    def whole_coef(q, J):
        rows = pl.ds(NJ + (q // 2) * 104 + J * 8, 8)
        outs = []
        for m in range(4):
            even, odd = coef[2 * m, rows, :], coef[2 * m + 1, rows, :]
            if q % 2:
                even = rolled(even, 64, 1)
            else:
                odd = rolled(odd, 64, 1)
            outs.append(jnp.where(lane < 64, even, odd))
        return jnp.concatenate(outs, axis=1)

    y_before = whole_coef(1, 0)
    y_out[pl.ds(0, 8), :] = y_before
    for J in range(12):
        rows = pl.ds(J * 8, 8)
        x, y, z, damp = (whole_coef(q, J + 1) for q in range(4))
        x_left = jnp.where(wide == 0, 0.0, rolled(x, 1, 1))
        z_top = jnp.where(level_k == 7, 0.0, z)
        total = x_left + x + y_before + y + rolled(z_top, 1, 0) + z_top + damp
        at = e * 8 + J - 2
        valid = jnp.logical_and(at >= 0, at < 8 * GY)
        total = jnp.where(valid, total, 1.0)
        weight_out[0, rows, :] = total
        weight_out[1, rows, :] = jnp.where(valid, RELAX / total, 0.0)
        x_low_out[rows, :] = x_left
        x_up_out[rows, :] = jnp.where(wide == 4 * NI - 1, 0.0, x)
        y_out[pl.ds(J * 8 + 8, 8), :] = y
        z_out[rows, :] = z_top
        y_before = y


def coarse_kernel(got, weight, x_low, x_up, y_all, z_all, res_out, cor_out, tmp, cor_tmp):
    d = lax.axis_index("gx")
    lane = lanes(8)

    def whole_res(J):
        rows = pl.ds(J * 8, 8)
        outs = []
        for m in range(4):
            value = jnp.where(lane <= 64, got[2 * m, rows, :], 0.0) + jnp.where(lane >= 63, got[2 * m + 1, rows, :], 0.0)
            if m > 0:
                value = value + jnp.where(lane == 0, got[2 * m - 1, rows, :], 0.0)
            if m < 3:
                value = value + jnp.where(lane == NI - 1, got[2 * m + 2, rows, :], 0.0)
            outs.append(value)
        return outs

    at = lambda ref, J: ref[pl.ds(J * 8, 8), :]
    diag = lambda J: weight[0, pl.ds(J * 8, 8), :]
    scale = lambda J: weight[1, pl.ds(J * 8, 8), :]
    res = []
    for J in range(12):
        outs = whole_res(J)
        if 2 <= J < 10:
            mine = outs[0]
            for m in range(1, 4):
                mine = jnp.where(d // 2 == m, outs[m], mine)
            mine = jnp.where(lax.rem(d, 2) == 1, rolled(mine, 64, 1), mine)
            tmp[pl.ds(J - 2, 8, stride=8), :] = mine
        res.append(jnp.concatenate(outs, axis=1))
    cor = {J: scale(J) * res[J] for J in range(12)}
    for low, high in ((1, 11), (2, 10)):
        new = {}
        for J in range(low, high):
            v = cor[J]
            z_top = at(z_all, J)
            applied = (
                diag(J) * v
                - at(x_low, J) * rolled(v, 1, 1)
                - at(x_up, J) * rolled(v, -1, 1)
                - at(y_all, J) * cor[J - 1]
                - at(y_all, J + 1) * cor[J + 1]
                - (rolled(z_top * v, 1, 0) + z_top * rolled(v, -1, 0))
            )
            new[J] = v + scale(J) * (res[J] - applied)
        cor = new
    for J in range(8):
        for m in range(4):
            cor_tmp[m, pl.ds(J, 8, stride=8), :] = cor[J + 2][:, m * NI : (m + 1) * NI]
    for m in range(4):
        cor_out[:, pl.ds(m * NI, NI)] = cor_tmp[m]
    res_out[...] = tmp[:, :64]


def spread(value, axis, count):
    many = jnp.broadcast_to(value[None], (count,) + value.shape)
    return lax.all_to_all(many, axis, split_axis=0, concat_axis=0, tiled=True)


def swap(near, far):
    pairs = [(n, n ^ 1) for n in range(GY)]
    others = [(n, (n + 1) % GY if n % 2 else (n - 1) % GY) for n in range(GY)]
    return lax.ppermute(near, "gy", pairs), lax.ppermute(far, "gy", others)


def body(forcing, pressure_in, x_coupling, y_coupling, z_coupling, damping):
    args = [v.reshape(ROWS, NI) for v in (forcing, pressure_in, x_coupling, y_coupling, z_coupling, damping)]
    whole = sds(ROWS, NI)
    kept = sds((2 * len(STEPS) + 1) * ROWS, NI)
    xs, near, far, coef = call(
        first_kernel,
        [sds(6 * ROWS, NI), sds(80, NI), sds(80, NI), sds(128, NI)],
        *[pltpu.with_memory_space_constraint(v, pltpu.HBM) for v in args],
        scratch=[(128, NI)],
        hbm=True,
        sems=6,
    )
    near, far = swap(near, far)
    below, g, a, b, mult, send = call(
        x_first_kernel, [sds(NK, NI), whole, whole, whole, kept, sds(NJ + 208, NI)], xs, near, far, coef
    )
    got_coef = got = spread(send, "gx", GX)
    yg, ya, yb, yw, yinv, xred, cl, send = call(
        y_first_kernel,
        [whole] * 5 + [sds(3 * GX, NJ, NI), sds(NJ, NI), sds(5 * NK, NI)],
        xs, got, g, a, b,
        scratch=[(GX + 1, NJ, NI), (GX + 1, NJ, NI), (ROWS, NI), (ROWS, NI), (ROWS, NI)],
    )
    got = spread(send, "gy", GY)
    g, yred, send = call(
        x_again_kernel,
        [whole, sds(3 * GY, NK, NI), sds(NJ, NI)],
        xs, below, got, yg, ya, yb, mult,
        scratch=[(GY + 1, NK, NI), (ROWS, NI), (ROWS, NI)],
    )
    got = spread(send, "gx", GX)
    yg, send = call(
        y_again_kernel,
        [whole, sds(2 * NK, NI)],
        xs, got, g, a, b, xred, cl, yw, yinv,
        scratch=[(GX + 1, NJ, NI), (ROWS, NI), (ROWS, NI)],
    )
    got = spread(send, "gy", GY)
    field, near, far, coarse = call(
        residual_kernel,
        [whole, sds(16, NI), sds(16, NI), sds(64, NI)],
        xs, below, got, yg, ya, yb, yred, cl,
        scratch=[(GY + 1, NK, NI), (ROWS, NI), (128, NI)],
    )
    near, far = swap(near, far)
    rows = sds(96, 4 * NI)
    matrix = call(
        coarse_matrix_kernel, [sds(2, 96, 4 * NI), rows, rows, sds(104, 4 * NI), rows], got_coef, flops=10**7
    )
    (send,) = call(join_kernel, [sds(96, NI)], near, far, coarse)
    got = spread(send, "gx", GX)
    res, cor = call(coarse_kernel, [sds(64, 64), sds(64, 512)], got, *matrix, scratch=[(64, NI), (4, 64, NI)])
    return field.reshape(NK, NJ, NI), res.reshape(8, 8, 64), cor.reshape(8, 8, 512)


def solution(mesh):
    spec = P(None, "gy", "gx")
    return jax.shard_map(
        body, mesh=mesh, in_specs=(spec,) * 6, out_specs=(spec, spec, P(None, "gy", None)), check_vma=False
    )
```

```python
import functools

import jax
import jax.numpy as jnp
from jax import lax
from jax.experimental import pallas as pl
from jax.experimental.pallas import tpu as pltpu
from jax.sharding import PartitionSpec as P

RELAX = 0.8
NK, NJ, NI = 16, 16, 128
ROWS = NK * NJ
GX, GY = 8, 16
STEPS = (1, 2, 4, 8, 16, 32, 64)
F32 = jnp.float32


def sds(*shape):
    return jax.ShapeDtypeStruct(shape, F32)


def call(kernel, outs, *args, scratch=(), hbm=False, aliases={}, sems=0, flops=None):
    spec = pl.BlockSpec(memory_space=pltpu.VMEM)
    inside = pl.BlockSpec(memory_space=pltpu.HBM) if hbm else spec
    shapes = [pltpu.VMEM(v, F32) for v in scratch]
    if sems:
        shapes.append(pltpu.SemaphoreType.DMA((sems,)))
    cost = None if flops is None else pl.CostEstimate(flops=flops, bytes_accessed=1 << 20, transcendentals=0)
    return pl.pallas_call(
        kernel,
        out_shape=outs,
        in_specs=[inside] * len(args),
        out_specs=[spec] * len(outs),
        scratch_shapes=shapes,
        input_output_aliases=aliases,
        cost_estimate=cost,
        compiler_params=pltpu.CompilerParams(vmem_limit_bytes=16 * 1024 * 1024),
    )(*args)


def parts(xs):
    return [xs.at[pl.ds(n * ROWS, ROWS), :] for n in range(6)]


def lanes(rows, width=NI):
    return lax.broadcasted_iota(jnp.int32, (rows, width), 1)


def rolled(value, amount, axis):
    return pltpu.roll(value, amount % value.shape[axis], axis)


def level(ref, k):
    return ref[pl.ds(k * NJ, NJ), :]


def across(ref, j, count=NK, stride=NJ):
    return ref[pl.ds(j, count, stride=stride), :]


def column(value, k):
    return jnp.broadcast_to(value[:, k : k + 1], (value.shape[0], NI))


def z_pair(zc, k):
    return (level(zc, k - 1) if k > 0 else None, level(zc, k) if k < NK - 1 else None)


def z_sum(zc, k, base):
    low, top = z_pair(zc, k)
    if low is not None:
        base = base + low
    if top is not None:
        base = base + top
    return base


def z_terms(zc, field, k, base):
    low, top = z_pair(zc, k)
    if low is not None:
        base = base + low * level(field, k - 1)
    if top is not None:
        base = base + top * level(field, k + 1)
    return base


def y_left_of(yc, halo, k):
    row = lax.broadcasted_iota(jnp.int32, (NJ, NI), 0)
    return jnp.where(row == 0, halo[pl.ds(k, 1), :], rolled(level(yc, k), 1, 0))


def squeeze(values, scale=0.125, start=0):
    source = lax.broadcasted_iota(jnp.int32, (NI, NI), 0)
    target = lax.broadcasted_iota(jnp.int32, (NI, NI), 1)
    matrix = jnp.where(source // 2 + start == target, scale, 0.0).astype(F32)
    return jnp.dot(values, matrix, precision=lax.Precision.HIGHEST, preferred_element_type=F32)


def edges(values, scale=0.125):
    source = lax.broadcasted_iota(jnp.int32, (NI, NI), 0)
    target = lax.broadcasted_iota(jnp.int32, (NI, NI), 1)
    hit = ((source == NI - 1) & (target == 64)) | ((source == 0) & (target == NI - 1))
    matrix = jnp.where(hit, scale, 0.0).astype(F32)
    return jnp.dot(values, matrix, precision=lax.Precision.HIGHEST, preferred_element_type=F32)


def parity_shift(values):
    odd = lax.rem(lax.axis_index("gx"), 2) == 1
    return jnp.where(odd, rolled(values, 64, 1), values)


def store_coarse(out, base, tmp):
    for J in range(NJ // 2):
        out[pl.ds(base + J * 8, 8), :] = across(tmp, 2 * J, 8) + across(tmp, 2 * J + 1, 8)


def first_kernel(fh, ph, xh, yh, zh, dh, xs, near, far, coarse, tmp, sems):
    copies = [
        pltpu.make_async_copy(ref, xs.at[pl.ds(n * ROWS, ROWS), :], sems.at[n])
        for n, ref in enumerate((fh, ph, xh, yh, zh, dh))
    ]
    for copy in copies:
        copy.start()
    for copy in copies:
        copy.wait()
    f, p, xc, yc, zc, dp = parts(xs)
    odd = lax.rem(lax.axis_index("gy"), 2) == 1
    for q, two in enumerate(((xc, yc), (zc, dp))):
        total = jnp.zeros((128, NI), F32)
        for half, ref in enumerate(two):
            pairs = jnp.concatenate([level(ref, 2 * K) + level(ref, 2 * K + 1) for K in range(NK // 2)], axis=0)
            total = total + squeeze(pairs, start=64 * half)
        tmp[...] = total
        store_coarse(coarse, q * 64, tmp)

    def put(place, up, down):
        near[place, :] = jnp.where(odd, down, up)
        far[place, :] = jnp.where(odd, up, down)

    put(pl.ds(0, NK), across(p, NJ - 1), across(p, 0))
    put(pl.ds(NK, NK), across(yc, NJ - 1), across(yc, 0))
    for q in range(2):
        put(pl.ds(2 * NK + q * 24, 24), coarse[pl.ds(q * 64 + 40, 24), :], coarse[pl.ds(q * 64, 24), :])


def sorted_out(near, far, place):
    e = lax.axis_index("gy")
    odd = lax.rem(e, 2) == 1
    one, two = near[place, :], far[place, :]
    return (
        jnp.where(e == 0, 0.0, jnp.where(odd, one, two)),
        jnp.where(e == GY - 1, 0.0, jnp.where(odd, two, one)),
    )


def x_matrix(x, rest):
    d = lax.axis_index("gx")
    lane = lanes(x.shape[0])
    inner = jnp.logical_or(lane < NI - 1, d == GX - 1)
    diag = jnp.where(lane == 0, 0.0, rolled(x, 1, 1)) + jnp.where(inner, x, 0.0) + rest
    return diag, jnp.where(lane == NI - 1, 0.0, -x)


def x_eliminate(diag, off, rhs, keep):
    wide = lanes(diag.shape[0])
    ends = jnp.where(jnp.logical_or(wide == 0, wide == NI - 1), 1.0, 0.0).astype(F32)
    for n, s in enumerate(STEPS):
        inv = 1.0 / diag
        low = rolled(off, s, 1)
        alpha = -low * rolled(inv, s, 1)
        beta = -off * rolled(inv, -s, 1)
        keep(2 * n, alpha)
        keep(2 * n + 1, beta)
        diag = diag + alpha * low + beta * off
        rhs = rhs + alpha * rolled(rhs, s, 1) + beta * rolled(rhs, -s, 1)
        if s < NI // 2:
            off = beta * rolled(off, -s, 1)
            ends = ends + alpha * rolled(ends, s, 1) + beta * rolled(ends, -s, 1)
    inv = 1.0 / diag
    keep(2 * len(STEPS), inv)
    other = rolled(ends, NI // 2, 1)
    left = jnp.where(wide < NI // 2, ends, alpha * other)
    right = jnp.where(wide < NI // 2, beta * other, ends)
    return rhs * inv, left * inv, right * inv


def x_picks(g, a, b, x):
    return column(g, 0), column(g, NI - 1), column(a, 0), column(b, 0), column(b, NI - 1), column(x, NI - 1)


def x_first_kernel(xs, g, a, b, mult, packed_out):
    f, p, xc, yc, zc, dp = parts(xs)
    lane = lanes(NJ)
    row = lax.broadcasted_iota(jnp.int32, (NJ, NI), 0)
    packed = jnp.zeros((NJ, NI), F32)
    group = 2
    for k0 in range(0, NK, group):
        diag, off, rhs = [], [], []
        for k in range(k0, k0 + group):
            y, v = level(yc, k), level(p, k)
            y_left = jnp.where(row == 0, 0.0, rolled(y, 1, 0))
            matrix = x_matrix(level(xc, k), z_sum(zc, k, y_left + y + level(dp, k)))
            diag.append(matrix[0])
            off.append(matrix[1])
            after = jnp.where(row == NJ - 1, 0.0, rolled(v, -1, 0))
            rhs.append(z_terms(zc, p, k, level(f, k) + y_left * rolled(v, 1, 0) + y * after))
        diag, off, rhs = (jnp.concatenate(v, axis=0) for v in (diag, off, rhs))
        place = pl.ds(k0 * NJ, group * NJ)

        def keep(n, value):
            mult[pl.ds(n * ROWS + k0 * NJ, group * NJ), :] = value

        rhs, left, right = x_eliminate(diag, off, rhs, keep)
        g[place, :], a[place, :], b[place, :] = rhs, left, right
        for k in range(k0, k0 + group):
            part = slice((k - k0) * NJ, (k - k0 + 1) * NJ)
            for q, pick in enumerate(x_picks(rhs[part], left[part], right[part], level(xc, k))):
                packed = jnp.where(lane == q * NK + k, pick, packed)
    packed_out[...] = packed


def x_rim_kernel(xs, near, far, coarse, packed, g_in, a_in, b_in, mult_in, below, g, a, b, mult, send):
    f, p, xc, yc, zc, dp = parts(xs)
    lane = lanes(NK)
    row = lax.broadcasted_iota(jnp.int32, (NK, NI), 0)

    def lifted(j):
        z, v = across(zc, j), across(p, j)
        top = jnp.where(row == NK - 1, 0.0, z)
        low = rolled(top, 1, 0)
        return low, top, low * rolled(v, 1, 0) + top * rolled(v, -1, 0)

    p_below, p_above = sorted_out(near, far, pl.ds(0, NK))
    y_left, _ = sorted_out(near, far, pl.ds(NK, NK))
    below[...] = y_left
    low, top, z_part = lifted(0)
    y = across(yc, 0)
    diag, off = x_matrix(across(xc, 0), low + top + y + y_left + across(dp, 0))
    rhs = across(f, 0) + y_left * p_below + y * across(p, 1) + z_part

    def keep(n, value):
        mult[pl.ds(n * ROWS, NK, stride=NJ), :] = value

    rhs, left, right = x_eliminate(diag, off, rhs, keep)
    first = pl.ds(0, NK, stride=NJ)
    g[first, :], a[first, :], b[first, :] = rhs, left, right
    line = jnp.zeros((NK, NI), F32)
    for q, pick in enumerate(x_picks(rhs, left, right, across(xc, 0))):
        line = line + jnp.where(lane == q * NK + row, pick, 0.0)
    line = jnp.sum(line, axis=0, keepdims=True)

    j = NJ - 1
    _, _, z_part = lifted(j)
    y = across(yc, j)
    rhs = across(f, j) + across(yc, j - 1) * across(p, j - 1) + y * p_above + z_part
    rhs = x_second_solve(rhs, lambda n: mult_in[pl.ds(n * ROWS + j, NK, stride=NJ), :])
    g[pl.ds(j, NK, stride=NJ), :] = rhs
    last = jnp.where(lane == row, column(rhs, 0), 0.0) + jnp.where(lane == NK + row, column(rhs, NI - 1), 0.0)
    last = jnp.sum(last, axis=0, keepdims=True)
    was = packed[...]
    was = jnp.where(row == 0, line, was)
    send[pl.ds(0, NJ), :] = jnp.where(jnp.logical_and(row == NJ - 1, lane < 2 * NK), last, was)
    for q in range(2):
        at = NJ + q * 104
        lower, upper = sorted_out(near, far, pl.ds(2 * NK + q * 24, 24))
        send[pl.ds(at, 24), :] = lower
        send[pl.ds(at + 24, 64), :] = coarse[pl.ds(q * 64, 64), :]
        send[pl.ds(at + 88, 16), :] = upper[:16]


def x_second_solve(rhs, kept):
    for n, s in enumerate(STEPS):
        rhs = rhs + kept(2 * n) * rolled(rhs, s, 1) + kept(2 * n + 1) * rolled(rhs, -s, 1)
    return rhs * kept(2 * len(STEPS))


def x_fluxes(fs, source, low, inv, up):
    zero = jnp.zeros((NJ, NI), F32)
    fs[0], fs[GX] = zero, zero
    forward = [source(0)]
    for d in range(1, GX - 1):
        forward.append(source(d) + low[d] * forward[-1])
    value = forward[-1] * inv[GX - 2]
    fs[GX - 1] = value
    for d in range(GX - 3, -1, -1):
        value = forward[d] * inv[d] + up[d] * value
        fs[1 + d] = value


def x_finish(fs, g, a, b, field):
    d = lax.axis_index("gx")
    flux_left, flux_right = fs[d], fs[d + 1]
    for k in range(NK):
        field[pl.ds(k * NJ, NJ), :] = (
            level(g, k) - level(a, k) * column(flux_left, k) + level(b, k) * column(flux_right, k)
        )
    return flux_left, flux_right


def y_source(f, xc, zc, field, fluxes, c_left, k):
    d = lax.axis_index("gx")
    lane = lanes(NJ)
    flux_left, flux_right = fluxes
    v, x = level(field, k), level(xc, k)
    before = jnp.where(lane == 0, column(c_left, k) * v - column(flux_left, k), rolled(x * v, 1, 1))
    last = jnp.where(d == GX - 1, 0.0, x * v + column(flux_right, k))
    after = jnp.where(lane == NI - 1, last, x * rolled(v, -1, 1))
    return z_terms(zc, field, k, level(f, k) + before + after)


def y_first_kernel(xs, got, g, a, b, yg, ya, yb, yw, yinv, xred, cl, send, fs, cs, field, src, base):
    f, p, xc, yc, zc, dp = parts(xs)
    d = lax.axis_index("gx")
    e = lax.axis_index("gy")
    lane = lanes(NJ)
    part = lambda n, q: rolled(got[n, pl.ds(0, NJ), :], -NK * q, 1)
    m = [part(n, 3) for n in range(GX)]
    low, inv, up = [None], [], []
    for n in range(GX - 1):
        dd = part(n, 4) + 1.0 / part(n, 5) + part(n + 1, 2)
        if n:
            low.append(m[n] * inv[-1])
            dd = dd - low[n] * m[n]
        inv.append(1.0 / dd)
        up.append(m[n + 1] * inv[n])
        xred[n], xred[GX + n], xred[2 * GX + n] = (low[n] if n else jnp.zeros_like(dd)), inv[n], up[n]
    x_fluxes(fs, lambda n: part(n + 1, 0) - part(n, 1), low, inv, up)
    cs[0] = jnp.zeros((NJ, NI), F32)
    for n in range(GX):
        cs[n + 1] = part(n, 5)
    c_left = cs[d]
    cl[...] = c_left
    fluxes = x_finish(fs, g, a, b, field)
    for k in range(NK):
        src[pl.ds(k * NJ, NJ), :] = y_source(f, xc, zc, field, fluxes, c_left, k)
        x = level(xc, k)
        x_left = jnp.where(lane == 0, column(c_left, k), rolled(x, 1, 1))
        base[pl.ds(k * NJ, NJ), :] = z_sum(zc, k, x_left + x + level(dp, k))
    ys, ws, invs, spike = [], [None], [], []
    for j in range(NJ):
        y = across(yc, j)
        diag = across(base, j)
        if j < NJ - 1:
            diag = diag + y
        else:
            diag = diag + jnp.where(e == GY - 1, y, 0.0)
        rhs = across(src, j)
        if j:
            y_before = across(yc, j - 1)
            w = y_before * invs[-1]
            ws.append(w)
            diag = diag + y_before - w * y_before
            rhs = rhs + w * ys[-1]
            spike.append(w * spike[-1])
            yw[pl.ds(j * NK, NK), :] = w
        else:
            spike.append(jnp.ones((NK, NI), F32))
            yw[pl.ds(0, NK), :] = jnp.zeros((NK, NI), F32)
        ys.append(rhs)
        invs.append(1.0 / diag)
        yinv[pl.ds(j * NK, NK), :] = invs[-1]
    for j in range(NJ - 1, -1, -1):
        if j == NJ - 1:
            gv, av, bv = ys[j] * invs[j], spike[j] * invs[j], invs[j]
            send[pl.ds(NK, NK), :] = gv
            send[pl.ds(4 * NK, NK), :] = bv + 1.0 / across(yc, j)
        else:
            w = ws[j + 1]
            gv, av, bv = ys[j] * invs[j] + w * gv, spike[j] * invs[j] + w * av, w * bv
        place = pl.ds(j * NK, NK)
        yg[place, :], ya[place, :], yb[place, :] = gv, av, bv
    send[pl.ds(0, NK), :] = gv
    send[pl.ds(2 * NK, NK), :] = av
    send[pl.ds(3 * NK, NK), :] = bv


def y_fluxes(fs, source, low, inv, up):
    zero = jnp.zeros((NK, NI), F32)
    fs[0], fs[GY] = zero, zero
    forward = [source(0)]
    for n in range(1, GY - 1):
        forward.append(source(n) + low(n) * forward[-1])
    value = forward[-1] * inv(GY - 2)
    fs[GY - 1] = value
    for n in range(GY - 3, -1, -1):
        value = forward[n] * inv(n) + up(n) * value
        fs[1 + n] = value


def y_finish(fs, yc, below, yg, ya, yb, field, terms):
    e = lax.axis_index("gy")
    flux_left, flux_right = fs[e], fs[e + 1]
    block = lambda ref, j: ref[pl.ds(j * NK, NK), :]
    p = [block(yg, j) - block(ya, j) * flux_left + block(yb, j) * flux_right for j in range(NJ)]
    for j in range(NJ):
        y = across(yc, j)
        if j:
            before = across(yc, j - 1) * p[j - 1]
        else:
            before = below[pl.ds(0, NK), :] * p[0] - flux_left
        if j < NJ - 1:
            after = y * p[j + 1]
        else:
            after = jnp.where(e == GY - 1, 0.0, y * p[j] + flux_right)
        field[pl.ds(j, NK, stride=NJ), :] = p[j]
        terms[pl.ds(j, NK, stride=NJ), :] = before + after


def x_again_kernel(xs, below, got, yg, ya, yb, mult, g, yred, send, fs, field, terms):
    f, p, xc, yc, zc, dp = parts(xs)
    part = lambda n, q: got[n, pl.ds(q * NK, NK), :]
    prev = None
    for n in range(GY - 1):
        dd = part(n, 4) + part(n + 1, 2)
        if n:
            m = part(n, 3)
            low = m * prev
            dd = dd - low * m
            yred[n] = low
        else:
            yred[n] = jnp.zeros_like(dd)
        prev = 1.0 / dd
        yred[GY + n] = prev
        yred[2 * GY + n] = part(n + 1, 3) * prev
    yred[GY - 1] = jnp.zeros((NK, NI), F32)
    yred[2 * GY - 1] = jnp.zeros((NK, NI), F32)
    yred[3 * GY - 1] = jnp.zeros((NK, NI), F32)
    y_fluxes(
        fs,
        lambda n: part(n + 1, 0) - part(n, 1),
        lambda n: yred[n],
        lambda n: yred[GY + n],
        lambda n: yred[2 * GY + n],
    )
    y_finish(fs, yc, below, yg, ya, yb, field, terms)
    lane = lanes(NJ)
    packed = jnp.zeros((NJ, NI), F32)
    group = 2
    for k0 in range(0, NK, group):
        rhs = jnp.concatenate(
            [z_terms(zc, field, k, level(f, k) + level(terms, k)) for k in range(k0, k0 + group)], axis=0
        )
        place = pl.ds(k0 * NJ, group * NJ)
        rhs = x_second_solve(rhs, lambda n: mult[pl.ds(n * ROWS + k0 * NJ, group * NJ), :])
        g[place, :] = rhs
        for k in range(k0, k0 + group):
            mine = rhs[(k - k0) * NJ : (k - k0 + 1) * NJ]
            packed = jnp.where(lane == k, column(mine, 0), packed)
            packed = jnp.where(lane == NK + k, column(mine, NI - 1), packed)
    send[...] = packed


def y_again_kernel(xs, got, g, a, b, xred, cl, yw, yinv, yg, send, fs, field, src):
    f, p, xc, yc, zc, dp = parts(xs)
    part = lambda n, q: rolled(got[n], -NK * q, 1)
    x_fluxes(
        fs,
        lambda n: part(n + 1, 0) - part(n, 1),
        [xred[n] for n in range(GX - 1)],
        [xred[GX + n] for n in range(GX - 1)],
        [xred[2 * GX + n] for n in range(GX - 1)],
    )
    fluxes = x_finish(fs, g, a, b, field)
    c_left = cl[...]
    for k in range(NK):
        src[pl.ds(k * NJ, NJ), :] = y_source(f, xc, zc, field, fluxes, c_left, k)
    block = lambda ref, j: ref[pl.ds(j * NK, NK), :]
    ys = []
    for j in range(NJ):
        rhs = across(src, j)
        if j:
            rhs = rhs + block(yw, j) * ys[-1]
        ys.append(rhs)
    value = None
    for j in range(NJ - 1, -1, -1):
        new = ys[j] * block(yinv, j)
        value = new if value is None else new + block(yw, j + 1) * value
        yg[pl.ds(j * NK, NK), :] = value
        if j == NJ - 1:
            send[pl.ds(NK, NK), :] = value
    send[pl.ds(0, NK), :] = value


def residual_kernel(xs, below, got, yg, ya, yb, yred, cl, field, near, far, coarse, fs, terms, tmp):
    f, p, xc, yc, zc, dp = parts(xs)
    d = lax.axis_index("gx")
    lane = lanes(NJ)
    part = lambda n, q: got[n, pl.ds(q * NK, NK), :]
    y_fluxes(
        fs,
        lambda n: part(n + 1, 0) - part(n, 1),
        lambda n: yred[n],
        lambda n: yred[GY + n],
        lambda n: yred[2 * GY + n],
    )
    y_finish(fs, yc, below, yg, ya, yb, field, terms)
    c_left = cl[...]
    main, rim = [], []
    for k in range(NK):
        v, x = level(field, k), level(xc, k)
        left = column(c_left, k)
        x_left = jnp.where(lane == 0, left, rolled(x, 1, 1))
        diag = z_sum(zc, k, x_left + x + y_left_of(yc, below, k) + level(yc, k) + level(dp, k))
        around = jnp.where(lane == 0, 0.0, x_left * rolled(v, 1, 1)) + jnp.where(lane == NI - 1, 0.0, x * rolled(v, -1, 1))
        main.append(level(f, k) - (diag * v - around - level(terms, k) - z_terms(zc, field, k, jnp.zeros((NJ, NI), F32))))
        last = jnp.where(d == GX - 1, 0.0, x * v)
        rim.append(jnp.where(lane == 0, left * v, jnp.where(lane == NI - 1, last, 0.0)))
    pairs = jnp.concatenate([main[2 * K] + main[2 * K + 1] for K in range(NK // 2)], axis=0)
    outer = jnp.concatenate([rim[2 * K] + rim[2 * K + 1] for K in range(NK // 2)], axis=0)
    tmp[...] = parity_shift(squeeze(pairs) + edges(outer))
    store_coarse(coarse, 0, tmp)
    odd = lax.rem(lax.axis_index("gy"), 2) == 1
    up, down = coarse[pl.ds(48, 16), :], coarse[pl.ds(0, 16), :]
    near[...] = jnp.where(odd, down, up)
    far[...] = jnp.where(odd, up, down)


def join_kernel(near, far, coarse, matrix, send):
    lower, upper = sorted_out(near, far, pl.ds(0, 16))
    send[pl.ds(0, 16), :] = lower
    send[pl.ds(16, 64), :] = coarse[...]
    send[pl.ds(80, 16), :] = upper


def coarse_matrix_kernel(coef, weight_out, x_low_out, x_up_out, y_out, z_out):
    e = lax.axis_index("gy")
    lane = lanes(8)
    wide = lanes(8, 4 * NI)
    level_k = lax.broadcasted_iota(jnp.int32, (8, 4 * NI), 0)

    def whole_coef(q, J):
        rows = pl.ds(NJ + (q // 2) * 104 + J * 8, 8)
        outs = []
        for m in range(4):
            even, odd = coef[2 * m, rows, :], coef[2 * m + 1, rows, :]
            if q % 2:
                even = rolled(even, 64, 1)
            else:
                odd = rolled(odd, 64, 1)
            outs.append(jnp.where(lane < 64, even, odd))
        return jnp.concatenate(outs, axis=1)

    y_before = whole_coef(1, 0)
    y_out[pl.ds(0, 8), :] = y_before
    for J in range(12):
        rows = pl.ds(J * 8, 8)
        x, y, z, damp = (whole_coef(q, J + 1) for q in range(4))
        x_left = jnp.where(wide == 0, 0.0, rolled(x, 1, 1))
        z_top = jnp.where(level_k == 7, 0.0, z)
        total = x_left + x + y_before + y + rolled(z_top, 1, 0) + z_top + damp
        at = e * 8 + J - 2
        valid = jnp.logical_and(at >= 0, at < 8 * GY)
        total = jnp.where(valid, total, 1.0)
        weight_out[0, rows, :] = total
        weight_out[1, rows, :] = jnp.where(valid, RELAX / total, 0.0)
        x_low_out[rows, :] = x_left
        x_up_out[rows, :] = jnp.where(wide == 4 * NI - 1, 0.0, x)
        y_out[pl.ds(J * 8 + 8, 8), :] = y
        z_out[rows, :] = z_top
        y_before = y


def coarse_kernel(got, weight, x_low, x_up, y_all, z_all, res_out, cor_out, tmp, cor_tmp):
    d = lax.axis_index("gx")
    lane = lanes(8)

    def whole_res(J):
        rows = pl.ds(J * 8, 8)
        outs = []
        for m in range(4):
            value = jnp.where(lane <= 64, got[2 * m, rows, :], 0.0) + jnp.where(lane >= 63, got[2 * m + 1, rows, :], 0.0)
            if m > 0:
                value = value + jnp.where(lane == 0, got[2 * m - 1, rows, :], 0.0)
            if m < 3:
                value = value + jnp.where(lane == NI - 1, got[2 * m + 2, rows, :], 0.0)
            outs.append(value)
        return outs

    at = lambda ref, J: ref[pl.ds(J * 8, 8), :]
    diag = lambda J: weight[0, pl.ds(J * 8, 8), :]
    scale = lambda J: weight[1, pl.ds(J * 8, 8), :]
    res = []
    for J in range(12):
        outs = whole_res(J)
        if 2 <= J < 10:
            mine = outs[0]
            for m in range(1, 4):
                mine = jnp.where(d // 2 == m, outs[m], mine)
            mine = jnp.where(lax.rem(d, 2) == 1, rolled(mine, 64, 1), mine)
            tmp[pl.ds(J - 2, 8, stride=8), :] = mine
        res.append(jnp.concatenate(outs, axis=1))
    cor = {J: scale(J) * res[J] for J in range(12)}
    for low, high in ((1, 11), (2, 10)):
        new = {}
        for J in range(low, high):
            v = cor[J]
            z_top = at(z_all, J)
            applied = (
                diag(J) * v
                - at(x_low, J) * rolled(v, 1, 1)
                - at(x_up, J) * rolled(v, -1, 1)
                - at(y_all, J) * cor[J - 1]
                - at(y_all, J + 1) * cor[J + 1]
                - (rolled(z_top * v, 1, 0) + z_top * rolled(v, -1, 0))
            )
            new[J] = v + scale(J) * (res[J] - applied)
        cor = new
    for J in range(8):
        for m in range(4):
            cor_tmp[m, pl.ds(J, 8, stride=8), :] = cor[J + 2][:, m * NI : (m + 1) * NI]
    for m in range(4):
        cor_out[:, pl.ds(m * NI, NI)] = cor_tmp[m]
    res_out[...] = tmp[:, :64]


def spread(value, axis, count):
    many = jnp.broadcast_to(value[None], (count,) + value.shape)
    return lax.all_to_all(many, axis, split_axis=0, concat_axis=0, tiled=True)


def swap(near, far):
    pairs = [(n, n ^ 1) for n in range(GY)]
    others = [(n, (n + 1) % GY if n % 2 else (n - 1) % GY) for n in range(GY)]
    return lax.ppermute(near, "gy", pairs), lax.ppermute(far, "gy", others)


def body(forcing, pressure_in, x_coupling, y_coupling, z_coupling, damping):
    args = [v.reshape(ROWS, NI) for v in (forcing, pressure_in, x_coupling, y_coupling, z_coupling, damping)]
    whole = sds(ROWS, NI)
    kept = sds((2 * len(STEPS) + 1) * ROWS, NI)
    xs, near, far, coef = call(
        first_kernel,
        [sds(6 * ROWS, NI), sds(80, NI), sds(80, NI), sds(128, NI)],
        *[pltpu.with_memory_space_constraint(v, pltpu.HBM) for v in args],
        scratch=[(128, NI)],
        hbm=True,
        sems=6,
    )
    near, far = swap(near, far)
    g, a, b, mult, packed = call(x_first_kernel, [whole, whole, whole, kept, sds(NJ, NI)], xs, flops=10**8)
    below, g, a, b, mult, send = call(
        x_rim_kernel,
        [sds(NK, NI), whole, whole, whole, kept, sds(NJ + 208, NI)],
        xs, near, far, coef, packed, g, a, b, mult,
        aliases={5: 1, 6: 2, 7: 3, 8: 4},
    )
    got_coef = got = spread(send, "gx", GX)
    yg, ya, yb, yw, yinv, xred, cl, send = call(
        y_first_kernel,
        [whole] * 5 + [sds(3 * GX, NJ, NI), sds(NJ, NI), sds(5 * NK, NI)],
        xs, got, g, a, b,
        scratch=[(GX + 1, NJ, NI), (GX + 1, NJ, NI), (ROWS, NI), (ROWS, NI), (ROWS, NI)],
    )
    got = spread(send, "gy", GY)
    g, yred, send = call(
        x_again_kernel,
        [whole, sds(3 * GY, NK, NI), sds(NJ, NI)],
        xs, below, got, yg, ya, yb, mult,
        scratch=[(GY + 1, NK, NI), (ROWS, NI), (ROWS, NI)],
    )
    got = spread(send, "gx", GX)
    yg, send = call(
        y_again_kernel,
        [whole, sds(2 * NK, NI)],
        xs, got, g, a, b, xred, cl, yw, yinv,
        scratch=[(GX + 1, NJ, NI), (ROWS, NI), (ROWS, NI)],
    )
    got = spread(send, "gy", GY)
    field, near, far, coarse = call(
        residual_kernel,
        [whole, sds(16, NI), sds(16, NI), sds(64, NI)],
        xs, below, got, yg, ya, yb, yred, cl,
        scratch=[(GY + 1, NK, NI), (ROWS, NI), (128, NI)],
    )
    near, far = swap(near, far)
    rows = sds(96, 4 * NI)
    matrix = call(
        coarse_matrix_kernel, [sds(2, 96, 4 * NI), rows, rows, sds(104, 4 * NI), rows], got_coef, flops=10**7
    )
    (send,) = call(join_kernel, [sds(96, NI)], near, far, coarse, matrix[-1])
    got = spread(send, "gx", GX)
    res, cor = call(coarse_kernel, [sds(64, 64), sds(64, 512)], got, *matrix, scratch=[(64, NI), (4, 64, NI)])
    return field.reshape(NK, NJ, NI), res.reshape(8, 8, 64), cor.reshape(8, 8, 512)


def solution(mesh):
    spec = P(None, "gy", "gx")
    return jax.shard_map(
        body, mesh=mesh, in_specs=(spec,) * 6, out_specs=(spec, spec, P(None, "gy", None)), check_vma=False
    )
```

```python
import functools

import jax
import jax.numpy as jnp
from jax import lax
from jax.experimental import pallas as pl
from jax.experimental.pallas import tpu as pltpu
from jax.sharding import PartitionSpec as P

RELAX = 0.8
NK, NJ, NI = 16, 16, 128
ROWS = NK * NJ
GX, GY = 8, 16
STEPS = (1, 2, 4, 8, 16, 32, 64)
F32 = jnp.float32


def sds(*shape):
    return jax.ShapeDtypeStruct(shape, F32)


def call(kernel, outs, *args, scratch=(), hbm=False, aliases={}, sems=0, flops=None):
    spec = pl.BlockSpec(memory_space=pltpu.VMEM)
    inside = pl.BlockSpec(memory_space=pltpu.HBM) if hbm else spec
    shapes = [pltpu.VMEM(v, F32) for v in scratch]
    if sems:
        shapes.append(pltpu.SemaphoreType.DMA((sems,)))
    cost = None if flops is None else pl.CostEstimate(flops=flops, bytes_accessed=1 << 20, transcendentals=0)
    return pl.pallas_call(
        kernel,
        out_shape=outs,
        in_specs=[inside] * len(args),
        out_specs=[spec] * len(outs),
        scratch_shapes=shapes,
        input_output_aliases=aliases,
        cost_estimate=cost,
        compiler_params=pltpu.CompilerParams(vmem_limit_bytes=16 * 1024 * 1024),
    )(*args)


def parts(xs):
    return [xs.at[pl.ds(n * ROWS, ROWS), :] for n in range(6)]


def lanes(rows, width=NI):
    return lax.broadcasted_iota(jnp.int32, (rows, width), 1)


def rolled(value, amount, axis):
    return pltpu.roll(value, amount % value.shape[axis], axis)


def level(ref, k):
    return ref[pl.ds(k * NJ, NJ), :]


def across(ref, j, count=NK, stride=NJ):
    return ref[pl.ds(j, count, stride=stride), :]


def column(value, k):
    return jnp.broadcast_to(value[:, k : k + 1], (value.shape[0], NI))


def z_pair(zc, k):
    return (level(zc, k - 1) if k > 0 else None, level(zc, k) if k < NK - 1 else None)


def z_sum(zc, k, base):
    low, top = z_pair(zc, k)
    if low is not None:
        base = base + low
    if top is not None:
        base = base + top
    return base


def z_terms(zc, field, k, base):
    low, top = z_pair(zc, k)
    if low is not None:
        base = base + low * level(field, k - 1)
    if top is not None:
        base = base + top * level(field, k + 1)
    return base


def y_left_of(yc, halo, k):
    row = lax.broadcasted_iota(jnp.int32, (NJ, NI), 0)
    return jnp.where(row == 0, halo[pl.ds(k, 1), :], rolled(level(yc, k), 1, 0))


def squeeze(values, scale=0.125, start=0):
    source = lax.broadcasted_iota(jnp.int32, (NI, NI), 0)
    target = lax.broadcasted_iota(jnp.int32, (NI, NI), 1)
    matrix = jnp.where(source // 2 + start == target, scale, 0.0).astype(F32)
    return jnp.dot(values, matrix, precision=lax.Precision.HIGHEST, preferred_element_type=F32)


def edges(values, scale=0.125):
    source = lax.broadcasted_iota(jnp.int32, (NI, NI), 0)
    target = lax.broadcasted_iota(jnp.int32, (NI, NI), 1)
    hit = ((source == NI - 1) & (target == 64)) | ((source == 0) & (target == NI - 1))
    matrix = jnp.where(hit, scale, 0.0).astype(F32)
    return jnp.dot(values, matrix, precision=lax.Precision.HIGHEST, preferred_element_type=F32)


def parity_shift(values):
    odd = lax.rem(lax.axis_index("gx"), 2) == 1
    return jnp.where(odd, rolled(values, 64, 1), values)


def store_coarse(out, base, tmp):
    for J in range(NJ // 2):
        out[pl.ds(base + J * 8, 8), :] = across(tmp, 2 * J, 8) + across(tmp, 2 * J + 1, 8)


def first_kernel(fh, ph, xh, yh, zh, dh, xs, near, far, tmp, sems):
    copies = {
        n: pltpu.make_async_copy(ref, xs.at[pl.ds(n * ROWS, ROWS), :], sems.at[n])
        for n, ref in enumerate((fh, ph, xh, yh, zh, dh))
    }
    for n in (1, 3, 0, 2, 4, 5):
        copies[n].start()
    copies[1].wait()
    copies[3].wait()
    f, p, xc, yc, zc, dp = parts(xs)
    odd = lax.rem(lax.axis_index("gy"), 2) == 1

    def put(place, up, down):
        near[place, :] = jnp.where(odd, down, up)
        far[place, :] = jnp.where(odd, up, down)

    put(pl.ds(0, NK), across(p, NJ - 1), across(p, 0))
    put(pl.ds(NK, NK), across(yc, NJ - 1), across(yc, 0))
    tmp[...] = squeeze(across(yc, NJ - 2) + across(yc, NJ - 1))
    row = tmp[pl.ds(0, 8, stride=2), :] + tmp[pl.ds(1, 8, stride=2), :]
    put(pl.ds(2 * NK, 8), row, row)
    for n in (0, 2, 4, 5):
        copies[n].wait()


def sorted_out(near, far, place):
    e = lax.axis_index("gy")
    odd = lax.rem(e, 2) == 1
    one, two = near[place, :], far[place, :]
    return (
        jnp.where(e == 0, 0.0, jnp.where(odd, one, two)),
        jnp.where(e == GY - 1, 0.0, jnp.where(odd, two, one)),
    )


def x_matrix(x, rest):
    d = lax.axis_index("gx")
    lane = lanes(x.shape[0])
    inner = jnp.logical_or(lane < NI - 1, d == GX - 1)
    diag = jnp.where(lane == 0, 0.0, rolled(x, 1, 1)) + jnp.where(inner, x, 0.0) + rest
    return diag, jnp.where(lane == NI - 1, 0.0, -x)


def x_eliminate(diag, off, rhs, keep):
    wide = lanes(diag.shape[0])
    ends = jnp.where(jnp.logical_or(wide == 0, wide == NI - 1), 1.0, 0.0).astype(F32)
    for n, s in enumerate(STEPS):
        inv = 1.0 / diag
        low = rolled(off, s, 1)
        alpha = -low * rolled(inv, s, 1)
        beta = -off * rolled(inv, -s, 1)
        keep(2 * n, alpha)
        keep(2 * n + 1, beta)
        diag = diag + alpha * low + beta * off
        rhs = rhs + alpha * rolled(rhs, s, 1) + beta * rolled(rhs, -s, 1)
        if s < NI // 2:
            off = beta * rolled(off, -s, 1)
            ends = ends + alpha * rolled(ends, s, 1) + beta * rolled(ends, -s, 1)
    inv = 1.0 / diag
    keep(2 * len(STEPS), inv)
    other = rolled(ends, NI // 2, 1)
    left = jnp.where(wide < NI // 2, ends, alpha * other)
    right = jnp.where(wide < NI // 2, beta * other, ends)
    return rhs * inv, left * inv, right * inv


def x_picks(g, a, b, x):
    return column(g, 0), column(g, NI - 1), column(a, 0), column(b, 0), column(b, NI - 1), column(x, NI - 1)


def x_first_kernel(xs, g, a, b, mult, packed_out, coarse, tmp):
    f, p, xc, yc, zc, dp = parts(xs)
    lane = lanes(NJ)
    row = lax.broadcasted_iota(jnp.int32, (NJ, NI), 0)
    packed = jnp.zeros((NJ, NI), F32)
    group = 2
    for k0 in range(0, NK, group):
        diag, off, rhs = [], [], []
        for k in range(k0, k0 + group):
            y, v = level(yc, k), level(p, k)
            y_left = jnp.where(row == 0, 0.0, rolled(y, 1, 0))
            matrix = x_matrix(level(xc, k), z_sum(zc, k, y_left + y + level(dp, k)))
            diag.append(matrix[0])
            off.append(matrix[1])
            after = jnp.where(row == NJ - 1, 0.0, rolled(v, -1, 0))
            rhs.append(z_terms(zc, p, k, level(f, k) + y_left * rolled(v, 1, 0) + y * after))
        diag, off, rhs = (jnp.concatenate(v, axis=0) for v in (diag, off, rhs))
        place = pl.ds(k0 * NJ, group * NJ)

        def keep(n, value):
            mult[pl.ds(n * ROWS + k0 * NJ, group * NJ), :] = value

        rhs, left, right = x_eliminate(diag, off, rhs, keep)
        g[place, :], a[place, :], b[place, :] = rhs, left, right
        for k in range(k0, k0 + group):
            part = slice((k - k0) * NJ, (k - k0 + 1) * NJ)
            for q, pick in enumerate(x_picks(rhs[part], left[part], right[part], level(xc, k))):
                packed = jnp.where(lane == q * NK + k, pick, packed)
    packed_out[...] = packed
    for q, two in enumerate(((xc, yc), (zc, dp))):
        total = jnp.zeros((128, NI), F32)
        for half, ref in enumerate(two):
            pairs = jnp.concatenate([level(ref, 2 * K) + level(ref, 2 * K + 1) for K in range(NK // 2)], axis=0)
            total = total + squeeze(pairs, start=64 * half)
        tmp[...] = total
        store_coarse(coarse, q * 64, tmp)


def x_rim_kernel(xs, near, far, coarse, packed, g_in, a_in, b_in, mult_in, below, g, a, b, mult, send):
    f, p, xc, yc, zc, dp = parts(xs)
    lane = lanes(NK)
    row = lax.broadcasted_iota(jnp.int32, (NK, NI), 0)

    def lifted(j):
        z, v = across(zc, j), across(p, j)
        top = jnp.where(row == NK - 1, 0.0, z)
        low = rolled(top, 1, 0)
        return low, top, low * rolled(v, 1, 0) + top * rolled(v, -1, 0)

    p_below, p_above = sorted_out(near, far, pl.ds(0, NK))
    y_left, _ = sorted_out(near, far, pl.ds(NK, NK))
    below[...] = y_left
    low, top, z_part = lifted(0)
    y = across(yc, 0)
    diag, off = x_matrix(across(xc, 0), low + top + y + y_left + across(dp, 0))
    rhs = across(f, 0) + y_left * p_below + y * across(p, 1) + z_part

    def keep(n, value):
        mult[pl.ds(n * ROWS, NK, stride=NJ), :] = value

    rhs, left, right = x_eliminate(diag, off, rhs, keep)
    first = pl.ds(0, NK, stride=NJ)
    g[first, :], a[first, :], b[first, :] = rhs, left, right
    line = jnp.zeros((NK, NI), F32)
    for q, pick in enumerate(x_picks(rhs, left, right, across(xc, 0))):
        line = line + jnp.where(lane == q * NK + row, pick, 0.0)
    line = jnp.sum(line, axis=0, keepdims=True)

    j = NJ - 1
    _, _, z_part = lifted(j)
    y = across(yc, j)
    rhs = across(f, j) + across(yc, j - 1) * across(p, j - 1) + y * p_above + z_part
    rhs = x_second_solve(rhs, lambda n: mult_in[pl.ds(n * ROWS + j, NK, stride=NJ), :])
    g[pl.ds(j, NK, stride=NJ), :] = rhs
    last = jnp.where(lane == row, column(rhs, 0), 0.0) + jnp.where(lane == NK + row, column(rhs, NI - 1), 0.0)
    last = jnp.sum(last, axis=0, keepdims=True)
    was = packed[...]
    was = jnp.where(row == 0, line, was)
    send[pl.ds(0, NJ), :] = jnp.where(jnp.logical_and(row == NJ - 1, lane < 2 * NK), last, was)
    send[pl.ds(NJ, 128), :] = coarse[...]
    send[pl.ds(NJ + 128, 8), :] = sorted_out(near, far, pl.ds(2 * NK, 8))[0]


def x_second_solve(rhs, kept):
    for n, s in enumerate(STEPS):
        rhs = rhs + kept(2 * n) * rolled(rhs, s, 1) + kept(2 * n + 1) * rolled(rhs, -s, 1)
    return rhs * kept(2 * len(STEPS))


def x_fluxes(fs, source, low, inv, up):
    zero = jnp.zeros((NJ, NI), F32)
    fs[0], fs[GX] = zero, zero
    forward = [source(0)]
    for d in range(1, GX - 1):
        forward.append(source(d) + low[d] * forward[-1])
    value = forward[-1] * inv[GX - 2]
    fs[GX - 1] = value
    for d in range(GX - 3, -1, -1):
        value = forward[d] * inv[d] + up[d] * value
        fs[1 + d] = value


def x_finish(fs, g, a, b, field):
    d = lax.axis_index("gx")
    flux_left, flux_right = fs[d], fs[d + 1]
    for k in range(NK):
        field[pl.ds(k * NJ, NJ), :] = (
            level(g, k) - level(a, k) * column(flux_left, k) + level(b, k) * column(flux_right, k)
        )
    return flux_left, flux_right


def y_source(f, xc, zc, field, fluxes, c_left, k):
    d = lax.axis_index("gx")
    lane = lanes(NJ)
    flux_left, flux_right = fluxes
    v, x = level(field, k), level(xc, k)
    before = jnp.where(lane == 0, column(c_left, k) * v - column(flux_left, k), rolled(x * v, 1, 1))
    last = jnp.where(d == GX - 1, 0.0, x * v + column(flux_right, k))
    after = jnp.where(lane == NI - 1, last, x * rolled(v, -1, 1))
    return z_terms(zc, field, k, level(f, k) + before + after)


def y_first_kernel(xs, got, g, a, b, yg, ya, yb, yw, yinv, xred, cl, send, fs, cs, field, src, base):
    f, p, xc, yc, zc, dp = parts(xs)
    d = lax.axis_index("gx")
    e = lax.axis_index("gy")
    lane = lanes(NJ)
    part = lambda n, q: rolled(got[n, pl.ds(0, NJ), :], -NK * q, 1)
    m = [part(n, 3) for n in range(GX)]
    low, inv, up = [None], [], []
    for n in range(GX - 1):
        dd = part(n, 4) + 1.0 / part(n, 5) + part(n + 1, 2)
        if n:
            low.append(m[n] * inv[-1])
            dd = dd - low[n] * m[n]
        inv.append(1.0 / dd)
        up.append(m[n + 1] * inv[n])
        xred[n], xred[GX + n], xred[2 * GX + n] = (low[n] if n else jnp.zeros_like(dd)), inv[n], up[n]
    x_fluxes(fs, lambda n: part(n + 1, 0) - part(n, 1), low, inv, up)
    cs[0] = jnp.zeros((NJ, NI), F32)
    for n in range(GX):
        cs[n + 1] = part(n, 5)
    c_left = cs[d]
    cl[...] = c_left
    fluxes = x_finish(fs, g, a, b, field)
    for k in range(NK):
        src[pl.ds(k * NJ, NJ), :] = y_source(f, xc, zc, field, fluxes, c_left, k)
        x = level(xc, k)
        x_left = jnp.where(lane == 0, column(c_left, k), rolled(x, 1, 1))
        base[pl.ds(k * NJ, NJ), :] = z_sum(zc, k, x_left + x + level(dp, k))
    ys, ws, invs, spike = [], [None], [], []
    for j in range(NJ):
        y = across(yc, j)
        diag = across(base, j)
        if j < NJ - 1:
            diag = diag + y
        else:
            diag = diag + jnp.where(e == GY - 1, y, 0.0)
        rhs = across(src, j)
        if j:
            y_before = across(yc, j - 1)
            w = y_before * invs[-1]
            ws.append(w)
            diag = diag + y_before - w * y_before
            rhs = rhs + w * ys[-1]
            spike.append(w * spike[-1])
            yw[pl.ds(j * NK, NK), :] = w
        else:
            spike.append(jnp.ones((NK, NI), F32))
            yw[pl.ds(0, NK), :] = jnp.zeros((NK, NI), F32)
        ys.append(rhs)
        invs.append(1.0 / diag)
        yinv[pl.ds(j * NK, NK), :] = invs[-1]
    for j in range(NJ - 1, -1, -1):
        if j == NJ - 1:
            gv, av, bv = ys[j] * invs[j], spike[j] * invs[j], invs[j]
            send[pl.ds(NK, NK), :] = gv
            send[pl.ds(4 * NK, NK), :] = bv + 1.0 / across(yc, j)
        else:
            w = ws[j + 1]
            gv, av, bv = ys[j] * invs[j] + w * gv, spike[j] * invs[j] + w * av, w * bv
        place = pl.ds(j * NK, NK)
        yg[place, :], ya[place, :], yb[place, :] = gv, av, bv
    send[pl.ds(0, NK), :] = gv
    send[pl.ds(2 * NK, NK), :] = av
    send[pl.ds(3 * NK, NK), :] = bv


def y_fluxes(fs, source, low, inv, up):
    zero = jnp.zeros((NK, NI), F32)
    fs[0], fs[GY] = zero, zero
    forward = [source(0)]
    for n in range(1, GY - 1):
        forward.append(source(n) + low(n) * forward[-1])
    value = forward[-1] * inv(GY - 2)
    fs[GY - 1] = value
    for n in range(GY - 3, -1, -1):
        value = forward[n] * inv(n) + up(n) * value
        fs[1 + n] = value


def y_finish(fs, yc, below, yg, ya, yb, field, terms):
    e = lax.axis_index("gy")
    flux_left, flux_right = fs[e], fs[e + 1]
    block = lambda ref, j: ref[pl.ds(j * NK, NK), :]
    p = [block(yg, j) - block(ya, j) * flux_left + block(yb, j) * flux_right for j in range(NJ)]
    for j in range(NJ):
        y = across(yc, j)
        if j:
            before = across(yc, j - 1) * p[j - 1]
        else:
            before = below[pl.ds(0, NK), :] * p[0] - flux_left
        if j < NJ - 1:
            after = y * p[j + 1]
        else:
            after = jnp.where(e == GY - 1, 0.0, y * p[j] + flux_right)
        field[pl.ds(j, NK, stride=NJ), :] = p[j]
        terms[pl.ds(j, NK, stride=NJ), :] = before + after


def x_again_kernel(xs, below, mine, other, yg, ya, yb, mult, w, g, yred, send, fs, field, terms):
    f, p, xc, yc, zc, dp = parts(xs)
    odd = lax.rem(lax.axis_index("gy"), 2) == 1

    def part(n, q):
        one, two = mine[n // 2, pl.ds(q * NK, NK), :], other[n // 2, pl.ds(q * NK, NK), :]
        return jnp.where(odd, one, two) if n % 2 else jnp.where(odd, two, one)

    prev = None
    for n in range(GY - 1):
        dd = part(n, 4) + part(n + 1, 2)
        if n:
            m = part(n, 3)
            low = m * prev
            dd = dd - low * m
            yred[n] = low
        else:
            yred[n] = jnp.zeros_like(dd)
        prev = 1.0 / dd
        yred[GY + n] = prev
        yred[2 * GY + n] = part(n + 1, 3) * prev
    yred[GY - 1] = jnp.zeros((NK, NI), F32)
    yred[2 * GY - 1] = jnp.zeros((NK, NI), F32)
    yred[3 * GY - 1] = jnp.zeros((NK, NI), F32)
    y_fluxes(
        fs,
        lambda n: part(n + 1, 0) - part(n, 1),
        lambda n: yred[n],
        lambda n: yred[GY + n],
        lambda n: yred[2 * GY + n],
    )
    y_finish(fs, yc, below, yg, ya, yb, field, terms)
    lane = lanes(NJ)
    packed = jnp.zeros((NJ, NI), F32)
    group = 2
    for k0 in range(0, NK, group):
        rhs = jnp.concatenate(
            [z_terms(zc, field, k, level(f, k) + level(terms, k)) for k in range(k0, k0 + group)], axis=0
        )
        place = pl.ds(k0 * NJ, group * NJ)
        rhs = x_second_solve(rhs, lambda n: mult[pl.ds(n * ROWS + k0 * NJ, group * NJ), :])
        g[place, :] = rhs
        for k in range(k0, k0 + group):
            mine = rhs[(k - k0) * NJ : (k - k0 + 1) * NJ]
            packed = jnp.where(lane == k, column(mine, 0), packed)
            packed = jnp.where(lane == NK + k, column(mine, NI - 1), packed)
    send[...] = packed


def y_again_kernel(xs, got, g, a, b, xred, cl, yw, yinv, yg, send, fs, field, src):
    f, p, xc, yc, zc, dp = parts(xs)
    part = lambda n, q: rolled(got[n], -NK * q, 1)
    x_fluxes(
        fs,
        lambda n: part(n + 1, 0) - part(n, 1),
        [xred[n] for n in range(GX - 1)],
        [xred[GX + n] for n in range(GX - 1)],
        [xred[2 * GX + n] for n in range(GX - 1)],
    )
    fluxes = x_finish(fs, g, a, b, field)
    c_left = cl[...]
    for k in range(NK):
        src[pl.ds(k * NJ, NJ), :] = y_source(f, xc, zc, field, fluxes, c_left, k)
    block = lambda ref, j: ref[pl.ds(j * NK, NK), :]
    ys = []
    for j in range(NJ):
        rhs = across(src, j)
        if j:
            rhs = rhs + block(yw, j) * ys[-1]
        ys.append(rhs)
    value = None
    for j in range(NJ - 1, -1, -1):
        new = ys[j] * block(yinv, j)
        value = new if value is None else new + block(yw, j + 1) * value
        yg[pl.ds(j * NK, NK), :] = value
        if j == NJ - 1:
            send[pl.ds(NK, NK), :] = value
    send[pl.ds(0, NK), :] = value


def residual_kernel(xs, below, got, yg, ya, yb, yred, cl, field, coarse, fs, terms, tmp):
    f, p, xc, yc, zc, dp = parts(xs)
    d = lax.axis_index("gx")
    lane = lanes(NJ)
    part = lambda n, q: got[n, pl.ds(q * NK, NK), :]
    y_fluxes(
        fs,
        lambda n: part(n + 1, 0) - part(n, 1),
        lambda n: yred[n],
        lambda n: yred[GY + n],
        lambda n: yred[2 * GY + n],
    )
    y_finish(fs, yc, below, yg, ya, yb, field, terms)
    c_left = cl[...]
    main, rim = [], []
    for k in range(NK):
        v, x = level(field, k), level(xc, k)
        left = column(c_left, k)
        x_left = jnp.where(lane == 0, left, rolled(x, 1, 1))
        diag = z_sum(zc, k, x_left + x + y_left_of(yc, below, k) + level(yc, k) + level(dp, k))
        around = jnp.where(lane == 0, 0.0, x_left * rolled(v, 1, 1)) + jnp.where(lane == NI - 1, 0.0, x * rolled(v, -1, 1))
        main.append(level(f, k) - (diag * v - around - level(terms, k) - z_terms(zc, field, k, jnp.zeros((NJ, NI), F32))))
        last = jnp.where(d == GX - 1, 0.0, x * v)
        rim.append(jnp.where(lane == 0, left * v, jnp.where(lane == NI - 1, last, 0.0)))
    pairs = jnp.concatenate([main[2 * K] + main[2 * K + 1] for K in range(NK // 2)], axis=0)
    outer = jnp.concatenate([rim[2 * K] + rim[2 * K + 1] for K in range(NK // 2)], axis=0)
    tmp[...] = parity_shift(squeeze(pairs) + edges(outer))
    store_coarse(coarse, 0, tmp)


def coarse_matrix_kernel(coef, w, xl, xu, yl, yu, zl, zu):
    lane = lanes(8)
    wide = lanes(8, 4 * NI)
    level_k = lax.broadcasted_iota(jnp.int32, (8, 4 * NI), 0)

    def whole(at, half):
        rows = pl.ds(at, 8)
        outs = []
        for m in range(4):
            even, odd = coef[2 * m, rows, :], coef[2 * m + 1, rows, :]
            if half:
                even = rolled(even, 64, 1)
            else:
                odd = rolled(odd, 64, 1)
            outs.append(jnp.where(lane < 64, even, odd))
        return jnp.concatenate(outs, axis=1)

    y_before = whole(NJ + 128, 0)
    for J in range(8):
        rows = pl.ds(J * 8, 8)
        x, y, z, damp = (whole(NJ + (q // 2) * 64 + J * 8, q % 2) for q in range(4))
        x_left = jnp.where(wide == 0, 0.0, rolled(x, 1, 1))
        z_top = jnp.where(level_k == 7, 0.0, z)
        z_low = rolled(z_top, 1, 0)
        weight = RELAX / (x_left + x + y_before + y + z_low + z_top + damp)
        w[rows, :] = weight
        xl[rows, :] = weight * x_left
        xu[rows, :] = jnp.where(wide == 4 * NI - 1, 0.0, weight * x)
        yl[rows, :] = weight * y_before
        yu[rows, :] = weight * y
        zl[rows, :] = weight * z_low
        zu[rows, :] = weight * z_top
        y_before = y


def eight(ref, J):
    return ref[pl.ds(J * 8, 8), :]


def flat_terms(v, J, xl, xu, zl, zu):
    return (
        eight(xl, J) * rolled(v, 1, 1)
        + eight(xu, J) * rolled(v, -1, 1)
        + eight(zl, J) * rolled(v, 1, 0)
        + eight(zu, J) * rolled(v, -1, 0)
    )


def coarse_one_kernel(got, w, xl, xu, yl, yu, zl, zu, res_out, c0, c1, near, far, tmp):
    d = lax.axis_index("gx")
    lane = lanes(8)
    for J in range(8):
        rows = pl.ds(J * 8, 8)
        outs = []
        for m in range(4):
            value = jnp.where(lane <= 64, got[2 * m, rows, :], 0.0) + jnp.where(lane >= 63, got[2 * m + 1, rows, :], 0.0)
            if m > 0:
                value = value + jnp.where(lane == 0, got[2 * m - 1, rows, :], 0.0)
            if m < 3:
                value = value + jnp.where(lane == NI - 1, got[2 * m + 2, rows, :], 0.0)
            outs.append(value)
        mine = outs[0]
        for m in range(1, 4):
            mine = jnp.where(d // 2 == m, outs[m], mine)
        mine = jnp.where(lax.rem(d, 2) == 1, rolled(mine, 64, 1), mine)
        tmp[pl.ds(J, 8, stride=8), :] = mine
        c0[rows, :] = eight(w, J) * jnp.concatenate(outs, axis=1)
    for J in range(8):
        v = eight(c0, J)
        new = (2.0 - RELAX) * v + flat_terms(v, J, xl, xu, zl, zu)
        if J:
            new = new + eight(yl, J) * eight(c0, J - 1)
        if J < 7:
            new = new + eight(yu, J) * eight(c0, J + 1)
        c1[pl.ds(J * 8, 8), :] = new
    odd = lax.rem(lax.axis_index("gy"), 2) == 1
    for n, (up, down) in enumerate(((eight(c0, 7), eight(c0, 0)), (eight(c1, 7), eight(c1, 0)), (eight(yu, 7), eight(yl, 0)))):
        near[pl.ds(n * 8, 8), :] = jnp.where(odd, down, up)
        far[pl.ds(n * 8, 8), :] = jnp.where(odd, up, down)
    res_out[...] = tmp[:, :64]


def coarse_two_kernel(c0, c1, xl, xu, yl, yu, zl, zu, c2):
    for J in range(8):
        v = eight(c1, J)
        new = eight(c0, J) + (1.0 - RELAX) * v + flat_terms(v, J, xl, xu, zl, zu)
        if J:
            new = new + eight(yl, J) * eight(c1, J - 1)
        if J < 7:
            new = new + eight(yu, J) * eight(c1, J + 1)
        c2[pl.ds(J * 8, 8), :] = new


def coarse_three_kernel(near, far, c0, c2, xl, xu, yl, yu, zl, zu, out, tmp):
    sides = [sorted_out(near, far, pl.ds(n * 8, 8)) for n in range(3)]
    extra = {}
    for side, (J, inward, coupling) in enumerate(((0, 1, yl), (7, 6, yu))):
        their0, their1, weight = (pair[side] for pair in sides)
        change = eight(coupling, J) * their0
        beside = their1 + weight * eight(c0, J)
        extra[J] = (1.0 - RELAX) * change + flat_terms(change, J, xl, xu, zl, zu) + eight(coupling, J) * beside
        extra[inward] = eight(coupling, inward) * change
    for J in range(8):
        new = eight(c2, J)
        if J in extra:
            new = new + extra[J]
        for m in range(4):
            tmp[m, pl.ds(J, 8, stride=8), :] = new[:, m * NI : (m + 1) * NI]
    for m in range(4):
        out[:, pl.ds(m * NI, NI)] = tmp[m]


def spread(value, axis, count):
    many = jnp.broadcast_to(value[None], (count,) + value.shape)
    return lax.all_to_all(many, axis, split_axis=0, concat_axis=0, tiled=True)


def spread_by_core(value):
    groups = [list(range(0, GY, 2)), list(range(1, GY, 2))]
    many = jnp.broadcast_to(value[None], (GY // 2,) + value.shape)
    mine = lax.all_to_all(many, "gy", split_axis=0, concat_axis=0, tiled=True, axis_index_groups=groups)
    return mine, lax.ppermute(mine, "gy", [(n, n ^ 1) for n in range(GY)])


def swap(near, far):
    pairs = [(n, n ^ 1) for n in range(GY)]
    others = [(n, (n + 1) % GY if n % 2 else (n - 1) % GY) for n in range(GY)]
    return lax.ppermute(near, "gy", pairs), lax.ppermute(far, "gy", others)


def body(forcing, pressure_in, x_coupling, y_coupling, z_coupling, damping):
    args = [v.reshape(ROWS, NI) for v in (forcing, pressure_in, x_coupling, y_coupling, z_coupling, damping)]
    whole = sds(ROWS, NI)
    kept = sds((2 * len(STEPS) + 1) * ROWS, NI)
    xs, near, far = call(
        first_kernel,
        [sds(6 * ROWS, NI), sds(40, NI), sds(40, NI)],
        *[pltpu.with_memory_space_constraint(v, pltpu.HBM) for v in args],
        scratch=[(NK, NI)],
        hbm=True,
        sems=6,
    )
    near, far = swap(near, far)
    g, a, b, mult, packed, coef = call(
        x_first_kernel,
        [whole, whole, whole, kept, sds(NJ, NI), sds(128, NI)],
        xs,
        scratch=[(128, NI)],
        flops=10**8,
    )
    below, g, a, b, mult, send = call(
        x_rim_kernel,
        [sds(NK, NI), whole, whole, whole, kept, sds(NJ + 136, NI)],
        xs, near, far, coef, packed, g, a, b, mult,
        aliases={5: 1, 6: 2, 7: 3, 8: 4},
    )
    got_coef = got = spread(send, "gx", GX)
    yg, ya, yb, yw, yinv, xred, cl, send = call(
        y_first_kernel,
        [whole] * 5 + [sds(3 * GX, NJ, NI), sds(NJ, NI), sds(5 * NK, NI)],
        xs, got, g, a, b,
        scratch=[(GX + 1, NJ, NI), (GX + 1, NJ, NI), (ROWS, NI), (ROWS, NI), (ROWS, NI)],
    )
    got = spread_by_core(send)
    rows = sds(64, 4 * NI)
    w, *matrix = call(coarse_matrix_kernel, [rows] * 7, got_coef, flops=10**7)
    g, yred, send = call(
        x_again_kernel,
        [whole, sds(3 * GY, NK, NI), sds(NJ, NI)],
        xs, below, *got, yg, ya, yb, mult, w,
        scratch=[(GY + 1, NK, NI), (ROWS, NI), (ROWS, NI)],
    )
    got = spread(send, "gx", GX)
    yg, send = call(
        y_again_kernel,
        [whole, sds(2 * NK, NI)],
        xs, got, g, a, b, xred, cl, yw, yinv,
        scratch=[(GX + 1, NJ, NI), (ROWS, NI), (ROWS, NI)],
    )
    got = spread(send, "gy", GY)
    field, coarse = call(
        residual_kernel,
        [whole, sds(64, NI)],
        xs, below, got, yg, ya, yb, yred, cl,
        scratch=[(GY + 1, NK, NI), (ROWS, NI), (128, NI)],
    )
    got = spread(coarse, "gx", GX)
    res, c0, c1, near, far = call(
        coarse_one_kernel,
        [sds(64, 64), rows, rows, sds(24, 4 * NI), sds(24, 4 * NI)],
        got, w, *matrix,
        scratch=[(64, NI)],
    )
    near, far = swap(near, far)
    (c2,) = call(coarse_two_kernel, [rows], c0, c1, *matrix, flops=10**7)
    (cor,) = call(coarse_three_kernel, [sds(64, 4 * NI)], near, far, c0, c2, *matrix, scratch=[(4, 64, NI)])
    return field.reshape(NK, NJ, NI), res.reshape(8, 8, 64), cor.reshape(8, 8, 512)


def solution(mesh):
    spec = P(None, "gy", "gx")
    return jax.shard_map(
        body, mesh=mesh, in_specs=(spec,) * 6, out_specs=(spec, spec, P(None, "gy", None)), check_vma=False
    )
```

```python
import functools

import jax
import jax.numpy as jnp
from jax import lax
from jax.experimental import pallas as pl
from jax.experimental.pallas import tpu as pltpu
from jax.sharding import PartitionSpec as P

RELAX = 0.8
NK, NJ, NI = 16, 16, 128
ROWS = NK * NJ
GX, GY = 8, 16
STEPS = (1, 2, 4, 8, 16, 32, 64)
F32 = jnp.float32


def sds(*shape):
    return jax.ShapeDtypeStruct(shape, F32)


def call(kernel, outs, *args, scratch=(), hbm=0, aliases={}, sems=0, flops=None):
    spec = pl.BlockSpec(memory_space=pltpu.VMEM)
    outside = pl.BlockSpec(memory_space=pltpu.HBM)
    args = [pltpu.with_memory_space_constraint(v, pltpu.HBM) for v in args[:hbm]] + list(args[hbm:])
    shapes = [pltpu.VMEM(v, F32) for v in scratch]
    if sems:
        shapes.append(pltpu.SemaphoreType.DMA((sems,)))
    cost = None if flops is None else pl.CostEstimate(flops=flops, bytes_accessed=1 << 20, transcendentals=0)
    return pl.pallas_call(
        kernel,
        out_shape=outs,
        in_specs=[outside] * hbm + [spec] * (len(args) - hbm),
        out_specs=[spec] * len(outs),
        scratch_shapes=shapes,
        input_output_aliases=aliases,
        cost_estimate=cost,
        compiler_params=pltpu.CompilerParams(vmem_limit_bytes=16 * 1024 * 1024),
    )(*args)


def parts(xs):
    return [xs.at[pl.ds(n * ROWS, ROWS), :] for n in range(6)]


def lanes(rows, width=NI):
    return lax.broadcasted_iota(jnp.int32, (rows, width), 1)


def rolled(value, amount, axis):
    return pltpu.roll(value, amount % value.shape[axis], axis)


def level(ref, k):
    return ref[pl.ds(k * NJ, NJ), :]


def across(ref, j, count=NK, stride=NJ):
    return ref[pl.ds(j, count, stride=stride), :]


def column(value, k):
    return jnp.broadcast_to(value[:, k : k + 1], (value.shape[0], NI))


def z_pair(zc, k):
    return (level(zc, k - 1) if k > 0 else None, level(zc, k) if k < NK - 1 else None)


def z_sum(zc, k, base):
    low, top = z_pair(zc, k)
    if low is not None:
        base = base + low
    if top is not None:
        base = base + top
    return base


def z_terms(zc, field, k, base):
    low, top = z_pair(zc, k)
    if low is not None:
        base = base + low * level(field, k - 1)
    if top is not None:
        base = base + top * level(field, k + 1)
    return base


def y_left_of(yc, halo, k):
    row = lax.broadcasted_iota(jnp.int32, (NJ, NI), 0)
    return jnp.where(row == 0, halo[pl.ds(k, 1), :], rolled(level(yc, k), 1, 0))


def squeeze(values, scale=0.125, start=0):
    source = lax.broadcasted_iota(jnp.int32, (NI, NI), 0)
    target = lax.broadcasted_iota(jnp.int32, (NI, NI), 1)
    matrix = jnp.where(source // 2 + start == target, scale, 0.0).astype(F32)
    return jnp.dot(values, matrix, precision=lax.Precision.HIGHEST, preferred_element_type=F32)


def edges(values, scale=0.125):
    source = lax.broadcasted_iota(jnp.int32, (NI, NI), 0)
    target = lax.broadcasted_iota(jnp.int32, (NI, NI), 1)
    hit = ((source == NI - 1) & (target == 64)) | ((source == 0) & (target == NI - 1))
    matrix = jnp.where(hit, scale, 0.0).astype(F32)
    return jnp.dot(values, matrix, precision=lax.Precision.HIGHEST, preferred_element_type=F32)


def parity_shift(values):
    odd = lax.rem(lax.axis_index("gx"), 2) == 1
    return jnp.where(odd, rolled(values, 64, 1), values)


def store_coarse(out, base, tmp):
    for J in range(NJ // 2):
        out[pl.ds(base + J * 8, 8), :] = across(tmp, 2 * J, 8) + across(tmp, 2 * J + 1, 8)


def first_kernel(ph, yh, near, far, rows, tmp, sems):
    picks = ((ph, NJ - 1), (ph, 0), (yh, NJ - 1), (yh, NJ - 2))
    copies = [pltpu.make_async_copy(ref.at[:, j, :], rows.at[n], sems.at[n]) for n, (ref, j) in enumerate(picks)]
    for copy in copies:
        copy.start()
    for copy in copies:
        copy.wait()
    odd = lax.rem(lax.axis_index("gy"), 2) == 1

    def put(place, up, down):
        near[place, :] = jnp.where(odd, down, up)
        far[place, :] = jnp.where(odd, up, down)

    put(pl.ds(0, NK), rows[0], rows[1])
    put(pl.ds(NK, NK), rows[2], rows[2])
    tmp[...] = squeeze(rows[2] + rows[3])
    row = tmp[pl.ds(0, 8, stride=2), :] + tmp[pl.ds(1, 8, stride=2), :]
    put(pl.ds(2 * NK, 8), row, row)


def sorted_out(near, far, place):
    e = lax.axis_index("gy")
    odd = lax.rem(e, 2) == 1
    one, two = near[place, :], far[place, :]
    return (
        jnp.where(e == 0, 0.0, jnp.where(odd, one, two)),
        jnp.where(e == GY - 1, 0.0, jnp.where(odd, two, one)),
    )


def x_matrix(x, rest):
    d = lax.axis_index("gx")
    lane = lanes(x.shape[0])
    inner = jnp.logical_or(lane < NI - 1, d == GX - 1)
    diag = jnp.where(lane == 0, 0.0, rolled(x, 1, 1)) + jnp.where(inner, x, 0.0) + rest
    return diag, jnp.where(lane == NI - 1, 0.0, -x)


def x_eliminate(diag, off, rhs, keep):
    wide = lanes(diag.shape[0])
    ends = jnp.where(jnp.logical_or(wide == 0, wide == NI - 1), 1.0, 0.0).astype(F32)
    for n, s in enumerate(STEPS):
        inv = 1.0 / diag
        low = rolled(off, s, 1)
        alpha = -low * rolled(inv, s, 1)
        beta = -off * rolled(inv, -s, 1)
        keep(2 * n, alpha)
        keep(2 * n + 1, beta)
        diag = diag + alpha * low + beta * off
        rhs = rhs + alpha * rolled(rhs, s, 1) + beta * rolled(rhs, -s, 1)
        if s < NI // 2:
            off = beta * rolled(off, -s, 1)
            ends = ends + alpha * rolled(ends, s, 1) + beta * rolled(ends, -s, 1)
    inv = 1.0 / diag
    keep(2 * len(STEPS), inv)
    other = rolled(ends, NI // 2, 1)
    left = jnp.where(wide < NI // 2, ends, alpha * other)
    right = jnp.where(wide < NI // 2, beta * other, ends)
    return rhs * inv, left * inv, right * inv


def x_picks(g, a, b, x):
    return column(g, 0), column(g, NI - 1), column(a, 0), column(b, 0), column(b, NI - 1), column(x, NI - 1)


def x_first_kernel(fh, ph, xh, yh, zh, dh, order, xs, g, a, b, mult, packed_out, coarse, tmp, sems):
    copies = [
        pltpu.make_async_copy(ref, xs.at[pl.ds(n * ROWS, ROWS), :], sems.at[n])
        for n, ref in enumerate((fh, ph, xh, yh, zh, dh))
    ]
    for copy in copies:
        copy.start()
    for copy in copies:
        copy.wait()
    f, p, xc, yc, zc, dp = parts(xs)
    lane = lanes(NJ)
    row = lax.broadcasted_iota(jnp.int32, (NJ, NI), 0)
    packed = jnp.zeros((NJ, NI), F32)
    group = 8
    for k0 in range(0, NK, group):
        diag, off, rhs = [], [], []
        for k in range(k0, k0 + group):
            y, v = level(yc, k), level(p, k)
            y_left = jnp.where(row == 0, 0.0, rolled(y, 1, 0))
            matrix = x_matrix(level(xc, k), z_sum(zc, k, y_left + y + level(dp, k)))
            diag.append(matrix[0])
            off.append(matrix[1])
            after = jnp.where(row == NJ - 1, 0.0, rolled(v, -1, 0))
            rhs.append(z_terms(zc, p, k, level(f, k) + y_left * rolled(v, 1, 0) + y * after))
        diag, off, rhs = (jnp.concatenate(v, axis=0) for v in (diag, off, rhs))
        place = pl.ds(k0 * NJ, group * NJ)

        def keep(n, value):
            mult[pl.ds(n * ROWS + k0 * NJ, group * NJ), :] = value

        rhs, left, right = x_eliminate(diag, off, rhs, keep)
        g[place, :], a[place, :], b[place, :] = rhs, left, right
        for k in range(k0, k0 + group):
            part = slice((k - k0) * NJ, (k - k0 + 1) * NJ)
            for q, pick in enumerate(x_picks(rhs[part], left[part], right[part], level(xc, k))):
                packed = jnp.where(lane == q * NK + k, pick, packed)
    packed_out[...] = packed
    for q, two in enumerate(((xc, yc), (zc, dp))):
        total = jnp.zeros((128, NI), F32)
        for half, ref in enumerate(two):
            pairs = jnp.concatenate([level(ref, 2 * K) + level(ref, 2 * K + 1) for K in range(NK // 2)], axis=0)
            total = total + squeeze(pairs, start=64 * half)
        tmp[...] = total
        store_coarse(coarse, q * 64, tmp)


def x_rim_kernel(xs, near, far, coarse, packed, g_in, a_in, b_in, mult_in, below, g, a, b, mult, send):
    f, p, xc, yc, zc, dp = parts(xs)
    lane = lanes(NK)
    row = lax.broadcasted_iota(jnp.int32, (NK, NI), 0)

    def lifted(j):
        z, v = across(zc, j), across(p, j)
        top = jnp.where(row == NK - 1, 0.0, z)
        low = rolled(top, 1, 0)
        return low, top, low * rolled(v, 1, 0) + top * rolled(v, -1, 0)

    p_below, p_above = sorted_out(near, far, pl.ds(0, NK))
    y_left, _ = sorted_out(near, far, pl.ds(NK, NK))
    below[...] = y_left
    low, top, z_part = lifted(0)
    y = across(yc, 0)
    diag, off = x_matrix(across(xc, 0), low + top + y + y_left + across(dp, 0))
    rhs = across(f, 0) + y_left * p_below + y * across(p, 1) + z_part

    def keep(n, value):
        mult[pl.ds(n * ROWS, NK, stride=NJ), :] = value

    rhs, left, right = x_eliminate(diag, off, rhs, keep)
    first = pl.ds(0, NK, stride=NJ)
    g[first, :], a[first, :], b[first, :] = rhs, left, right
    line = jnp.zeros((NK, NI), F32)
    for q, pick in enumerate(x_picks(rhs, left, right, across(xc, 0))):
        line = line + jnp.where(lane == q * NK + row, pick, 0.0)
    line = jnp.sum(line, axis=0, keepdims=True)

    j = NJ - 1
    _, _, z_part = lifted(j)
    y = across(yc, j)
    rhs = across(f, j) + across(yc, j - 1) * across(p, j - 1) + y * p_above + z_part
    rhs = x_second_solve(rhs, lambda n: mult_in[pl.ds(n * ROWS + j, NK, stride=NJ), :])
    g[pl.ds(j, NK, stride=NJ), :] = rhs
    last = jnp.where(lane == row, column(rhs, 0), 0.0) + jnp.where(lane == NK + row, column(rhs, NI - 1), 0.0)
    last = jnp.sum(last, axis=0, keepdims=True)
    was = packed[...]
    was = jnp.where(row == 0, line, was)
    send[pl.ds(0, NJ), :] = jnp.where(jnp.logical_and(row == NJ - 1, lane < 2 * NK), last, was)
    send[pl.ds(NJ, 128), :] = coarse[...]
    send[pl.ds(NJ + 128, 8), :] = sorted_out(near, far, pl.ds(2 * NK, 8))[0]


def x_second_solve(rhs, kept):
    for n, s in enumerate(STEPS):
        rhs = rhs + kept(2 * n) * rolled(rhs, s, 1) + kept(2 * n + 1) * rolled(rhs, -s, 1)
    return rhs * kept(2 * len(STEPS))


def x_fluxes(fs, source, low, inv, up):
    zero = jnp.zeros((NJ, NI), F32)
    fs[0], fs[GX] = zero, zero
    forward = [source(0)]
    for d in range(1, GX - 1):
        forward.append(source(d) + low[d] * forward[-1])
    value = forward[-1] * inv[GX - 2]
    fs[GX - 1] = value
    for d in range(GX - 3, -1, -1):
        value = forward[d] * inv[d] + up[d] * value
        fs[1 + d] = value


def x_finish(fs, g, a, b, field):
    d = lax.axis_index("gx")
    flux_left, flux_right = fs[d], fs[d + 1]
    for k in range(NK):
        field[pl.ds(k * NJ, NJ), :] = (
            level(g, k) - level(a, k) * column(flux_left, k) + level(b, k) * column(flux_right, k)
        )
    return flux_left, flux_right


def y_source(f, xc, zc, field, fluxes, c_left, k):
    d = lax.axis_index("gx")
    lane = lanes(NJ)
    flux_left, flux_right = fluxes
    v, x = level(field, k), level(xc, k)
    before = jnp.where(lane == 0, column(c_left, k) * v - column(flux_left, k), rolled(x * v, 1, 1))
    last = jnp.where(d == GX - 1, 0.0, x * v + column(flux_right, k))
    after = jnp.where(lane == NI - 1, last, x * rolled(v, -1, 1))
    return z_terms(zc, field, k, level(f, k) + before + after)


def y_first_kernel(xs, got, g, a, b, yg, ya, yb, yw, yinv, xred, cl, send, fs, cs, field, src, base):
    f, p, xc, yc, zc, dp = parts(xs)
    d = lax.axis_index("gx")
    e = lax.axis_index("gy")
    lane = lanes(NJ)
    part = lambda n, q: rolled(got[n, pl.ds(0, NJ), :], -NK * q, 1)
    m = [part(n, 3) for n in range(GX)]
    low, inv, up = [None], [], []
    for n in range(GX - 1):
        dd = part(n, 4) + 1.0 / part(n, 5) + part(n + 1, 2)
        if n:
            low.append(m[n] * inv[-1])
            dd = dd - low[n] * m[n]
        inv.append(1.0 / dd)
        up.append(m[n + 1] * inv[n])
        xred[n], xred[GX + n], xred[2 * GX + n] = (low[n] if n else jnp.zeros_like(dd)), inv[n], up[n]
    x_fluxes(fs, lambda n: part(n + 1, 0) - part(n, 1), low, inv, up)
    cs[0] = jnp.zeros((NJ, NI), F32)
    for n in range(GX):
        cs[n + 1] = part(n, 5)
    c_left = cs[d]
    cl[...] = c_left
    fluxes = x_finish(fs, g, a, b, field)
    for k in range(NK):
        src[pl.ds(k * NJ, NJ), :] = y_source(f, xc, zc, field, fluxes, c_left, k)
        x = level(xc, k)
        x_left = jnp.where(lane == 0, column(c_left, k), rolled(x, 1, 1))
        base[pl.ds(k * NJ, NJ), :] = z_sum(zc, k, x_left + x + level(dp, k))
    ys, ws, invs, spike = [], [None], [], []
    for j in range(NJ):
        y = across(yc, j)
        diag = across(base, j)
        if j < NJ - 1:
            diag = diag + y
        else:
            diag = diag + jnp.where(e == GY - 1, y, 0.0)
        rhs = across(src, j)
        if j:
            y_before = across(yc, j - 1)
            w = y_before * invs[-1]
            ws.append(w)
            diag = diag + y_before - w * y_before
            rhs = rhs + w * ys[-1]
            spike.append(w * spike[-1])
            yw[pl.ds(j * NK, NK), :] = w
        else:
            spike.append(jnp.ones((NK, NI), F32))
            yw[pl.ds(0, NK), :] = jnp.zeros((NK, NI), F32)
        ys.append(rhs)
        invs.append(1.0 / diag)
        yinv[pl.ds(j * NK, NK), :] = invs[-1]
    for j in range(NJ - 1, -1, -1):
        if j == NJ - 1:
            gv, av, bv = ys[j] * invs[j], spike[j] * invs[j], invs[j]
            send[pl.ds(NK, NK), :] = gv
            send[pl.ds(4 * NK, NK), :] = bv + 1.0 / across(yc, j)
        else:
            w = ws[j + 1]
            gv, av, bv = ys[j] * invs[j] + w * gv, spike[j] * invs[j] + w * av, w * bv
        place = pl.ds(j * NK, NK)
        yg[place, :], ya[place, :], yb[place, :] = gv, av, bv
    send[pl.ds(0, NK), :] = gv
    send[pl.ds(2 * NK, NK), :] = av
    send[pl.ds(3 * NK, NK), :] = bv


def y_fluxes(fs, source, low, inv, up):
    zero = jnp.zeros((NK, NI), F32)
    fs[0], fs[GY] = zero, zero
    forward = [source(0)]
    for n in range(1, GY - 1):
        forward.append(source(n) + low(n) * forward[-1])
    value = forward[-1] * inv(GY - 2)
    fs[GY - 1] = value
    for n in range(GY - 3, -1, -1):
        value = forward[n] * inv(n) + up(n) * value
        fs[1 + n] = value


def y_finish(fs, yc, below, yg, ya, yb, field, terms):
    e = lax.axis_index("gy")
    flux_left, flux_right = fs[e], fs[e + 1]
    block = lambda ref, j: ref[pl.ds(j * NK, NK), :]
    p = [block(yg, j) - block(ya, j) * flux_left + block(yb, j) * flux_right for j in range(NJ)]
    for j in range(NJ):
        y = across(yc, j)
        if j:
            before = across(yc, j - 1) * p[j - 1]
        else:
            before = below[pl.ds(0, NK), :] * p[0] - flux_left
        if j < NJ - 1:
            after = y * p[j + 1]
        else:
            after = jnp.where(e == GY - 1, 0.0, y * p[j] + flux_right)
        field[pl.ds(j, NK, stride=NJ), :] = p[j]
        terms[pl.ds(j, NK, stride=NJ), :] = before + after


def x_again_kernel(xs, below, mine, other, yg, ya, yb, mult, w, g, yred, send, fs, field, terms):
    f, p, xc, yc, zc, dp = parts(xs)
    odd = lax.rem(lax.axis_index("gy"), 2) == 1

    def part(n, q):
        one, two = mine[n // 2, pl.ds(q * NK, NK), :], other[n // 2, pl.ds(q * NK, NK), :]
        return jnp.where(odd, one, two) if n % 2 else jnp.where(odd, two, one)

    prev = None
    for n in range(GY - 1):
        dd = part(n, 4) + part(n + 1, 2)
        if n:
            m = part(n, 3)
            low = m * prev
            dd = dd - low * m
            yred[n] = low
        else:
            yred[n] = jnp.zeros_like(dd)
        prev = 1.0 / dd
        yred[GY + n] = prev
        yred[2 * GY + n] = part(n + 1, 3) * prev
    yred[GY - 1] = jnp.zeros((NK, NI), F32)
    yred[2 * GY - 1] = jnp.zeros((NK, NI), F32)
    yred[3 * GY - 1] = jnp.zeros((NK, NI), F32)
    y_fluxes(
        fs,
        lambda n: part(n + 1, 0) - part(n, 1),
        lambda n: yred[n],
        lambda n: yred[GY + n],
        lambda n: yred[2 * GY + n],
    )
    y_finish(fs, yc, below, yg, ya, yb, field, terms)
    lane = lanes(NJ)
    packed = jnp.zeros((NJ, NI), F32)
    group = 2
    for k0 in range(0, NK, group):
        rhs = jnp.concatenate(
            [z_terms(zc, field, k, level(f, k) + level(terms, k)) for k in range(k0, k0 + group)], axis=0
        )
        place = pl.ds(k0 * NJ, group * NJ)
        rhs = x_second_solve(rhs, lambda n: mult[pl.ds(n * ROWS + k0 * NJ, group * NJ), :])
        g[place, :] = rhs
        for k in range(k0, k0 + group):
            mine = rhs[(k - k0) * NJ : (k - k0 + 1) * NJ]
            packed = jnp.where(lane == k, column(mine, 0), packed)
            packed = jnp.where(lane == NK + k, column(mine, NI - 1), packed)
    send[...] = packed


def y_again_kernel(xs, got, g, a, b, xred, cl, yw, yinv, yg, send, fs, field, src):
    f, p, xc, yc, zc, dp = parts(xs)
    part = lambda n, q: rolled(got[n], -NK * q, 1)
    x_fluxes(
        fs,
        lambda n: part(n + 1, 0) - part(n, 1),
        [xred[n] for n in range(GX - 1)],
        [xred[GX + n] for n in range(GX - 1)],
        [xred[2 * GX + n] for n in range(GX - 1)],
    )
    fluxes = x_finish(fs, g, a, b, field)
    c_left = cl[...]
    for k in range(NK):
        src[pl.ds(k * NJ, NJ), :] = y_source(f, xc, zc, field, fluxes, c_left, k)
    block = lambda ref, j: ref[pl.ds(j * NK, NK), :]
    ys = []
    for j in range(NJ):
        rhs = across(src, j)
        if j:
            rhs = rhs + block(yw, j) * ys[-1]
        ys.append(rhs)
    value = None
    for j in range(NJ - 1, -1, -1):
        new = ys[j] * block(yinv, j)
        value = new if value is None else new + block(yw, j + 1) * value
        yg[pl.ds(j * NK, NK), :] = value
        if j == NJ - 1:
            send[pl.ds(NK, NK), :] = value
    send[pl.ds(0, NK), :] = value


def residual_kernel(xs, below, got, yg, ya, yb, yred, cl, fluxes, coarse, fs, terms, tmp, field):
    f, p, xc, yc, zc, dp = parts(xs)
    d = lax.axis_index("gx")
    lane = lanes(NJ)
    part = lambda n, q: got[n, pl.ds(q * NK, NK), :]
    y_fluxes(
        fs,
        lambda n: part(n + 1, 0) - part(n, 1),
        lambda n: yred[n],
        lambda n: yred[GY + n],
        lambda n: yred[2 * GY + n],
    )
    e = lax.axis_index("gy")
    fluxes[0], fluxes[1] = fs[e], fs[e + 1]
    y_finish(fs, yc, below, yg, ya, yb, field, terms)
    c_left = cl[...]
    main, rim = [], []
    for k in range(NK):
        v, x = level(field, k), level(xc, k)
        left = column(c_left, k)
        x_left = jnp.where(lane == 0, left, rolled(x, 1, 1))
        diag = z_sum(zc, k, x_left + x + y_left_of(yc, below, k) + level(yc, k) + level(dp, k))
        around = jnp.where(lane == 0, 0.0, x_left * rolled(v, 1, 1)) + jnp.where(lane == NI - 1, 0.0, x * rolled(v, -1, 1))
        main.append(level(f, k) - (diag * v - around - level(terms, k) - z_terms(zc, field, k, jnp.zeros((NJ, NI), F32))))
        last = jnp.where(d == GX - 1, 0.0, x * v)
        rim.append(jnp.where(lane == 0, left * v, jnp.where(lane == NI - 1, last, 0.0)))
    pairs = jnp.concatenate([main[2 * K] + main[2 * K + 1] for K in range(NK // 2)], axis=0)
    outer = jnp.concatenate([rim[2 * K] + rim[2 * K + 1] for K in range(NK // 2)], axis=0)
    tmp[...] = parity_shift(squeeze(pairs) + edges(outer))
    store_coarse(coarse, 0, tmp)


def coarse_matrix_kernel(coef, w, xl, xu, yl, yu, zl, zu):
    lane = lanes(8)
    wide = lanes(8, 4 * NI)
    level_k = lax.broadcasted_iota(jnp.int32, (8, 4 * NI), 0)

    def whole(at, half):
        rows = pl.ds(at, 8)
        outs = []
        for m in range(4):
            even, odd = coef[2 * m, rows, :], coef[2 * m + 1, rows, :]
            if half:
                even = rolled(even, 64, 1)
            else:
                odd = rolled(odd, 64, 1)
            outs.append(jnp.where(lane < 64, even, odd))
        return jnp.concatenate(outs, axis=1)

    y_before = whole(NJ + 128, 0)
    for J in range(8):
        rows = pl.ds(J * 8, 8)
        x, y, z, damp = (whole(NJ + (q // 2) * 64 + J * 8, q % 2) for q in range(4))
        x_left = jnp.where(wide == 0, 0.0, rolled(x, 1, 1))
        z_top = jnp.where(level_k == 7, 0.0, z)
        z_low = rolled(z_top, 1, 0)
        weight = RELAX / (x_left + x + y_before + y + z_low + z_top + damp)
        w[rows, :] = weight
        xl[rows, :] = weight * x_left
        xu[rows, :] = jnp.where(wide == 4 * NI - 1, 0.0, weight * x)
        yl[rows, :] = weight * y_before
        yu[rows, :] = weight * y
        zl[rows, :] = weight * z_low
        zu[rows, :] = weight * z_top
        y_before = y


def eight(ref, J):
    return ref[pl.ds(J * 8, 8), :]


def flat_terms(v, J, xl, xu, zl, zu):
    return (
        eight(xl, J) * rolled(v, 1, 1)
        + eight(xu, J) * rolled(v, -1, 1)
        + eight(zl, J) * rolled(v, 1, 0)
        + eight(zu, J) * rolled(v, -1, 0)
    )


def coarse_one_kernel(got, w, xl, xu, yl, yu, zl, zu, tmp, c0, c1, near, far):
    d = lax.axis_index("gx")
    lane = lanes(8)
    for J in range(8):
        rows = pl.ds(J * 8, 8)
        outs = []
        for m in range(4):
            value = jnp.where(lane <= 64, got[2 * m, rows, :], 0.0) + jnp.where(lane >= 63, got[2 * m + 1, rows, :], 0.0)
            if m > 0:
                value = value + jnp.where(lane == 0, got[2 * m - 1, rows, :], 0.0)
            if m < 3:
                value = value + jnp.where(lane == NI - 1, got[2 * m + 2, rows, :], 0.0)
            outs.append(value)
        mine = outs[0]
        for m in range(1, 4):
            mine = jnp.where(d // 2 == m, outs[m], mine)
        mine = jnp.where(lax.rem(d, 2) == 1, rolled(mine, 64, 1), mine)
        tmp[pl.ds(J, 8, stride=8), :] = mine
        c0[rows, :] = eight(w, J) * jnp.concatenate(outs, axis=1)
    for J in range(8):
        v = eight(c0, J)
        new = (2.0 - RELAX) * v + flat_terms(v, J, xl, xu, zl, zu)
        if J:
            new = new + eight(yl, J) * eight(c0, J - 1)
        if J < 7:
            new = new + eight(yu, J) * eight(c0, J + 1)
        c1[pl.ds(J * 8, 8), :] = new
    odd = lax.rem(lax.axis_index("gy"), 2) == 1
    for n, (up, down) in enumerate(((eight(c0, 7), eight(c0, 0)), (eight(c1, 7), eight(c1, 0)), (eight(yu, 7), eight(yl, 0)))):
        near[pl.ds(n * 8, 8), :] = jnp.where(odd, down, up)
        far[pl.ds(n * 8, 8), :] = jnp.where(odd, up, down)


def coarse_two_kernel(c0, c1, xl, xu, yl, yu, zl, zu, res, fluxes, yg, ya, yb, c2, res_out, field):
    res_out[...] = res[:, :64]
    for j in range(NJ):
        place = pl.ds(j * NK, NK)
        field[pl.ds(j, NK, stride=NJ), :] = yg[place, :] - ya[place, :] * fluxes[0] + yb[place, :] * fluxes[1]
    for J in range(8):
        v = eight(c1, J)
        new = eight(c0, J) + (1.0 - RELAX) * v + flat_terms(v, J, xl, xu, zl, zu)
        if J:
            new = new + eight(yl, J) * eight(c1, J - 1)
        if J < 7:
            new = new + eight(yu, J) * eight(c1, J + 1)
        c2[pl.ds(J * 8, 8), :] = new


def coarse_three_kernel(near, far, c0, c2, xl, xu, yl, yu, zl, zu, out, tmp):
    sides = [sorted_out(near, far, pl.ds(n * 8, 8)) for n in range(3)]
    extra = {}
    for side, (J, inward, coupling) in enumerate(((0, 1, yl), (7, 6, yu))):
        their0, their1, weight = (pair[side] for pair in sides)
        change = eight(coupling, J) * their0
        beside = their1 + weight * eight(c0, J)
        extra[J] = (1.0 - RELAX) * change + flat_terms(change, J, xl, xu, zl, zu) + eight(coupling, J) * beside
        extra[inward] = eight(coupling, inward) * change
    for J in range(8):
        new = eight(c2, J)
        if J in extra:
            new = new + extra[J]
        for m in range(4):
            tmp[m, pl.ds(J, 8, stride=8), :] = new[:, m * NI : (m + 1) * NI]
    for m in range(4):
        out[:, pl.ds(m * NI, NI)] = tmp[m]


def spread(value, axis, count):
    many = jnp.broadcast_to(value[None], (count,) + value.shape)
    return lax.all_to_all(many, axis, split_axis=0, concat_axis=0, tiled=True)


def spread_by_core(value):
    groups = [list(range(0, GY, 2)), list(range(1, GY, 2))]
    many = jnp.broadcast_to(value[None], (GY // 2,) + value.shape)
    mine = lax.all_to_all(many, "gy", split_axis=0, concat_axis=0, tiled=True, axis_index_groups=groups)
    return mine, lax.ppermute(mine, "gy", [(n, n ^ 1) for n in range(GY)])


def swap(near, far):
    pairs = [(n, n ^ 1) for n in range(GY)]
    others = [(n, (n + 1) % GY if n % 2 else (n - 1) % GY) for n in range(GY)]
    return lax.ppermute(near, "gy", pairs), lax.ppermute(far, "gy", others)


def body(forcing, pressure_in, x_coupling, y_coupling, z_coupling, damping):
    args = (forcing, pressure_in, x_coupling, y_coupling, z_coupling, damping)
    whole = sds(ROWS, NI)
    kept = sds((2 * len(STEPS) + 1) * ROWS, NI)
    mine = call(
        first_kernel,
        [sds(40, NI), sds(40, NI)],
        pressure_in, y_coupling,
        scratch=[(4, NK, NI), (NK, NI)],
        hbm=2,
        sems=4,
    )
    near, far = swap(*mine)
    xs, g, a, b, mult, packed, coef = call(
        x_first_kernel,
        [sds(6 * ROWS, NI), whole, whole, whole, kept, sds(NJ, NI), sds(128, NI)],
        *[v.reshape(ROWS, NI) for v in args], mine[0],
        scratch=[(128, NI)],
        hbm=6,
        sems=6,
        flops=10**8,
    )
    below, g, a, b, mult, send = call(
        x_rim_kernel,
        [sds(NK, NI), whole, whole, whole, kept, sds(NJ + 136, NI)],
        xs, near, far, coef, packed, g, a, b, mult,
        aliases={5: 1, 6: 2, 7: 3, 8: 4},
    )
    got_coef = got = spread(send, "gx", GX)
    yg, ya, yb, yw, yinv, xred, cl, send = call(
        y_first_kernel,
        [whole] * 5 + [sds(3 * GX, NJ, NI), sds(NJ, NI), sds(5 * NK, NI)],
        xs, got, g, a, b,
        scratch=[(GX + 1, NJ, NI), (GX + 1, NJ, NI), (ROWS, NI), (ROWS, NI), (ROWS, NI)],
    )
    got = spread_by_core(send)
    rows = sds(64, 4 * NI)
    w, *matrix = call(coarse_matrix_kernel, [rows] * 7, got_coef, flops=10**7)
    g, yred, send = call(
        x_again_kernel,
        [whole, sds(3 * GY, NK, NI), sds(NJ, NI)],
        xs, below, *got, yg, ya, yb, mult, w,
        scratch=[(GY + 1, NK, NI), (ROWS, NI), (ROWS, NI)],
    )
    got = spread(send, "gx", GX)
    yg, send = call(
        y_again_kernel,
        [whole, sds(2 * NK, NI)],
        xs, got, g, a, b, xred, cl, yw, yinv,
        scratch=[(GX + 1, NJ, NI), (ROWS, NI), (ROWS, NI)],
    )
    got = spread(send, "gy", GY)
    fluxes, coarse = call(
        residual_kernel,
        [sds(2, NK, NI), sds(64, NI)],
        xs, below, got, yg, ya, yb, yred, cl,
        scratch=[(GY + 1, NK, NI), (ROWS, NI), (128, NI), (ROWS, NI)],
    )
    got = spread(coarse, "gx", GX)
    res, c0, c1, near, far = call(
        coarse_one_kernel,
        [sds(64, NI), rows, rows, sds(24, 4 * NI), sds(24, 4 * NI)],
        got, w, *matrix,
    )
    near, far = swap(near, far)
    c2, res, field = call(
        coarse_two_kernel,
        [rows, sds(64, 64), whole],
        c0, c1, *matrix, res, fluxes, yg, ya, yb,
        flops=10**7,
    )
    (cor,) = call(coarse_three_kernel, [sds(64, 4 * NI)], near, far, c0, c2, *matrix, scratch=[(4, 64, NI)])
    return field.reshape(NK, NJ, NI), res.reshape(8, 8, 64), cor.reshape(8, 8, 512)


def solution(mesh):
    spec = P(None, "gy", "gx")
    return jax.shard_map(
        body, mesh=mesh, in_specs=(spec,) * 6, out_specs=(spec, spec, P(None, "gy", None)), check_vma=False
    )
```

```python
import functools

import jax
import jax.numpy as jnp
from jax import lax
from jax.experimental import pallas as pl
from jax.experimental.pallas import tpu as pltpu
from jax.sharding import PartitionSpec as P

RELAX = 0.8
NK, NJ, NI = 16, 16, 128
ROWS = NK * NJ
GX, GY = 8, 16
STEPS = (1, 2, 4, 8, 16, 32, 64)
F32 = jnp.float32


def sds(*shape):
    return jax.ShapeDtypeStruct(shape, F32)


def call(kernel, outs, *args, scratch=(), hbm=0, aliases={}, sems=0, flops=None):
    spec = pl.BlockSpec(memory_space=pltpu.VMEM)
    outside = pl.BlockSpec(memory_space=pltpu.HBM)
    args = [pltpu.with_memory_space_constraint(v, pltpu.HBM) for v in args[:hbm]] + list(args[hbm:])
    shapes = [pltpu.VMEM(v, F32) for v in scratch]
    if sems:
        shapes.append(pltpu.SemaphoreType.DMA((sems,)))
    cost = None if flops is None else pl.CostEstimate(flops=flops, bytes_accessed=1 << 20, transcendentals=0)
    return pl.pallas_call(
        kernel,
        out_shape=outs,
        in_specs=[outside] * hbm + [spec] * (len(args) - hbm),
        out_specs=[spec] * len(outs),
        scratch_shapes=shapes,
        input_output_aliases=aliases,
        cost_estimate=cost,
        compiler_params=pltpu.CompilerParams(vmem_limit_bytes=16 * 1024 * 1024),
    )(*args)


def parts(xs):
    return [xs.at[pl.ds(n * ROWS, ROWS), :] for n in range(6)]


def lanes(rows, width=NI):
    return lax.broadcasted_iota(jnp.int32, (rows, width), 1)


def rolled(value, amount, axis):
    return pltpu.roll(value, amount % value.shape[axis], axis)


def level(ref, k):
    return ref[pl.ds(k * NJ, NJ), :]


def across(ref, j, count=NK, stride=NJ):
    return ref[pl.ds(j, count, stride=stride), :]


def column(value, k):
    return jnp.broadcast_to(value[:, k : k + 1], (value.shape[0], NI))


def z_pair(zc, k):
    return (level(zc, k - 1) if k > 0 else None, level(zc, k) if k < NK - 1 else None)


def z_sum(zc, k, base):
    low, top = z_pair(zc, k)
    if low is not None:
        base = base + low
    if top is not None:
        base = base + top
    return base


def z_terms(zc, field, k, base):
    low, top = z_pair(zc, k)
    if low is not None:
        base = base + low * level(field, k - 1)
    if top is not None:
        base = base + top * level(field, k + 1)
    return base


def y_left_of(yc, halo, k):
    row = lax.broadcasted_iota(jnp.int32, (NJ, NI), 0)
    return jnp.where(row == 0, halo[pl.ds(k, 1), :], rolled(level(yc, k), 1, 0))


def squeeze(values, scale=0.125, start=0):
    source = lax.broadcasted_iota(jnp.int32, (NI, NI), 0)
    target = lax.broadcasted_iota(jnp.int32, (NI, NI), 1)
    matrix = jnp.where(source // 2 + start == target, scale, 0.0).astype(F32)
    return jnp.dot(values, matrix, precision=lax.Precision.HIGHEST, preferred_element_type=F32)


def edges(values, scale=0.125):
    source = lax.broadcasted_iota(jnp.int32, (NI, NI), 0)
    target = lax.broadcasted_iota(jnp.int32, (NI, NI), 1)
    hit = ((source == NI - 1) & (target == 64)) | ((source == 0) & (target == NI - 1))
    matrix = jnp.where(hit, scale, 0.0).astype(F32)
    return jnp.dot(values, matrix, precision=lax.Precision.HIGHEST, preferred_element_type=F32)


def store_coarse(out, base, tmp):
    for J in range(NJ // 2):
        out[pl.ds(base + J * 8, 8), :] = across(tmp, 2 * J, 8) + across(tmp, 2 * J + 1, 8)


def first_kernel(fh, ph, xh, yh, zh, dh, xs, near, far, coarse, tmp, sems):
    copies = [
        pltpu.make_async_copy(ref, xs.at[pl.ds(n * ROWS, ROWS), :], sems.at[n])
        for n, ref in enumerate((fh, ph, xh, yh, zh, dh))
    ]
    for copy in copies:
        copy.start()
    for copy in copies[1:]:
        copy.wait()
    f, p, xc, yc, zc, dp = parts(xs)
    odd = lax.rem(lax.axis_index("gy"), 2) == 1
    for q, two in enumerate(((xc, yc), (zc, dp))):
        total = jnp.zeros((128, NI), F32)
        for half, ref in enumerate(two):
            pairs = jnp.concatenate([level(ref, 2 * K) + level(ref, 2 * K + 1) for K in range(NK // 2)], axis=0)
            total = total + squeeze(pairs, start=64 * half)
        tmp[...] = total
        store_coarse(coarse, q * 64, tmp)

    def put(place, up, down):
        near[place, :] = jnp.where(odd, down, up)
        far[place, :] = jnp.where(odd, up, down)

    put(pl.ds(0, NK), across(p, NJ - 1), across(p, 0))
    put(pl.ds(NK, NK), across(yc, NJ - 1), across(yc, 0))
    for q in range(2):
        put(pl.ds(2 * NK + q * 24, 24), coarse[pl.ds(q * 64 + 40, 24), :], coarse[pl.ds(q * 64, 24), :])
    copies[0].wait()


def sorted_out(near, far, place):
    e = lax.axis_index("gy")
    odd = lax.rem(e, 2) == 1
    one, two = near[place, :], far[place, :]
    return (
        jnp.where(e == 0, 0.0, jnp.where(odd, one, two)),
        jnp.where(e == GY - 1, 0.0, jnp.where(odd, two, one)),
    )


def x_matrix(x, rest):
    d = lax.axis_index("gx")
    lane = lanes(x.shape[0])
    inner = jnp.logical_or(lane < NI - 1, d == GX - 1)
    diag = jnp.where(lane == 0, 0.0, rolled(x, 1, 1)) + jnp.where(inner, x, 0.0) + rest
    return diag, jnp.where(lane == NI - 1, 0.0, -x)


def x_eliminate(diag, off, rhs, keep):
    wide = lanes(diag.shape[0])
    ends = jnp.where(jnp.logical_or(wide == 0, wide == NI - 1), 1.0, 0.0).astype(F32)
    for n, s in enumerate(STEPS):
        inv = 1.0 / diag
        low = rolled(off, s, 1)
        alpha = -low * rolled(inv, s, 1)
        beta = -off * rolled(inv, -s, 1)
        keep(2 * n, alpha)
        keep(2 * n + 1, beta)
        diag = diag + alpha * low + beta * off
        rhs = rhs + alpha * rolled(rhs, s, 1) + beta * rolled(rhs, -s, 1)
        if s < NI // 2:
            off = beta * rolled(off, -s, 1)
            ends = ends + alpha * rolled(ends, s, 1) + beta * rolled(ends, -s, 1)
    inv = 1.0 / diag
    keep(2 * len(STEPS), inv)
    other = rolled(ends, NI // 2, 1)
    left = jnp.where(wide < NI // 2, ends, alpha * other)
    right = jnp.where(wide < NI // 2, beta * other, ends)
    return rhs * inv, left * inv, right * inv


def x_picks(g, a, b, x):
    return column(g, 0), column(g, NI - 1), column(a, 0), column(b, 0), column(b, NI - 1), column(x, NI - 1)


def x_first_kernel(xs, g, a, b, mult, packed_out):
    f, p, xc, yc, zc, dp = parts(xs)
    lane = lanes(NJ)
    row = lax.broadcasted_iota(jnp.int32, (NJ, NI), 0)
    packed = jnp.zeros((NJ, NI), F32)
    group = 8
    for k0 in range(0, NK, group):
        diag, off, rhs = [], [], []
        for k in range(k0, k0 + group):
            y, v = level(yc, k), level(p, k)
            y_left = jnp.where(row == 0, 0.0, rolled(y, 1, 0))
            matrix = x_matrix(level(xc, k), z_sum(zc, k, y_left + y + level(dp, k)))
            diag.append(matrix[0])
            off.append(matrix[1])
            after = jnp.where(row == NJ - 1, 0.0, rolled(v, -1, 0))
            rhs.append(z_terms(zc, p, k, level(f, k) + y_left * rolled(v, 1, 0) + y * after))
        diag, off, rhs = (jnp.concatenate(v, axis=0) for v in (diag, off, rhs))
        place = pl.ds(k0 * NJ, group * NJ)

        def keep(n, value):
            mult[pl.ds(n * ROWS + k0 * NJ, group * NJ), :] = value

        rhs, left, right = x_eliminate(diag, off, rhs, keep)
        g[place, :], a[place, :], b[place, :] = rhs, left, right
        for k in range(k0, k0 + group):
            part = slice((k - k0) * NJ, (k - k0 + 1) * NJ)
            for q, pick in enumerate(x_picks(rhs[part], left[part], right[part], level(xc, k))):
                packed = jnp.where(lane == q * NK + k, pick, packed)
    packed_out[...] = packed


def x_rim_kernel(xs, near, far, coarse, packed, g_in, a_in, b_in, mult_in, below, g, a, b, mult, send, ext):
    f, p, xc, yc, zc, dp = parts(xs)
    lane = lanes(NK)
    row = lax.broadcasted_iota(jnp.int32, (NK, NI), 0)

    def lifted(j):
        z, v = across(zc, j), across(p, j)
        top = jnp.where(row == NK - 1, 0.0, z)
        low = rolled(top, 1, 0)
        return low, top, low * rolled(v, 1, 0) + top * rolled(v, -1, 0)

    p_below, p_above = sorted_out(near, far, pl.ds(0, NK))
    y_left, _ = sorted_out(near, far, pl.ds(NK, NK))
    below[...] = y_left
    low, top, z_part = lifted(0)
    y = across(yc, 0)
    diag, off = x_matrix(across(xc, 0), low + top + y + y_left + across(dp, 0))
    rhs = across(f, 0) + y_left * p_below + y * across(p, 1) + z_part

    def keep(n, value):
        mult[pl.ds(n * ROWS, NK, stride=NJ), :] = value

    rhs, left, right = x_eliminate(diag, off, rhs, keep)
    first = pl.ds(0, NK, stride=NJ)
    g[first, :], a[first, :], b[first, :] = rhs, left, right
    line = jnp.zeros((NK, NI), F32)
    for q, pick in enumerate(x_picks(rhs, left, right, across(xc, 0))):
        line = line + jnp.where(lane == q * NK + row, pick, 0.0)
    line = jnp.sum(line, axis=0, keepdims=True)

    j = NJ - 1
    _, _, z_part = lifted(j)
    y = across(yc, j)
    rhs = across(f, j) + across(yc, j - 1) * across(p, j - 1) + y * p_above + z_part
    rhs = x_second_solve(rhs, lambda n: mult_in[pl.ds(n * ROWS + j, NK, stride=NJ), :])
    g[pl.ds(j, NK, stride=NJ), :] = rhs
    last = jnp.where(lane == row, column(rhs, 0), 0.0) + jnp.where(lane == NK + row, column(rhs, NI - 1), 0.0)
    last = jnp.sum(last, axis=0, keepdims=True)
    was = packed[...]
    was = jnp.where(row == 0, line, was)
    send[pl.ds(0, NJ), :] = jnp.where(jnp.logical_and(row == NJ - 1, lane < 2 * NK), last, was)
    coarse_share(near, far, coarse, send, ext)


def coarse_share(near, far, coarse, send, ext):
    wide = lanes(8)
    level_k = lax.broadcasted_iota(jnp.int32, (8, NI), 0)
    fields = [[], [], [], []]
    for q in range(2):
        lower, upper = sorted_out(near, far, pl.ds(2 * NK + q * 24, 24))
        rows = [lower[n * 8 : n * 8 + 8] for n in range(3)]
        rows += [coarse[pl.ds(q * 64 + n * 8, 8), :] for n in range(8)]
        rows += [upper[n * 8 : n * 8 + 8] for n in range(2)]
        for row in rows:
            fields[2 * q].append(jnp.where(wide < 64, row, 0.0))
            fields[2 * q + 1].append(jnp.where(wide < 64, rolled(row, 64, 1), 0.0))
    xs_, ys_, zs_, damps = fields
    shares = [jnp.zeros((8, NI), F32)] * 4
    for J in range(12):
        top = jnp.where(level_k == 7, 0.0, zs_[J + 1])
        rest = damps[J + 1] + ys_[J + 1] + ys_[J] + top + rolled(top, 1, 0) + xs_[J + 1] + rolled(xs_[J + 1], 1, 1)
        for n, value in enumerate((xs_[J + 1], ys_[J + 1], top, rest)):
            ext[pl.ds(n * 96 + J * 8, 8), :] = value
            at = 10 * J
            first, last = rolled(value, at, 1), rolled(value, at + 5 - 59, 1)
            share = jnp.where(jnp.logical_and(wide >= at, wide < at + 5), first, shares[n])
            shares[n] = jnp.where(jnp.logical_and(wide >= at + 5, wide < at + 10), last, share)
    for n in range(4):
        send[pl.ds(NJ + n * 8, 8), :] = shares[n]


def x_second_solve(rhs, kept):
    for n, s in enumerate(STEPS):
        rhs = rhs + kept(2 * n) * rolled(rhs, s, 1) + kept(2 * n + 1) * rolled(rhs, -s, 1)
    return rhs * kept(2 * len(STEPS))


def x_fluxes(fs, source, low, inv, up):
    zero = jnp.zeros((NJ, NI), F32)
    fs[0], fs[GX] = zero, zero
    forward = [source(0)]
    for d in range(1, GX - 1):
        forward.append(source(d) + low[d] * forward[-1])
    value = forward[-1] * inv[GX - 2]
    fs[GX - 1] = value
    for d in range(GX - 3, -1, -1):
        value = forward[d] * inv[d] + up[d] * value
        fs[1 + d] = value


def x_finish(fs, g, a, b, field):
    d = lax.axis_index("gx")
    flux_left, flux_right = fs[d], fs[d + 1]
    for k in range(NK):
        field[pl.ds(k * NJ, NJ), :] = (
            level(g, k) - level(a, k) * column(flux_left, k) + level(b, k) * column(flux_right, k)
        )
    return flux_left, flux_right


def y_source(f, xc, zc, field, fluxes, c_left, k):
    d = lax.axis_index("gx")
    lane = lanes(NJ)
    flux_left, flux_right = fluxes
    v, x = level(field, k), level(xc, k)
    before = jnp.where(lane == 0, column(c_left, k) * v - column(flux_left, k), rolled(x * v, 1, 1))
    last = jnp.where(d == GX - 1, 0.0, x * v + column(flux_right, k))
    after = jnp.where(lane == NI - 1, last, x * rolled(v, -1, 1))
    return z_terms(zc, field, k, level(f, k) + before + after)


def y_first_kernel(xs, got, g, a, b, yg, ya, yb, yw, yinv, xred, cl, send, fs, cs, field, src, base):
    f, p, xc, yc, zc, dp = parts(xs)
    d = lax.axis_index("gx")
    e = lax.axis_index("gy")
    lane = lanes(NJ)
    part = lambda n, q: rolled(got[n, pl.ds(0, NJ), :], -NK * q, 1)
    m = [part(n, 3) for n in range(GX)]
    low, inv, up = [None], [], []
    for n in range(GX - 1):
        dd = part(n, 4) + 1.0 / part(n, 5) + part(n + 1, 2)
        if n:
            low.append(m[n] * inv[-1])
            dd = dd - low[n] * m[n]
        inv.append(1.0 / dd)
        up.append(m[n + 1] * inv[n])
        xred[n], xred[GX + n], xred[2 * GX + n] = (low[n] if n else jnp.zeros_like(dd)), inv[n], up[n]
    x_fluxes(fs, lambda n: part(n + 1, 0) - part(n, 1), low, inv, up)
    cs[0] = jnp.zeros((NJ, NI), F32)
    for n in range(GX):
        cs[n + 1] = part(n, 5)
    c_left = cs[d]
    cl[...] = c_left
    fluxes = x_finish(fs, g, a, b, field)
    for k in range(NK):
        src[pl.ds(k * NJ, NJ), :] = y_source(f, xc, zc, field, fluxes, c_left, k)
        x = level(xc, k)
        x_left = jnp.where(lane == 0, column(c_left, k), rolled(x, 1, 1))
        base[pl.ds(k * NJ, NJ), :] = z_sum(zc, k, x_left + x + level(dp, k))
    ys, ws, invs, spike = [], [None], [], []
    for j in range(NJ):
        y = across(yc, j)
        diag = across(base, j)
        if j < NJ - 1:
            diag = diag + y
        else:
            diag = diag + jnp.where(e == GY - 1, y, 0.0)
        rhs = across(src, j)
        if j:
            y_before = across(yc, j - 1)
            w = y_before * invs[-1]
            ws.append(w)
            diag = diag + y_before - w * y_before
            rhs = rhs + w * ys[-1]
            spike.append(w * spike[-1])
            yw[pl.ds(j * NK, NK), :] = w
        else:
            spike.append(jnp.ones((NK, NI), F32))
            yw[pl.ds(0, NK), :] = jnp.zeros((NK, NI), F32)
        ys.append(rhs)
        invs.append(1.0 / diag)
        yinv[pl.ds(j * NK, NK), :] = invs[-1]
    for j in range(NJ - 1, -1, -1):
        if j == NJ - 1:
            gv, av, bv = ys[j] * invs[j], spike[j] * invs[j], invs[j]
            send[pl.ds(NK, NK), :] = gv
            send[pl.ds(4 * NK, NK), :] = bv + 1.0 / across(yc, j)
        else:
            w = ws[j + 1]
            gv, av, bv = ys[j] * invs[j] + w * gv, spike[j] * invs[j] + w * av, w * bv
        place = pl.ds(j * NK, NK)
        yg[place, :], ya[place, :], yb[place, :] = gv, av, bv
    send[pl.ds(0, NK), :] = gv
    send[pl.ds(2 * NK, NK), :] = av
    send[pl.ds(3 * NK, NK), :] = bv


def y_fluxes(fs, source, low, inv, up):
    zero = jnp.zeros((NK, NI), F32)
    fs[0], fs[GY] = zero, zero
    forward = [source(0)]
    for n in range(1, GY - 1):
        forward.append(source(n) + low(n) * forward[-1])
    value = forward[-1] * inv(GY - 2)
    fs[GY - 1] = value
    for n in range(GY - 3, -1, -1):
        value = forward[n] * inv(n) + up(n) * value
        fs[1 + n] = value


def y_finish(fs, yc, below, yg, ya, yb, field, terms):
    e = lax.axis_index("gy")
    flux_left, flux_right = fs[e], fs[e + 1]
    block = lambda ref, j: ref[pl.ds(j * NK, NK), :]
    p = [block(yg, j) - block(ya, j) * flux_left + block(yb, j) * flux_right for j in range(NJ)]
    for j in range(NJ):
        y = across(yc, j)
        if j:
            before = across(yc, j - 1) * p[j - 1]
        else:
            before = below[pl.ds(0, NK), :] * p[0] - flux_left
        if j < NJ - 1:
            after = y * p[j + 1]
        else:
            after = jnp.where(e == GY - 1, 0.0, y * p[j] + flux_right)
        field[pl.ds(j, NK, stride=NJ), :] = p[j]
        terms[pl.ds(j, NK, stride=NJ), :] = before + after


def x_again_kernel(xs, below, mine, other, yg, ya, yb, mult, order, g, yred, send, fs, field, terms):
    f, p, xc, yc, zc, dp = parts(xs)
    odd = lax.rem(lax.axis_index("gy"), 2) == 1

    def part(n, q):
        one, two = mine[n // 2, pl.ds(q * NK, NK), :], other[n // 2, pl.ds(q * NK, NK), :]
        return jnp.where(odd, one, two) if n % 2 else jnp.where(odd, two, one)

    prev = None
    for n in range(GY - 1):
        dd = part(n, 4) + part(n + 1, 2)
        if n:
            m = part(n, 3)
            low = m * prev
            dd = dd - low * m
            yred[n] = low
        else:
            yred[n] = jnp.zeros_like(dd)
        prev = 1.0 / dd
        yred[GY + n] = prev
        yred[2 * GY + n] = part(n + 1, 3) * prev
    yred[GY - 1] = jnp.zeros((NK, NI), F32)
    yred[2 * GY - 1] = jnp.zeros((NK, NI), F32)
    yred[3 * GY - 1] = jnp.zeros((NK, NI), F32)
    y_fluxes(
        fs,
        lambda n: part(n + 1, 0) - part(n, 1),
        lambda n: yred[n],
        lambda n: yred[GY + n],
        lambda n: yred[2 * GY + n],
    )
    y_finish(fs, yc, below, yg, ya, yb, field, terms)
    lane = lanes(NJ)
    packed = jnp.zeros((NJ, NI), F32)
    group = 2
    for k0 in range(0, NK, group):
        rhs = jnp.concatenate(
            [z_terms(zc, field, k, level(f, k) + level(terms, k)) for k in range(k0, k0 + group)], axis=0
        )
        place = pl.ds(k0 * NJ, group * NJ)
        rhs = x_second_solve(rhs, lambda n: mult[pl.ds(n * ROWS + k0 * NJ, group * NJ), :])
        g[place, :] = rhs
        for k in range(k0, k0 + group):
            mine = rhs[(k - k0) * NJ : (k - k0 + 1) * NJ]
            packed = jnp.where(lane == k, column(mine, 0), packed)
            packed = jnp.where(lane == NK + k, column(mine, NI - 1), packed)
    send[...] = packed


def y_again_kernel(xs, got, g, a, b, xred, cl, yw, yinv, yg, send, fs, field, src):
    f, p, xc, yc, zc, dp = parts(xs)
    part = lambda n, q: rolled(got[n], -NK * q, 1)
    x_fluxes(
        fs,
        lambda n: part(n + 1, 0) - part(n, 1),
        [xred[n] for n in range(GX - 1)],
        [xred[GX + n] for n in range(GX - 1)],
        [xred[2 * GX + n] for n in range(GX - 1)],
    )
    fluxes = x_finish(fs, g, a, b, field)
    c_left = cl[...]
    for k in range(NK):
        src[pl.ds(k * NJ, NJ), :] = y_source(f, xc, zc, field, fluxes, c_left, k)
    block = lambda ref, j: ref[pl.ds(j * NK, NK), :]
    ys = []
    for j in range(NJ):
        rhs = across(src, j)
        if j:
            rhs = rhs + block(yw, j) * ys[-1]
        ys.append(rhs)
    value = None
    for j in range(NJ - 1, -1, -1):
        new = ys[j] * block(yinv, j)
        value = new if value is None else new + block(yw, j + 1) * value
        yg[pl.ds(j * NK, NK), :] = value
        if j == NJ - 1:
            send[pl.ds(NK, NK), :] = value
    send[pl.ds(0, NK), :] = value


def residual_kernel(xs, below, got, yg, ya, yb, yred, cl, fluxes, coarse, near, far, fs, terms, tmp, field):
    f, p, xc, yc, zc, dp = parts(xs)
    d = lax.axis_index("gx")
    lane = lanes(NJ)
    part = lambda n, q: got[n, pl.ds(q * NK, NK), :]
    y_fluxes(
        fs,
        lambda n: part(n + 1, 0) - part(n, 1),
        lambda n: yred[n],
        lambda n: yred[GY + n],
        lambda n: yred[2 * GY + n],
    )
    e = lax.axis_index("gy")
    fluxes[0], fluxes[1] = fs[e], fs[e + 1]
    y_finish(fs, yc, below, yg, ya, yb, field, terms)
    c_left = cl[...]
    main, rim = [], []
    for k in range(NK):
        v, x = level(field, k), level(xc, k)
        left = column(c_left, k)
        x_left = jnp.where(lane == 0, left, rolled(x, 1, 1))
        diag = z_sum(zc, k, x_left + x + y_left_of(yc, below, k) + level(yc, k) + level(dp, k))
        around = jnp.where(lane == 0, 0.0, x_left * rolled(v, 1, 1)) + jnp.where(lane == NI - 1, 0.0, x * rolled(v, -1, 1))
        main.append(level(f, k) - (diag * v - around - level(terms, k) - z_terms(zc, field, k, jnp.zeros((NJ, NI), F32))))
        last = jnp.where(d == GX - 1, 0.0, x * v)
        rim.append(jnp.where(lane == 0, left * v, jnp.where(lane == NI - 1, last, 0.0)))
    pairs = jnp.concatenate([main[2 * K] + main[2 * K + 1] for K in range(NK // 2)], axis=0)
    outer = jnp.concatenate([rim[2 * K] + rim[2 * K + 1] for K in range(NK // 2)], axis=0)
    tmp[...] = squeeze(pairs) + edges(outer)
    store_coarse(coarse, 0, tmp)
    odd = lax.rem(e, 2) == 1
    up, down = coarse[pl.ds(48, 16), :], coarse[pl.ds(0, 16), :]
    near[...] = jnp.where(odd, down, up)
    far[...] = jnp.where(odd, up, down)


def eight(ref, J):
    return ref[pl.ds(J * 8, 8), :]


def coarse_matrix_kernel(ext, got, *outs):
    e = lax.axis_index("gy")
    lane = lanes(8)

    def joint(n, J):
        value = jnp.zeros((8, NI), F32)
        for d in range(GX):
            moved = rolled(got[d, pl.ds(NJ + n * 8, 8), :], 10 * (d - J), 1)
            value = jnp.where(jnp.logical_and(lane >= 10 * d, lane < 10 * d + 10), moved, value)
        return value

    own = lambda n, J: ext[pl.ds(n * 96 + J * 8, 8), :]
    first = jnp.logical_and(lax.rem(lane, 10) == 0, lane > 0)
    for out, source, width in ((outs[0], own, 64), (outs[1], joint, 10 * GX)):
        y_before = jnp.zeros((8, NI), F32)
        for J in range(12):
            x, y, z_top, rest = (source(n, J) for n in range(4))
            x_left = rolled(x, 1, 1)
            at = e * 8 + J - 2
            valid = jnp.logical_and(jnp.logical_and(at >= 0, at < 8 * GY), lane < width)
            if width != 64:
                rest = rest + jnp.where(first, x_left, 0.0)
            weight = jnp.where(valid, RELAX / jnp.where(valid, rest, 1.0), 0.0)
            couplings = (x_left, x, y_before, y, rolled(z_top, 1, 0), z_top)
            for n, value in enumerate((weight, *(weight * c for c in couplings))):
                out[n, pl.ds(J * 8, 8), :] = value
            y_before = y


def relaxed(res, matrix):
    at = lambda n, J: matrix[n, pl.ds(J * 8, 8), :]

    def around(v, J):
        return (
            at(1, J) * rolled(v[J], 1, 1)
            + at(2, J) * rolled(v[J], -1, 1)
            + at(3, J) * v[J - 1]
            + at(4, J) * v[J + 1]
            + at(5, J) * rolled(v[J], 1, 0)
            + at(6, J) * rolled(v[J], -1, 0)
        )

    first = {J: at(0, J) * res[J] for J in range(12)}
    second = {J: (2.0 - RELAX) * first[J] + around(first, J) for J in range(1, 11)}
    return [first[J] + (1.0 - RELAX) * second[J] + around(second, J) for J in range(2, 10)]


def coarse_own_kernel(order, near, far, coarse, matrix, send):
    lane = lanes(8)
    lower, upper = sorted_out(near, far, pl.ds(0, 16))
    res = [lower[:8], lower[8:], *(eight(coarse, J) for J in range(8)), upper[:8], upper[8:]]
    done = relaxed(res, matrix)
    for t in range(4):
        send[pl.ds(t * 8, 8), :] = jnp.where(lane < 64, done[t], rolled(done[t + 4], 64, 1))
    strips = [jnp.zeros((8, NI), F32)] * 2
    for J in range(12):
        at = 16 * (J % 8)
        strip = jnp.where(jnp.logical_and(lane >= at, lane < at + 6), rolled(res[J], at + 1, 1), strips[J // 8])
        strips[J // 8] = jnp.where(jnp.logical_and(lane >= at + 6, lane < at + 12), rolled(res[J], at + 6 - 59, 1), strip)
    send[pl.ds(32, 8), :] = strips[0]
    send[pl.ds(40, 8), :] = strips[1]


def coarse_last_kernel(got, coarse, matrix, res_out, cor_out, tmp, res_tmp):
    d_own = lax.axis_index("gx")
    lane = lanes(8)
    joint = []
    for J in range(12):
        value = jnp.zeros((8, NI), F32)
        for d in range(GX):
            low = 10 * d - 1
            moved = rolled(got[d, pl.ds(32 + 8 * (J // 8), 8), :], low - 16 * (J % 8), 1)
            value = value + jnp.where(jnp.logical_and(lane >= low, lane < low + 12), moved, 0.0)
        joint.append(value)
    done = relaxed(joint, matrix)
    for J in range(8):
        ends = joint[J + 2]
        mine = rolled(ends, 0, 1)
        for d in range(1, GX):
            mine = jnp.where(d_own == d, rolled(ends, -10 * d, 1), mine)
        mine = jnp.where(lane == 0, mine, jnp.where(lane == 63, rolled(mine, 54, 1), eight(coarse, J)))
        res_tmp[pl.ds(J, 8, stride=8), :] = mine
        rows = pl.ds((J % 4) * 8, 8)
        for m in range(4):
            even, odd = got[2 * m, rows, :], got[2 * m + 1, rows, :]
            if J < 4:
                odd = rolled(odd, 64, 1)
            else:
                even = rolled(even, 64, 1)
            value = jnp.where(lane < 64, even, odd)
            for d in (2 * m, 2 * m + 1):
                start = 64 * (d % 2)
                left = jnp.logical_and(lane >= start, lane < start + 3)
                right = jnp.logical_and(lane >= start + 61, lane < start + 64)
                value = jnp.where(left, rolled(done[J], start - 10 * d, 1), value)
                value = jnp.where(right, rolled(done[J], start + 54 - 10 * d, 1), value)
            tmp[m, pl.ds(J, 8, stride=8), :] = value
    for m in range(4):
        cor_out[:, pl.ds(m * NI, NI)] = tmp[m]
    res_out[...] = res_tmp[:, :64]


def field_kernel(fluxes, yg, ya, yb, field):
    for j in range(NJ):
        place = pl.ds(j * NK, NK)
        field[pl.ds(j, NK, stride=NJ), :] = yg[place, :] - ya[place, :] * fluxes[0] + yb[place, :] * fluxes[1]


def spread(value, axis, count):
    many = jnp.broadcast_to(value[None], (count,) + value.shape)
    return lax.all_to_all(many, axis, split_axis=0, concat_axis=0, tiled=True)


def spread_by_core(value):
    groups = [list(range(0, GY, 2)), list(range(1, GY, 2))]
    many = jnp.broadcast_to(value[None], (GY // 2,) + value.shape)
    mine = lax.all_to_all(many, "gy", split_axis=0, concat_axis=0, tiled=True, axis_index_groups=groups)
    return mine, lax.ppermute(mine, "gy", [(n, n ^ 1) for n in range(GY)])


def swap(near, far):
    pairs = [(n, n ^ 1) for n in range(GY)]
    others = [(n, (n + 1) % GY if n % 2 else (n - 1) % GY) for n in range(GY)]
    return lax.ppermute(near, "gy", pairs), lax.ppermute(far, "gy", others)


def body(forcing, pressure_in, x_coupling, y_coupling, z_coupling, damping):
    args = (forcing, pressure_in, x_coupling, y_coupling, z_coupling, damping)
    whole = sds(ROWS, NI)
    kept = sds((2 * len(STEPS) + 1) * ROWS, NI)
    xs, near, far, coef = call(
        first_kernel,
        [sds(6 * ROWS, NI), sds(80, NI), sds(80, NI), sds(128, NI)],
        *[v.reshape(ROWS, NI) for v in args],
        scratch=[(128, NI)],
        hbm=6,
        sems=6,
    )
    near, far = swap(near, far)
    g, a, b, mult, packed = call(x_first_kernel, [whole, whole, whole, kept, sds(NJ, NI)], xs, flops=10**8)
    below, g, a, b, mult, send, ext = call(
        x_rim_kernel,
        [sds(NK, NI), whole, whole, whole, kept, sds(NJ + 32, NI), sds(4 * 96, NI)],
        xs, near, far, coef, packed, g, a, b, mult,
        aliases={5: 1, 6: 2, 7: 3, 8: 4},
    )
    got_coef = got = spread(send, "gx", GX)
    yg, ya, yb, yw, yinv, xred, cl, send = call(
        y_first_kernel,
        [whole] * 5 + [sds(3 * GX, NJ, NI), sds(NJ, NI), sds(5 * NK, NI)],
        xs, got, g, a, b,
        scratch=[(GX + 1, NJ, NI), (GX + 1, NJ, NI), (ROWS, NI), (ROWS, NI), (ROWS, NI)],
    )
    got = spread_by_core(send)
    own, joint = call(coarse_matrix_kernel, [sds(7, 96, NI)] * 2, ext, got_coef, flops=10**7)
    g, yred, send = call(
        x_again_kernel,
        [whole, sds(3 * GY, NK, NI), sds(NJ, NI)],
        xs, below, *got, yg, ya, yb, mult, joint,
        scratch=[(GY + 1, NK, NI), (ROWS, NI), (ROWS, NI)],
    )
    got = spread(send, "gx", GX)
    yg, send = call(
        y_again_kernel,
        [whole, sds(2 * NK, NI)],
        xs, got, g, a, b, xred, cl, yw, yinv,
        scratch=[(GX + 1, NJ, NI), (ROWS, NI), (ROWS, NI)],
    )
    got = spread(send, "gy", GY)
    fluxes, coarse, near, far = call(
        residual_kernel,
        [sds(2, NK, NI), sds(64, NI), sds(16, NI), sds(16, NI)],
        xs, below, got, yg, ya, yb, yred, cl,
        scratch=[(GY + 1, NK, NI), (ROWS, NI), (128, NI), (ROWS, NI)],
    )
    near, far = swap(near, far)
    (field,) = call(field_kernel, [whole], fluxes, yg, ya, yb, flops=10**7)
    (send,) = call(coarse_own_kernel, [sds(48, NI)], field, near, far, coarse, own, hbm=1)
    got = spread(send, "gx", GX)
    res, cor = call(
        coarse_last_kernel, [sds(64, 64), sds(64, 4 * NI)], got, coarse, joint, scratch=[(4, 64, NI), (64, NI)]
    )
    return field.reshape(NK, NJ, NI), res.reshape(8, 8, 64), cor.reshape(8, 8, 512)


def solution(mesh):
    spec = P(None, "gy", "gx")
    return jax.shard_map(
        body, mesh=mesh, in_specs=(spec,) * 6, out_specs=(spec, spec, P(None, "gy", None)), check_vma=False
    )
```

```python
import functools

import jax
import jax.numpy as jnp
from jax import lax
from jax.experimental import pallas as pl
from jax.experimental.pallas import tpu as pltpu
from jax.sharding import PartitionSpec as P

RELAX = 0.8
NK, NJ, NI = 16, 16, 128
ROWS = NK * NJ
GX, GY = 8, 16
CHIPS = GY // 2
STEPS = (1, 2, 4, 8, 16, 32, 64)
F32 = jnp.float32


def sds(*shape):
    return jax.ShapeDtypeStruct(shape, F32)


def call(kernel, outs, *args, scratch=(), hbm=0, aliases={}, sems=0, flops=None):
    spec = pl.BlockSpec(memory_space=pltpu.VMEM)
    outside = pl.BlockSpec(memory_space=pltpu.HBM)
    args = [pltpu.with_memory_space_constraint(v, pltpu.HBM) for v in args[:hbm]] + list(args[hbm:])
    shapes = [pltpu.VMEM(v, F32) for v in scratch]
    if sems:
        shapes.append(pltpu.SemaphoreType.DMA((sems,)))
    cost = None if flops is None else pl.CostEstimate(flops=flops, bytes_accessed=1 << 20, transcendentals=0)
    return pl.pallas_call(
        kernel,
        out_shape=outs,
        in_specs=[outside] * hbm + [spec] * (len(args) - hbm),
        out_specs=[spec] * len(outs),
        scratch_shapes=shapes,
        input_output_aliases=aliases,
        cost_estimate=cost,
        compiler_params=pltpu.CompilerParams(vmem_limit_bytes=16 * 1024 * 1024),
    )(*args)


def parts(xs):
    return [xs.at[pl.ds(n * ROWS, ROWS), :] for n in range(6)]


def lanes(rows, width=NI):
    return lax.broadcasted_iota(jnp.int32, (rows, width), 1)


def rolled(value, amount, axis):
    return pltpu.roll(value, amount % value.shape[axis], axis)


def level(ref, k):
    return ref[pl.ds(k * NJ, NJ), :]


def across(ref, j, count=NK, stride=NJ):
    return ref[pl.ds(j, count, stride=stride), :]


def column(value, k):
    return jnp.broadcast_to(value[:, k : k + 1], (value.shape[0], NI))


def z_pair(zc, k):
    return (level(zc, k - 1) if k > 0 else None, level(zc, k) if k < NK - 1 else None)


def z_sum(zc, k, base):
    low, top = z_pair(zc, k)
    if low is not None:
        base = base + low
    if top is not None:
        base = base + top
    return base


def z_terms(zc, field, k, base):
    low, top = z_pair(zc, k)
    if low is not None:
        base = base + low * level(field, k - 1)
    if top is not None:
        base = base + top * level(field, k + 1)
    return base


def y_left_of(yc, halo, k):
    row = lax.broadcasted_iota(jnp.int32, (NJ, NI), 0)
    return jnp.where(row == 0, halo[pl.ds(k, 1), :], rolled(level(yc, k), 1, 0))


def exact_dot(values, matrix):
    matrix = matrix.astype(jnp.bfloat16)
    total = None
    for _ in range(3):
        piece = values.astype(jnp.bfloat16)
        values = values - piece.astype(F32)
        part = jnp.dot(piece, matrix, preferred_element_type=F32)
        total = part if total is None else total + part
    return total


def squeeze(values, scale=0.125, start=0):
    source = lax.broadcasted_iota(jnp.int32, (NI, NI), 0)
    target = lax.broadcasted_iota(jnp.int32, (NI, NI), 1)
    matrix = jnp.where(source // 2 + start == target, scale, 0.0).astype(F32)
    return exact_dot(values, matrix)


def edges(values, scale=0.125):
    source = lax.broadcasted_iota(jnp.int32, (NI, NI), 0)
    target = lax.broadcasted_iota(jnp.int32, (NI, NI), 1)
    hit = ((source == NI - 1) & (target == 64)) | ((source == 0) & (target == NI - 1))
    matrix = jnp.where(hit, scale, 0.0).astype(F32)
    return exact_dot(values, matrix)


def store_coarse(out, base, tmp):
    for J in range(NJ // 2):
        out[pl.ds(base + J * 8, 8), :] = across(tmp, 2 * J, 8) + across(tmp, 2 * J + 1, 8)


def first_kernel(fh, ph, xh, yh, zh, dh, xs, near, far, coarse, tmp, sems):
    copies = [
        pltpu.make_async_copy(ref, xs.at[pl.ds(n * ROWS, ROWS), :], sems.at[n])
        for n, ref in enumerate((fh, ph, xh, yh, zh, dh))
    ]
    for copy in copies:
        copy.start()
    for copy in copies[1:]:
        copy.wait()
    f, p, xc, yc, zc, dp = parts(xs)
    odd = lax.rem(lax.axis_index("gy"), 2) == 1
    for q, two in enumerate(((xc, yc), (zc, dp))):
        total = jnp.zeros((128, NI), F32)
        for half, ref in enumerate(two):
            pairs = jnp.concatenate([level(ref, 2 * K) + level(ref, 2 * K + 1) for K in range(NK // 2)], axis=0)
            total = total + squeeze(pairs, start=64 * half)
        tmp[...] = total
        store_coarse(coarse, q * 64, tmp)

    def put(place, up, down):
        near[place, :] = jnp.where(odd, down, up)
        far[place, :] = jnp.where(odd, up, down)

    put(pl.ds(0, NK), across(p, NJ - 1), across(p, 0))
    put(pl.ds(NK, NK), across(yc, NJ - 1), across(yc, 0))
    for q in range(2):
        put(pl.ds(2 * NK + q * 24, 24), coarse[pl.ds(q * 64 + 40, 24), :], coarse[pl.ds(q * 64, 24), :])
    copies[0].wait()


def sorted_out(near, far, place):
    e = lax.axis_index("gy")
    odd = lax.rem(e, 2) == 1
    one, two = near[place, :], far[place, :]
    return (
        jnp.where(e == 0, 0.0, jnp.where(odd, one, two)),
        jnp.where(e == GY - 1, 0.0, jnp.where(odd, two, one)),
    )


def x_matrix(x, rest):
    d = lax.axis_index("gx")
    lane = lanes(x.shape[0])
    inner = jnp.logical_or(lane < NI - 1, d == GX - 1)
    diag = jnp.where(lane == 0, 0.0, rolled(x, 1, 1)) + jnp.where(inner, x, 0.0) + rest
    return diag, jnp.where(lane == NI - 1, 0.0, -x)


def x_eliminate(diag, off, rhs, keep):
    wide = lanes(diag.shape[0])
    ends = jnp.where(jnp.logical_or(wide == 0, wide == NI - 1), 1.0, 0.0).astype(F32)
    for n, s in enumerate(STEPS):
        inv = 1.0 / diag
        low = rolled(off, s, 1)
        alpha = -low * rolled(inv, s, 1)
        beta = -off * rolled(inv, -s, 1)
        keep(2 * n, alpha)
        keep(2 * n + 1, beta)
        diag = diag + alpha * low + beta * off
        rhs = rhs + alpha * rolled(rhs, s, 1) + beta * rolled(rhs, -s, 1)
        if s < NI // 2:
            off = beta * rolled(off, -s, 1)
            ends = ends + alpha * rolled(ends, s, 1) + beta * rolled(ends, -s, 1)
    inv = 1.0 / diag
    keep(2 * len(STEPS), inv)
    other = rolled(ends, NI // 2, 1)
    left = jnp.where(wide < NI // 2, ends, alpha * other)
    right = jnp.where(wide < NI // 2, beta * other, ends)
    return rhs * inv, left * inv, right * inv


def x_picks(g, a, b, x):
    return column(g, 0), column(g, NI - 1), column(a, 0), column(b, 0), column(b, NI - 1), column(x, NI - 1)


def x_first_kernel(xs, g, a, b, mult, packed_out):
    f, p, xc, yc, zc, dp = parts(xs)
    lane = lanes(NJ)
    row = lax.broadcasted_iota(jnp.int32, (NJ, NI), 0)
    packed = jnp.zeros((NJ, NI), F32)
    group = 8
    for k0 in range(0, NK, group):
        diag, off, rhs = [], [], []
        for k in range(k0, k0 + group):
            y, v = level(yc, k), level(p, k)
            y_left = jnp.where(row == 0, 0.0, rolled(y, 1, 0))
            matrix = x_matrix(level(xc, k), z_sum(zc, k, y_left + y + level(dp, k)))
            diag.append(matrix[0])
            off.append(matrix[1])
            after = jnp.where(row == NJ - 1, 0.0, rolled(v, -1, 0))
            rhs.append(z_terms(zc, p, k, level(f, k) + y_left * rolled(v, 1, 0) + y * after))
        diag, off, rhs = (jnp.concatenate(v, axis=0) for v in (diag, off, rhs))
        place = pl.ds(k0 * NJ, group * NJ)

        def keep(n, value):
            mult[pl.ds(n * ROWS + k0 * NJ, group * NJ), :] = value

        rhs, left, right = x_eliminate(diag, off, rhs, keep)
        g[place, :], a[place, :], b[place, :] = rhs, left, right
        for k in range(k0, k0 + group):
            part = slice((k - k0) * NJ, (k - k0 + 1) * NJ)
            for q, pick in enumerate(x_picks(rhs[part], left[part], right[part], level(xc, k))):
                packed = jnp.where(lane == q * NK + k, pick, packed)
    packed_out[...] = packed


def x_rim_kernel(xs, near, far, coarse, packed, g_in, a_in, b_in, mult_in, below, g, a, b, mult, send, ext):
    f, p, xc, yc, zc, dp = parts(xs)
    lane = lanes(NK)
    row = lax.broadcasted_iota(jnp.int32, (NK, NI), 0)

    def lifted(j):
        z, v = across(zc, j), across(p, j)
        top = jnp.where(row == NK - 1, 0.0, z)
        low = rolled(top, 1, 0)
        return low, top, low * rolled(v, 1, 0) + top * rolled(v, -1, 0)

    p_below, p_above = sorted_out(near, far, pl.ds(0, NK))
    y_left, _ = sorted_out(near, far, pl.ds(NK, NK))
    below[...] = y_left
    low, top, z_part = lifted(0)
    y = across(yc, 0)
    diag, off = x_matrix(across(xc, 0), low + top + y + y_left + across(dp, 0))
    rhs = across(f, 0) + y_left * p_below + y * across(p, 1) + z_part

    def keep(n, value):
        mult[pl.ds(n * ROWS, NK, stride=NJ), :] = value

    rhs, left, right = x_eliminate(diag, off, rhs, keep)
    first = pl.ds(0, NK, stride=NJ)
    g[first, :], a[first, :], b[first, :] = rhs, left, right
    line = jnp.zeros((NK, NI), F32)
    for q, pick in enumerate(x_picks(rhs, left, right, across(xc, 0))):
        line = line + jnp.where(lane == q * NK + row, pick, 0.0)
    line = jnp.sum(line, axis=0, keepdims=True)

    j = NJ - 1
    _, _, z_part = lifted(j)
    y = across(yc, j)
    rhs = across(f, j) + across(yc, j - 1) * across(p, j - 1) + y * p_above + z_part
    rhs = x_second_solve(rhs, lambda n: mult_in[pl.ds(n * ROWS + j, NK, stride=NJ), :])
    g[pl.ds(j, NK, stride=NJ), :] = rhs
    last = jnp.where(lane == row, column(rhs, 0), 0.0) + jnp.where(lane == NK + row, column(rhs, NI - 1), 0.0)
    last = jnp.sum(last, axis=0, keepdims=True)
    was = packed[...]
    was = jnp.where(row == 0, line, was)
    send[pl.ds(0, NJ), :] = jnp.where(jnp.logical_and(row == NJ - 1, lane < 2 * NK), last, was)
    coarse_share(near, far, coarse, send, ext)


def coarse_share(near, far, coarse, send, ext):
    wide = lanes(8)
    level_k = lax.broadcasted_iota(jnp.int32, (8, NI), 0)
    fields = [[], [], [], []]
    for q in range(2):
        lower, upper = sorted_out(near, far, pl.ds(2 * NK + q * 24, 24))
        rows = [lower[n * 8 : n * 8 + 8] for n in range(3)]
        rows += [coarse[pl.ds(q * 64 + n * 8, 8), :] for n in range(8)]
        rows += [upper[n * 8 : n * 8 + 8] for n in range(2)]
        for row in rows:
            fields[2 * q].append(jnp.where(wide < 64, row, 0.0))
            fields[2 * q + 1].append(jnp.where(wide < 64, rolled(row, 64, 1), 0.0))
    xs_, ys_, zs_, damps = fields
    shares = [jnp.zeros((8, NI), F32)] * 4
    for J in range(12):
        top = jnp.where(level_k == 7, 0.0, zs_[J + 1])
        rest = damps[J + 1] + ys_[J + 1] + ys_[J] + top + rolled(top, 1, 0) + xs_[J + 1] + rolled(xs_[J + 1], 1, 1)
        for n, value in enumerate((xs_[J + 1], ys_[J + 1], top, rest)):
            ext[pl.ds(n * 96 + J * 8, 8), :] = value
            at = 10 * J
            first, last = rolled(value, at, 1), rolled(value, at + 5 - 59, 1)
            share = jnp.where(jnp.logical_and(wide >= at, wide < at + 5), first, shares[n])
            shares[n] = jnp.where(jnp.logical_and(wide >= at + 5, wide < at + 10), last, share)
    for n in range(4):
        send[pl.ds(NJ + n * 8, 8), :] = shares[n]


def x_second_solve(rhs, kept):
    for n, s in enumerate(STEPS):
        rhs = rhs + kept(2 * n) * rolled(rhs, s, 1) + kept(2 * n + 1) * rolled(rhs, -s, 1)
    return rhs * kept(2 * len(STEPS))


def x_fluxes(fs, source, low, inv, up):
    zero = jnp.zeros((NJ, NI), F32)
    fs[0], fs[GX] = zero, zero
    forward = [source(0)]
    for d in range(1, GX - 1):
        forward.append(source(d) + low[d] * forward[-1])
    value = forward[-1] * inv[GX - 2]
    fs[GX - 1] = value
    for d in range(GX - 3, -1, -1):
        value = forward[d] * inv[d] + up[d] * value
        fs[1 + d] = value


def x_finish(fs, g, a, b, field):
    d = lax.axis_index("gx")
    flux_left, flux_right = fs[d], fs[d + 1]
    for k in range(NK):
        field[pl.ds(k * NJ, NJ), :] = (
            level(g, k) - level(a, k) * column(flux_left, k) + level(b, k) * column(flux_right, k)
        )
    return flux_left, flux_right


def y_source(f, xc, zc, field, fluxes, c_left, k):
    d = lax.axis_index("gx")
    lane = lanes(NJ)
    flux_left, flux_right = fluxes
    v, x = level(field, k), level(xc, k)
    before = jnp.where(lane == 0, column(c_left, k) * v - column(flux_left, k), rolled(x * v, 1, 1))
    last = jnp.where(d == GX - 1, 0.0, x * v + column(flux_right, k))
    after = jnp.where(lane == NI - 1, last, x * rolled(v, -1, 1))
    return z_terms(zc, field, k, level(f, k) + before + after)


def y_first_kernel(xs, got, g, a, b, yg, ya, yb, yw, yinv, xred, cl, send, fs, cs, field, src, base):
    f, p, xc, yc, zc, dp = parts(xs)
    d = lax.axis_index("gx")
    e = lax.axis_index("gy")
    lane = lanes(NJ)
    part = lambda n, q: rolled(got[n, pl.ds(0, NJ), :], -NK * q, 1)
    m = [part(n, 3) for n in range(GX)]
    low, inv, up = [None], [], []
    for n in range(GX - 1):
        dd = part(n, 4) + 1.0 / part(n, 5) + part(n + 1, 2)
        if n:
            low.append(m[n] * inv[-1])
            dd = dd - low[n] * m[n]
        inv.append(1.0 / dd)
        up.append(m[n + 1] * inv[n])
        xred[n], xred[GX + n], xred[2 * GX + n] = (low[n] if n else jnp.zeros_like(dd)), inv[n], up[n]
    x_fluxes(fs, lambda n: part(n + 1, 0) - part(n, 1), low, inv, up)
    cs[0] = jnp.zeros((NJ, NI), F32)
    for n in range(GX):
        cs[n + 1] = part(n, 5)
    c_left = cs[d]
    cl[...] = c_left
    fluxes = x_finish(fs, g, a, b, field)
    for k in range(NK):
        src[pl.ds(k * NJ, NJ), :] = y_source(f, xc, zc, field, fluxes, c_left, k)
        x = level(xc, k)
        x_left = jnp.where(lane == 0, column(c_left, k), rolled(x, 1, 1))
        base[pl.ds(k * NJ, NJ), :] = z_sum(zc, k, x_left + x + level(dp, k))
    ys, ws, invs, spike = [], [None], [], []
    for j in range(NJ):
        y = across(yc, j)
        diag = across(base, j)
        if j < NJ - 1:
            diag = diag + y
        else:
            diag = diag + jnp.where(e == GY - 1, y, 0.0)
        rhs = across(src, j)
        if j:
            y_before = across(yc, j - 1)
            w = y_before * invs[-1]
            ws.append(w)
            diag = diag + y_before - w * y_before
            rhs = rhs + w * ys[-1]
            spike.append(w * spike[-1])
            yw[pl.ds(j * NK, NK), :] = w
        else:
            spike.append(jnp.ones((NK, NI), F32))
            yw[pl.ds(0, NK), :] = jnp.zeros((NK, NI), F32)
        ys.append(rhs)
        invs.append(1.0 / diag)
        yinv[pl.ds(j * NK, NK), :] = invs[-1]
    for j in range(NJ - 1, -1, -1):
        if j == NJ - 1:
            gv, av, bv = ys[j] * invs[j], spike[j] * invs[j], invs[j]
            send[pl.ds(NK, NK), :] = gv
            send[pl.ds(4 * NK, NK), :] = bv + 1.0 / across(yc, j)
        else:
            w = ws[j + 1]
            gv, av, bv = ys[j] * invs[j] + w * gv, spike[j] * invs[j] + w * av, w * bv
        place = pl.ds(j * NK, NK)
        yg[place, :], ya[place, :], yb[place, :] = gv, av, bv
    send[pl.ds(0, NK), :] = gv
    send[pl.ds(2 * NK, NK), :] = av
    send[pl.ds(3 * NK, NK), :] = bv


def y_fluxes(fs, source, low, inv, up):
    zero = jnp.zeros((NK, NI), F32)
    fs[0], fs[CHIPS] = zero, zero
    forward = [source(0)]
    for n in range(1, CHIPS - 1):
        forward.append(source(n) + low(n) * forward[-1])
    value = forward[-1] * inv(CHIPS - 2)
    fs[CHIPS - 1] = value
    for n in range(CHIPS - 3, -1, -1):
        value = forward[n] * inv(n) + up(n) * value
        fs[1 + n] = value


def own_fluxes(fs, joint, inner):
    e = lax.axis_index("gy")
    outer_left, outer_right = fs[e // 2], fs[e // 2 + 1]
    between = inner[...] + joint[1] * outer_left + joint[2] * outer_right
    odd = lax.rem(e, 2) == 1
    return jnp.where(odd, between, outer_left), jnp.where(odd, outer_right, between)


def join_first_kernel(order, mine, theirs, send, joint, inner):
    odd = lax.rem(lax.axis_index("gy"), 2) == 1
    block = lambda ref, q: ref[pl.ds(q * NK, NK), :]
    low = [jnp.where(odd, block(theirs, q), block(mine, q)) for q in range(5)]
    high = [jnp.where(odd, block(mine, q), block(theirs, q)) for q in range(5)]
    inv = 1.0 / (low[4] + high[2])
    from_low, from_high = low[3] * inv, high[3] * inv
    base = (high[0] - low[1]) * inv
    values = (
        low[0] + low[3] * base,
        high[1] - high[3] * base,
        low[2] - low[3] * from_low,
        low[3] * from_high,
        high[4] - high[3] * from_high,
    )
    for q, value in enumerate(values):
        send[pl.ds(q * NK, NK), :] = value
    for n, value in enumerate((inv, from_low, from_high, low[3], high[3])):
        joint[n] = value
    inner[...] = base


def join_again_kernel(mine, theirs, joint, send, inner):
    odd = lax.rem(lax.axis_index("gy"), 2) == 1
    block = lambda ref, q: ref[pl.ds(q * NK, NK), :]
    low = [jnp.where(odd, block(theirs, q), block(mine, q)) for q in range(2)]
    high = [jnp.where(odd, block(mine, q), block(theirs, q)) for q in range(2)]
    base = (high[0] - low[1]) * joint[0]
    send[pl.ds(0, NK), :] = low[0] + joint[3] * base
    send[pl.ds(NK, NK), :] = high[1] - joint[4] * base
    inner[...] = base


def y_finish(fluxes, yc, below, yg, ya, yb, field, terms):
    e = lax.axis_index("gy")
    flux_left, flux_right = fluxes
    block = lambda ref, j: ref[pl.ds(j * NK, NK), :]
    p = [block(yg, j) - block(ya, j) * flux_left + block(yb, j) * flux_right for j in range(NJ)]
    for j in range(NJ):
        y = across(yc, j)
        if j:
            before = across(yc, j - 1) * p[j - 1]
        else:
            before = below[pl.ds(0, NK), :] * p[0] - flux_left
        if j < NJ - 1:
            after = y * p[j + 1]
        else:
            after = jnp.where(e == GY - 1, 0.0, y * p[j] + flux_right)
        field[pl.ds(j, NK, stride=NJ), :] = p[j]
        terms[pl.ds(j, NK, stride=NJ), :] = before + after


def x_again_kernel(xs, below, got, joint, inner, yg, ya, yb, mult, g, yred, send, fs, field, terms):
    f, p, xc, yc, zc, dp = parts(xs)
    part = lambda n, q: got[n, pl.ds(q * NK, NK), :]
    prev = None
    for n in range(CHIPS - 1):
        dd = part(n, 4) + part(n + 1, 2)
        if n:
            m = part(n, 3)
            low = m * prev
            dd = dd - low * m
            yred[n] = low
        else:
            yred[n] = jnp.zeros_like(dd)
        prev = 1.0 / dd
        yred[CHIPS + n] = prev
        yred[2 * CHIPS + n] = part(n + 1, 3) * prev
    for n in range(1, 4):
        yred[n * CHIPS - 1] = jnp.zeros((NK, NI), F32)
    y_fluxes(
        fs,
        lambda n: part(n + 1, 0) - part(n, 1),
        lambda n: yred[n],
        lambda n: yred[CHIPS + n],
        lambda n: yred[2 * CHIPS + n],
    )
    y_finish(own_fluxes(fs, joint, inner), yc, below, yg, ya, yb, field, terms)
    lane = lanes(NJ)
    packed = jnp.zeros((NJ, NI), F32)
    group = 2
    for k0 in range(0, NK, group):
        rhs = jnp.concatenate(
            [z_terms(zc, field, k, level(f, k) + level(terms, k)) for k in range(k0, k0 + group)], axis=0
        )
        place = pl.ds(k0 * NJ, group * NJ)
        rhs = x_second_solve(rhs, lambda n: mult[pl.ds(n * ROWS + k0 * NJ, group * NJ), :])
        g[place, :] = rhs
        for k in range(k0, k0 + group):
            mine = rhs[(k - k0) * NJ : (k - k0 + 1) * NJ]
            packed = jnp.where(lane == k, column(mine, 0), packed)
            packed = jnp.where(lane == NK + k, column(mine, NI - 1), packed)
    send[...] = jnp.where(lanes(8) < 2 * NK, packed[:8], rolled(packed[8:], 2 * NK, 1))


def y_again_kernel(xs, got, g, a, b, xred, cl, yw, yinv, yg, send, fs, field, src):
    f, p, xc, yc, zc, dp = parts(xs)
    part = lambda n, q: jnp.concatenate([rolled(got[n], -NK * q, 1), rolled(got[n], -NK * (q + 2), 1)], axis=0)
    x_fluxes(
        fs,
        lambda n: part(n + 1, 0) - part(n, 1),
        [xred[n] for n in range(GX - 1)],
        [xred[GX + n] for n in range(GX - 1)],
        [xred[2 * GX + n] for n in range(GX - 1)],
    )
    fluxes = x_finish(fs, g, a, b, field)
    c_left = cl[...]
    for k in range(NK):
        src[pl.ds(k * NJ, NJ), :] = y_source(f, xc, zc, field, fluxes, c_left, k)
    block = lambda ref, j: ref[pl.ds(j * NK, NK), :]
    ys = []
    for j in range(NJ):
        rhs = across(src, j)
        if j:
            rhs = rhs + block(yw, j) * ys[-1]
        ys.append(rhs)
    value = None
    for j in range(NJ - 1, -1, -1):
        new = ys[j] * block(yinv, j)
        value = new if value is None else new + block(yw, j + 1) * value
        yg[pl.ds(j * NK, NK), :] = value
        if j == NJ - 1:
            send[pl.ds(NK, NK), :] = value
    send[pl.ds(0, NK), :] = value


def residual_kernel(xs, below, got, joint, inner, yg, ya, yb, yred, cl, fluxes, coarse, near, far, fs, terms, tmp, field):
    f, p, xc, yc, zc, dp = parts(xs)
    d = lax.axis_index("gx")
    lane = lanes(NJ)
    part = lambda n, q: got[n, pl.ds(q * NK, NK), :]
    y_fluxes(
        fs,
        lambda n: part(n + 1, 0) - part(n, 1),
        lambda n: yred[n],
        lambda n: yred[CHIPS + n],
        lambda n: yred[2 * CHIPS + n],
    )
    e = lax.axis_index("gy")
    ends = own_fluxes(fs, joint, inner)
    fluxes[0], fluxes[1] = ends
    y_finish(ends, yc, below, yg, ya, yb, field, terms)
    c_left = cl[...]
    main, rim = [], []
    for k in range(NK):
        v, x = level(field, k), level(xc, k)
        left = column(c_left, k)
        x_left = jnp.where(lane == 0, left, rolled(x, 1, 1))
        diag = z_sum(zc, k, x_left + x + y_left_of(yc, below, k) + level(yc, k) + level(dp, k))
        around = jnp.where(lane == 0, 0.0, x_left * rolled(v, 1, 1)) + jnp.where(lane == NI - 1, 0.0, x * rolled(v, -1, 1))
        main.append(level(f, k) - (diag * v - around - level(terms, k) - z_terms(zc, field, k, jnp.zeros((NJ, NI), F32))))
        last = jnp.where(d == GX - 1, 0.0, x * v)
        rim.append(jnp.where(lane == 0, left * v, jnp.where(lane == NI - 1, last, 0.0)))
    pairs = jnp.concatenate([main[2 * K] + main[2 * K + 1] for K in range(NK // 2)], axis=0)
    outer = jnp.concatenate([rim[2 * K] + rim[2 * K + 1] for K in range(NK // 2)], axis=0)
    tmp[...] = squeeze(pairs) + edges(outer)
    store_coarse(coarse, 0, tmp)
    odd = lax.rem(e, 2) == 1
    up, down = coarse[pl.ds(48, 16), :], coarse[pl.ds(0, 16), :]
    near[...] = jnp.where(odd, down, up)
    far[...] = jnp.where(odd, up, down)


def eight(ref, J):
    return ref[pl.ds(J * 8, 8), :]


def coarse_matrix_kernel(ext, got, *outs):
    e = lax.axis_index("gy")
    lane = lanes(8)

    def joint(n, J):
        value = jnp.zeros((8, NI), F32)
        for d in range(GX):
            moved = rolled(got[d, pl.ds(NJ + n * 8, 8), :], 10 * (d - J), 1)
            value = jnp.where(jnp.logical_and(lane >= 10 * d, lane < 10 * d + 10), moved, value)
        return value

    own = lambda n, J: ext[pl.ds(n * 96 + J * 8, 8), :]
    first = jnp.logical_and(lax.rem(lane, 10) == 0, lane > 0)
    for out, source, width in ((outs[0], own, 64), (outs[1], joint, 10 * GX)):
        y_before = jnp.zeros((8, NI), F32)
        for J in range(12):
            x, y, z_top, rest = (source(n, J) for n in range(4))
            x_left = rolled(x, 1, 1)
            at = e * 8 + J - 2
            valid = jnp.logical_and(jnp.logical_and(at >= 0, at < 8 * GY), lane < width)
            if width != 64:
                rest = rest + jnp.where(first, x_left, 0.0)
            weight = jnp.where(valid, RELAX / jnp.where(valid, rest, 1.0), 0.0)
            couplings = (x_left, x, y_before, y, rolled(z_top, 1, 0), z_top)
            for n, value in enumerate((weight, *(weight * c for c in couplings))):
                out[n, pl.ds(J * 8, 8), :] = value
            y_before = y


def relaxed(res, matrix):
    at = lambda n, J: matrix[n, pl.ds(J * 8, 8), :]

    def around(v, J):
        return (
            at(1, J) * rolled(v[J], 1, 1)
            + at(2, J) * rolled(v[J], -1, 1)
            + at(3, J) * v[J - 1]
            + at(4, J) * v[J + 1]
            + at(5, J) * rolled(v[J], 1, 0)
            + at(6, J) * rolled(v[J], -1, 0)
        )

    first = {J: at(0, J) * res[J] for J in range(12)}
    second = {J: (2.0 - RELAX) * first[J] + around(first, J) for J in range(1, 11)}
    return [first[J] + (1.0 - RELAX) * second[J] + around(second, J) for J in range(2, 10)]


def coarse_own_kernel(order, near, far, coarse, matrix, send):
    lane = lanes(8)
    lower, upper = sorted_out(near, far, pl.ds(0, 16))
    res = [lower[:8], lower[8:], *(eight(coarse, J) for J in range(8)), upper[:8], upper[8:]]
    done = relaxed(res, matrix)
    for t in range(4):
        send[pl.ds(t * 8, 8), :] = jnp.where(lane < 64, done[t], rolled(done[t + 4], 64, 1))
    strips = [jnp.zeros((8, NI), F32)] * 2
    for J in range(12):
        at = 16 * (J % 8)
        strip = jnp.where(jnp.logical_and(lane >= at, lane < at + 6), rolled(res[J], at + 1, 1), strips[J // 8])
        strips[J // 8] = jnp.where(jnp.logical_and(lane >= at + 6, lane < at + 12), rolled(res[J], at + 6 - 59, 1), strip)
    send[pl.ds(32, 8), :] = strips[0]
    send[pl.ds(40, 8), :] = strips[1]


def coarse_last_kernel(got, coarse, matrix, res_out, cor_out, tmp, res_tmp):
    d_own = lax.axis_index("gx")
    lane = lanes(8)
    joint = []
    for J in range(12):
        value = jnp.zeros((8, NI), F32)
        for d in range(GX):
            low = 10 * d - 1
            moved = rolled(got[d, pl.ds(32 + 8 * (J // 8), 8), :], low - 16 * (J % 8), 1)
            value = value + jnp.where(jnp.logical_and(lane >= low, lane < low + 12), moved, 0.0)
        joint.append(value)
    done = relaxed(joint, matrix)
    for J in range(8):
        ends = joint[J + 2]
        mine = rolled(ends, 0, 1)
        for d in range(1, GX):
            mine = jnp.where(d_own == d, rolled(ends, -10 * d, 1), mine)
        mine = jnp.where(lane == 0, mine, jnp.where(lane == 63, rolled(mine, 54, 1), eight(coarse, J)))
        res_tmp[pl.ds(J, 8, stride=8), :] = mine
        rows = pl.ds((J % 4) * 8, 8)
        for m in range(4):
            even, odd = got[2 * m, rows, :], got[2 * m + 1, rows, :]
            if J < 4:
                odd = rolled(odd, 64, 1)
            else:
                even = rolled(even, 64, 1)
            value = jnp.where(lane < 64, even, odd)
            for d in (2 * m, 2 * m + 1):
                start = 64 * (d % 2)
                left = jnp.logical_and(lane >= start, lane < start + 3)
                right = jnp.logical_and(lane >= start + 61, lane < start + 64)
                value = jnp.where(left, rolled(done[J], start - 10 * d, 1), value)
                value = jnp.where(right, rolled(done[J], start + 54 - 10 * d, 1), value)
            tmp[m, pl.ds(J, 8, stride=8), :] = value
    for m in range(4):
        cor_out[:, pl.ds(m * NI, NI)] = tmp[m]
    res_out[...] = res_tmp[:, :64]


def field_kernel(fluxes, yg, ya, yb, field):
    for j in range(NJ):
        place = pl.ds(j * NK, NK)
        field[pl.ds(j, NK, stride=NJ), :] = yg[place, :] - ya[place, :] * fluxes[0] + yb[place, :] * fluxes[1]


def spread(value, axis, count):
    many = jnp.broadcast_to(value[None], (count,) + value.shape)
    return lax.all_to_all(many, axis, split_axis=0, concat_axis=0, tiled=True)


def other_core(value):
    return lax.ppermute(value, "gy", [(n, n ^ 1) for n in range(GY)])


def spread_by_core(value):
    groups = [list(range(0, GY, 2)), list(range(1, GY, 2))]
    many = jnp.broadcast_to(value[None], (CHIPS,) + value.shape)
    return lax.all_to_all(many, "gy", split_axis=0, concat_axis=0, tiled=True, axis_index_groups=groups)


def swap(near, far):
    pairs = [(n, n ^ 1) for n in range(GY)]
    others = [(n, (n + 1) % GY if n % 2 else (n - 1) % GY) for n in range(GY)]
    return lax.ppermute(near, "gy", pairs), lax.ppermute(far, "gy", others)


def body(forcing, pressure_in, x_coupling, y_coupling, z_coupling, damping):
    args = (forcing, pressure_in, x_coupling, y_coupling, z_coupling, damping)
    whole = sds(ROWS, NI)
    kept = sds((2 * len(STEPS) + 1) * ROWS, NI)
    xs, near, far, coef = call(
        first_kernel,
        [sds(6 * ROWS, NI), sds(80, NI), sds(80, NI), sds(128, NI)],
        *[v.reshape(ROWS, NI) for v in args],
        scratch=[(128, NI)],
        hbm=6,
        sems=6,
    )
    near, far = swap(near, far)
    g, a, b, mult, packed = call(x_first_kernel, [whole, whole, whole, kept, sds(NJ, NI)], xs, flops=10**8)
    below, g, a, b, mult, send, ext = call(
        x_rim_kernel,
        [sds(NK, NI), whole, whole, whole, kept, sds(NJ + 32, NI), sds(4 * 96, NI)],
        xs, near, far, coef, packed, g, a, b, mult,
        aliases={5: 1, 6: 2, 7: 3, 8: 4},
    )
    got_coef = got = spread(send, "gx", GX)
    yg, ya, yb, yw, yinv, xred, cl, send = call(
        y_first_kernel,
        [whole] * 5 + [sds(3 * GX, NJ, NI), sds(NJ, NI), sds(5 * NK, NI)],
        xs, got, g, a, b,
        scratch=[(GX + 1, NJ, NI), (GX + 1, NJ, NI), (ROWS, NI), (ROWS, NI), (ROWS, NI)],
    )
    theirs = other_core(send)
    own, ends = call(coarse_matrix_kernel, [sds(7, 96, NI)] * 2, ext, got_coef, flops=10**7)
    send, joint, inner = call(
        join_first_kernel, [sds(5 * NK, NI), sds(5, NK, NI), sds(NK, NI)], ends, send, theirs
    )
    got = spread_by_core(send)
    g, yred, send = call(
        x_again_kernel,
        [whole, sds(3 * CHIPS, NK, NI), sds(8, NI)],
        xs, below, got, joint, inner, yg, ya, yb, mult,
        scratch=[(CHIPS + 1, NK, NI), (ROWS, NI), (ROWS, NI)],
    )
    got = spread(send, "gx", GX)
    yg, send = call(
        y_again_kernel,
        [whole, sds(2 * NK, NI)],
        xs, got, g, a, b, xred, cl, yw, yinv,
        scratch=[(GX + 1, NJ, NI), (ROWS, NI), (ROWS, NI)],
    )
    send, inner = call(join_again_kernel, [sds(2 * NK, NI), sds(NK, NI)], send, other_core(send), joint)
    got = spread_by_core(send)
    fluxes, coarse, near, far = call(
        residual_kernel,
        [sds(2, NK, NI), sds(64, NI), sds(16, NI), sds(16, NI)],
        xs, below, got, joint, inner, yg, ya, yb, yred, cl,
        scratch=[(CHIPS + 1, NK, NI), (ROWS, NI), (128, NI), (ROWS, NI)],
    )
    near, far = swap(near, far)
    (field,) = call(field_kernel, [whole], fluxes, yg, ya, yb, flops=10**7)
    (send,) = call(coarse_own_kernel, [sds(48, NI)], field, near, far, coarse, own, hbm=1)
    got = spread(send, "gx", GX)
    res, cor = call(
        coarse_last_kernel, [sds(64, 64), sds(64, 4 * NI)], got, coarse, ends, scratch=[(4, 64, NI), (64, NI)]
    )
    return field.reshape(NK, NJ, NI), res.reshape(8, 8, 64), cor.reshape(8, 8, 512)


def solution(mesh):
    spec = P(None, "gy", "gx")
    return jax.shard_map(
        body, mesh=mesh, in_specs=(spec,) * 6, out_specs=(spec, spec, P(None, "gy", None)), check_vma=False
    )
```

```python
import functools

import jax
import jax.numpy as jnp
from jax import lax
from jax.experimental import pallas as pl
from jax.experimental.pallas import tpu as pltpu
from jax.sharding import PartitionSpec as P

RELAX = 0.8
NK, NJ, NI = 16, 16, 128
ROWS = NK * NJ
GX, GY = 8, 16
CHIPS = GY // 2
STEPS = (1, 2, 4, 8, 16, 32, 64)
F32 = jnp.float32


def sds(*shape):
    return jax.ShapeDtypeStruct(shape, F32)


def call(kernel, outs, *args, scratch=(), hbm=0, aliases={}, sems=0, flops=None):
    spec = pl.BlockSpec(memory_space=pltpu.VMEM)
    outside = pl.BlockSpec(memory_space=pltpu.HBM)
    args = [pltpu.with_memory_space_constraint(v, pltpu.HBM) for v in args[:hbm]] + list(args[hbm:])
    shapes = [pltpu.VMEM(v, F32) for v in scratch]
    if sems:
        shapes.append(pltpu.SemaphoreType.DMA((sems,)))
    cost = None if flops is None else pl.CostEstimate(flops=flops, bytes_accessed=1 << 20, transcendentals=0)
    return pl.pallas_call(
        kernel,
        out_shape=outs,
        in_specs=[outside] * hbm + [spec] * (len(args) - hbm),
        out_specs=[spec] * len(outs),
        scratch_shapes=shapes,
        input_output_aliases=aliases,
        cost_estimate=cost,
        compiler_params=pltpu.CompilerParams(vmem_limit_bytes=16 * 1024 * 1024),
    )(*args)


def parts(xs):
    return [xs.at[pl.ds(n * ROWS, ROWS), :] for n in range(6)]


def lanes(rows, width=NI):
    return lax.broadcasted_iota(jnp.int32, (rows, width), 1)


def rolled(value, amount, axis):
    return pltpu.roll(value, amount % value.shape[axis], axis)


def level(ref, k):
    return ref[pl.ds(k * NJ, NJ), :]


def across(ref, j, count=NK, stride=NJ):
    return ref[pl.ds(j, count, stride=stride), :]


def column(value, k):
    return jnp.broadcast_to(value[:, k : k + 1], (value.shape[0], NI))


def z_pair(zc, k):
    return (level(zc, k - 1) if k > 0 else None, level(zc, k) if k < NK - 1 else None)


def z_sum(zc, k, base):
    low, top = z_pair(zc, k)
    if low is not None:
        base = base + low
    if top is not None:
        base = base + top
    return base


def z_terms(zc, field, k, base):
    low, top = z_pair(zc, k)
    if low is not None:
        base = base + low * level(field, k - 1)
    if top is not None:
        base = base + top * level(field, k + 1)
    return base


def y_left_of(yc, halo, k):
    row = lax.broadcasted_iota(jnp.int32, (NJ, NI), 0)
    return jnp.where(row == 0, halo[pl.ds(k, 1), :], rolled(level(yc, k), 1, 0))


def exact_dot(values, matrix):
    matrix = matrix.astype(jnp.bfloat16)
    total = None
    for _ in range(3):
        piece = values.astype(jnp.bfloat16)
        values = values - piece.astype(F32)
        part = jnp.dot(piece, matrix, preferred_element_type=F32)
        total = part if total is None else total + part
    return total


def squeeze(values, scale=0.125, start=0):
    source = lax.broadcasted_iota(jnp.int32, (NI, NI), 0)
    target = lax.broadcasted_iota(jnp.int32, (NI, NI), 1)
    matrix = jnp.where(source // 2 + start == target, scale, 0.0).astype(F32)
    return exact_dot(values, matrix)


def edges(values, scale=0.125):
    source = lax.broadcasted_iota(jnp.int32, (NI, NI), 0)
    target = lax.broadcasted_iota(jnp.int32, (NI, NI), 1)
    hit = ((source == NI - 1) & (target == 64)) | ((source == 0) & (target == NI - 1))
    matrix = jnp.where(hit, scale, 0.0).astype(F32)
    return exact_dot(values, matrix)


def store_coarse(out, base, tmp):
    for J in range(NJ // 2):
        out[pl.ds(base + J * 8, 8), :] = across(tmp, 2 * J, 8) + across(tmp, 2 * J + 1, 8)


def first_kernel(fh, ph, xh, yh, zh, dh, xs, near, far, coarse, tmp, sems):
    copies = [
        pltpu.make_async_copy(ref, xs.at[pl.ds(n * ROWS, ROWS), :], sems.at[n])
        for n, ref in enumerate((fh, ph, xh, yh, zh, dh))
    ]
    for copy in copies:
        copy.start()
    for copy in copies[1:]:
        copy.wait()
    f, p, xc, yc, zc, dp = parts(xs)
    odd = lax.rem(lax.axis_index("gy"), 2) == 1
    for q, two in enumerate(((xc, yc), (zc, dp))):
        total = jnp.zeros((128, NI), F32)
        for half, ref in enumerate(two):
            pairs = jnp.concatenate([level(ref, 2 * K) + level(ref, 2 * K + 1) for K in range(NK // 2)], axis=0)
            total = total + squeeze(pairs, start=64 * half)
        tmp[...] = total
        store_coarse(coarse, q * 64, tmp)

    def put(place, up, down):
        near[place, :] = jnp.where(odd, down, up)
        far[place, :] = jnp.where(odd, up, down)

    put(pl.ds(0, NK), across(p, NJ - 1), across(p, 0))
    put(pl.ds(NK, NK), across(yc, NJ - 1), across(yc, 0))
    for q in range(2):
        put(pl.ds(2 * NK + q * 24, 24), coarse[pl.ds(q * 64 + 40, 24), :], coarse[pl.ds(q * 64, 24), :])
    copies[0].wait()


def sorted_out(near, far, place):
    e = lax.axis_index("gy")
    odd = lax.rem(e, 2) == 1
    one, two = near[place, :], far[place, :]
    return (
        jnp.where(e == 0, 0.0, jnp.where(odd, one, two)),
        jnp.where(e == GY - 1, 0.0, jnp.where(odd, two, one)),
    )


def x_matrix(x, rest):
    d = lax.axis_index("gx")
    lane = lanes(x.shape[0])
    inner = jnp.logical_or(lane < NI - 1, d == GX - 1)
    diag = jnp.where(lane == 0, 0.0, rolled(x, 1, 1)) + jnp.where(inner, x, 0.0) + rest
    return diag, jnp.where(lane == NI - 1, 0.0, -x)


def x_eliminate(diag, off, rhs, keep):
    wide = lanes(diag.shape[0])
    ends = jnp.where(jnp.logical_or(wide == 0, wide == NI - 1), 1.0, 0.0).astype(F32)
    for n, s in enumerate(STEPS):
        inv = 1.0 / diag
        low = rolled(off, s, 1)
        alpha = -low * rolled(inv, s, 1)
        beta = -off * rolled(inv, -s, 1)
        keep(2 * n, alpha)
        keep(2 * n + 1, beta)
        diag = diag + alpha * low + beta * off
        rhs = rhs + alpha * rolled(rhs, s, 1) + beta * rolled(rhs, -s, 1)
        if s < NI // 2:
            off = beta * rolled(off, -s, 1)
            ends = ends + alpha * rolled(ends, s, 1) + beta * rolled(ends, -s, 1)
    inv = 1.0 / diag
    keep(2 * len(STEPS), inv)
    other = rolled(ends, NI // 2, 1)
    left = jnp.where(wide < NI // 2, ends, alpha * other)
    right = jnp.where(wide < NI // 2, beta * other, ends)
    return rhs * inv, left * inv, right * inv


def x_picks(g, a, b, x):
    return column(g, 0), column(g, NI - 1), column(a, 0), column(b, 0), column(b, NI - 1), column(x, NI - 1)


def x_first_kernel(xs, order, g, a, b, mult, packed_out):
    f, p, xc, yc, zc, dp = parts(xs)
    lane = lanes(NJ)
    row = lax.broadcasted_iota(jnp.int32, (NJ, NI), 0)
    packed = jnp.zeros((NJ, NI), F32)
    group = 8
    for k0 in range(0, NK, group):
        diag, off, rhs = [], [], []
        for k in range(k0, k0 + group):
            y, v = level(yc, k), level(p, k)
            y_left = jnp.where(row == 0, 0.0, rolled(y, 1, 0))
            matrix = x_matrix(level(xc, k), z_sum(zc, k, y_left + y + level(dp, k)))
            diag.append(matrix[0])
            off.append(matrix[1])
            after = jnp.where(row == NJ - 1, 0.0, rolled(v, -1, 0))
            rhs.append(z_terms(zc, p, k, level(f, k) + y_left * rolled(v, 1, 0) + y * after))
        diag, off, rhs = (jnp.concatenate(v, axis=0) for v in (diag, off, rhs))
        place = pl.ds(k0 * NJ, group * NJ)

        def keep(n, value):
            mult[pl.ds(n * ROWS + k0 * NJ, group * NJ), :] = value

        rhs, left, right = x_eliminate(diag, off, rhs, keep)
        g[place, :], a[place, :], b[place, :] = rhs, left, right
        for k in range(k0, k0 + group):
            part = slice((k - k0) * NJ, (k - k0 + 1) * NJ)
            for q, pick in enumerate(x_picks(rhs[part], left[part], right[part], level(xc, k))):
                packed = jnp.where(lane == q * NK + k, pick, packed)
    packed_out[...] = packed


def x_rim_kernel(xs, near, far, coarse, packed, g_in, a_in, b_in, mult_in, below, g, a, b, mult, send, ext):
    f, p, xc, yc, zc, dp = parts(xs)
    lane = lanes(NK)
    row = lax.broadcasted_iota(jnp.int32, (NK, NI), 0)

    def lifted(j):
        z, v = across(zc, j), across(p, j)
        top = jnp.where(row == NK - 1, 0.0, z)
        low = rolled(top, 1, 0)
        return low, top, low * rolled(v, 1, 0) + top * rolled(v, -1, 0)

    p_below, p_above = sorted_out(near, far, pl.ds(0, NK))
    y_left, _ = sorted_out(near, far, pl.ds(NK, NK))
    below[...] = y_left
    low, top, z_part = lifted(0)
    y = across(yc, 0)
    diag, off = x_matrix(across(xc, 0), low + top + y + y_left + across(dp, 0))
    rhs = across(f, 0) + y_left * p_below + y * across(p, 1) + z_part

    def keep(n, value):
        mult[pl.ds(n * ROWS, NK, stride=NJ), :] = value

    rhs, left, right = x_eliminate(diag, off, rhs, keep)
    first = pl.ds(0, NK, stride=NJ)
    g[first, :], a[first, :], b[first, :] = rhs, left, right
    line = jnp.zeros((NK, NI), F32)
    for q, pick in enumerate(x_picks(rhs, left, right, across(xc, 0))):
        line = line + jnp.where(lane == q * NK + row, pick, 0.0)
    line = jnp.sum(line, axis=0, keepdims=True)

    j = NJ - 1
    _, _, z_part = lifted(j)
    y = across(yc, j)
    rhs = across(f, j) + across(yc, j - 1) * across(p, j - 1) + y * p_above + z_part
    rhs = x_second_solve(rhs, lambda n: mult_in[pl.ds(n * ROWS + j, NK, stride=NJ), :])
    g[pl.ds(j, NK, stride=NJ), :] = rhs
    last = jnp.where(lane == row, column(rhs, 0), 0.0) + jnp.where(lane == NK + row, column(rhs, NI - 1), 0.0)
    last = jnp.sum(last, axis=0, keepdims=True)
    was = packed[...]
    was = jnp.where(row == 0, line, was)
    send[pl.ds(0, NJ), :] = jnp.where(jnp.logical_and(row == NJ - 1, lane < 2 * NK), last, was)
    coarse_share(near, far, coarse, send, ext)


def coarse_share(near, far, coarse, send, ext):
    wide = lanes(8)
    level_k = lax.broadcasted_iota(jnp.int32, (8, NI), 0)
    fields = [[], [], [], []]
    for q in range(2):
        lower, upper = sorted_out(near, far, pl.ds(2 * NK + q * 24, 24))
        rows = [lower[n * 8 : n * 8 + 8] for n in range(3)]
        rows += [coarse[pl.ds(q * 64 + n * 8, 8), :] for n in range(8)]
        rows += [upper[n * 8 : n * 8 + 8] for n in range(2)]
        for row in rows:
            fields[2 * q].append(jnp.where(wide < 64, row, 0.0))
            fields[2 * q + 1].append(jnp.where(wide < 64, rolled(row, 64, 1), 0.0))
    xs_, ys_, zs_, damps = fields
    shares = [jnp.zeros((8, NI), F32)] * 4
    for J in range(12):
        top = jnp.where(level_k == 7, 0.0, zs_[J + 1])
        rest = damps[J + 1] + ys_[J + 1] + ys_[J] + top + rolled(top, 1, 0) + xs_[J + 1] + rolled(xs_[J + 1], 1, 1)
        for n, value in enumerate((xs_[J + 1], ys_[J + 1], top, rest)):
            ext[pl.ds(n * 96 + J * 8, 8), :] = value
            at = 10 * J
            first, last = rolled(value, at, 1), rolled(value, at + 5 - 59, 1)
            share = jnp.where(jnp.logical_and(wide >= at, wide < at + 5), first, shares[n])
            shares[n] = jnp.where(jnp.logical_and(wide >= at + 5, wide < at + 10), last, share)
    for n in range(4):
        send[pl.ds(NJ + n * 8, 8), :] = shares[n]


def x_second_solve(rhs, kept):
    for n, s in enumerate(STEPS):
        rhs = rhs + kept(2 * n) * rolled(rhs, s, 1) + kept(2 * n + 1) * rolled(rhs, -s, 1)
    return rhs * kept(2 * len(STEPS))


def x_fluxes(fs, source, low, inv, up):
    zero = jnp.zeros((NJ, NI), F32)
    fs[0], fs[GX] = zero, zero
    forward = [source(0)]
    for d in range(1, GX - 1):
        forward.append(source(d) + low[d] * forward[-1])
    value = forward[-1] * inv[GX - 2]
    fs[GX - 1] = value
    for d in range(GX - 3, -1, -1):
        value = forward[d] * inv[d] + up[d] * value
        fs[1 + d] = value


def x_finish(fs, g, a, b, field):
    d = lax.axis_index("gx")
    flux_left, flux_right = fs[d], fs[d + 1]
    for k in range(NK):
        field[pl.ds(k * NJ, NJ), :] = (
            level(g, k) - level(a, k) * column(flux_left, k) + level(b, k) * column(flux_right, k)
        )
    return flux_left, flux_right


def y_source(f, xc, zc, field, fluxes, c_left, k):
    d = lax.axis_index("gx")
    lane = lanes(NJ)
    flux_left, flux_right = fluxes
    v, x = level(field, k), level(xc, k)
    before = jnp.where(lane == 0, column(c_left, k) * v - column(flux_left, k), rolled(x * v, 1, 1))
    last = jnp.where(d == GX - 1, 0.0, x * v + column(flux_right, k))
    after = jnp.where(lane == NI - 1, last, x * rolled(v, -1, 1))
    return z_terms(zc, field, k, level(f, k) + before + after)


def y_first_kernel(xs, got, g, a, b, yg, ya, yb, yw, yinv, xred, cl, send, fs, cs, field, src, base):
    f, p, xc, yc, zc, dp = parts(xs)
    d = lax.axis_index("gx")
    e = lax.axis_index("gy")
    lane = lanes(NJ)
    part = lambda n, q: rolled(got[n, pl.ds(0, NJ), :], -NK * q, 1)
    m = [part(n, 3) for n in range(GX)]
    low, inv, up = [None], [], []
    for n in range(GX - 1):
        dd = part(n, 4) + 1.0 / part(n, 5) + part(n + 1, 2)
        if n:
            low.append(m[n] * inv[-1])
            dd = dd - low[n] * m[n]
        inv.append(1.0 / dd)
        up.append(m[n + 1] * inv[n])
        xred[n], xred[GX + n], xred[2 * GX + n] = (low[n] if n else jnp.zeros_like(dd)), inv[n], up[n]
    x_fluxes(fs, lambda n: part(n + 1, 0) - part(n, 1), low, inv, up)
    cs[0] = jnp.zeros((NJ, NI), F32)
    for n in range(GX):
        cs[n + 1] = part(n, 5)
    c_left = cs[d]
    cl[...] = c_left
    fluxes = x_finish(fs, g, a, b, field)
    for k in range(NK):
        src[pl.ds(k * NJ, NJ), :] = y_source(f, xc, zc, field, fluxes, c_left, k)
        x = level(xc, k)
        x_left = jnp.where(lane == 0, column(c_left, k), rolled(x, 1, 1))
        base[pl.ds(k * NJ, NJ), :] = z_sum(zc, k, x_left + x + level(dp, k))
    ys, ws, invs, spike = [], [None], [], []
    for j in range(NJ):
        y = across(yc, j)
        diag = across(base, j)
        if j < NJ - 1:
            diag = diag + y
        else:
            diag = diag + jnp.where(e == GY - 1, y, 0.0)
        rhs = across(src, j)
        if j:
            y_before = across(yc, j - 1)
            w = y_before * invs[-1]
            ws.append(w)
            diag = diag + y_before - w * y_before
            rhs = rhs + w * ys[-1]
            spike.append(w * spike[-1])
            yw[pl.ds(j * NK, NK), :] = w
        else:
            spike.append(jnp.ones((NK, NI), F32))
            yw[pl.ds(0, NK), :] = jnp.zeros((NK, NI), F32)
        ys.append(rhs)
        invs.append(1.0 / diag)
        yinv[pl.ds(j * NK, NK), :] = invs[-1]
    for j in range(NJ - 1, -1, -1):
        if j == NJ - 1:
            gv, av, bv = ys[j] * invs[j], spike[j] * invs[j], invs[j]
            send[pl.ds(NK, NK), :] = gv
            send[pl.ds(4 * NK, NK), :] = bv + 1.0 / across(yc, j)
        else:
            w = ws[j + 1]
            gv, av, bv = ys[j] * invs[j] + w * gv, spike[j] * invs[j] + w * av, w * bv
        place = pl.ds(j * NK, NK)
        yg[place, :], ya[place, :], yb[place, :] = gv, av, bv
    send[pl.ds(0, NK), :] = gv
    send[pl.ds(2 * NK, NK), :] = av
    send[pl.ds(3 * NK, NK), :] = bv


def y_fluxes(fs, source, low, inv, up):
    zero = jnp.zeros((NK, NI), F32)
    fs[0], fs[CHIPS] = zero, zero
    forward = [source(0)]
    for n in range(1, CHIPS - 1):
        forward.append(source(n) + low(n) * forward[-1])
    value = forward[-1] * inv(CHIPS - 2)
    fs[CHIPS - 1] = value
    for n in range(CHIPS - 3, -1, -1):
        value = forward[n] * inv(n) + up(n) * value
        fs[1 + n] = value


def own_fluxes(fs, joint, inner):
    e = lax.axis_index("gy")
    outer_left, outer_right = fs[e // 2], fs[e // 2 + 1]
    between = inner[...] + joint[1] * outer_left + joint[2] * outer_right
    odd = lax.rem(e, 2) == 1
    return jnp.where(odd, between, outer_left), jnp.where(odd, outer_right, between)


def join_first_kernel(order, mine, theirs, send, joint, inner):
    odd = lax.rem(lax.axis_index("gy"), 2) == 1
    block = lambda ref, q: ref[pl.ds(q * NK, NK), :]
    low = [jnp.where(odd, block(theirs, q), block(mine, q)) for q in range(5)]
    high = [jnp.where(odd, block(mine, q), block(theirs, q)) for q in range(5)]
    inv = 1.0 / (low[4] + high[2])
    from_low, from_high = low[3] * inv, high[3] * inv
    base = (high[0] - low[1]) * inv
    values = (
        low[0] + low[3] * base,
        high[1] - high[3] * base,
        low[2] - low[3] * from_low,
        low[3] * from_high,
        high[4] - high[3] * from_high,
    )
    for q, value in enumerate(values):
        send[pl.ds(q * NK, NK), :] = value
    for n, value in enumerate((inv, from_low, from_high, low[3], high[3])):
        joint[n] = value
    inner[...] = base


def join_again_kernel(mine, theirs, joint, send, inner):
    odd = lax.rem(lax.axis_index("gy"), 2) == 1
    block = lambda ref, q: ref[pl.ds(q * NK, NK), :]
    low = [jnp.where(odd, block(theirs, q), block(mine, q)) for q in range(2)]
    high = [jnp.where(odd, block(mine, q), block(theirs, q)) for q in range(2)]
    base = (high[0] - low[1]) * joint[0]
    send[pl.ds(0, NK), :] = low[0] + joint[3] * base
    send[pl.ds(NK, NK), :] = high[1] - joint[4] * base
    inner[...] = base


def y_finish(fluxes, yc, below, yg, ya, yb, field, terms):
    e = lax.axis_index("gy")
    flux_left, flux_right = fluxes
    block = lambda ref, j: ref[pl.ds(j * NK, NK), :]
    p = [block(yg, j) - block(ya, j) * flux_left + block(yb, j) * flux_right for j in range(NJ)]
    for j in range(NJ):
        y = across(yc, j)
        if j:
            before = across(yc, j - 1) * p[j - 1]
        else:
            before = below[pl.ds(0, NK), :] * p[0] - flux_left
        if j < NJ - 1:
            after = y * p[j + 1]
        else:
            after = jnp.where(e == GY - 1, 0.0, y * p[j] + flux_right)
        field[pl.ds(j, NK, stride=NJ), :] = p[j]
        terms[pl.ds(j, NK, stride=NJ), :] = before + after


def x_again_kernel(xs, below, got, joint, inner, yg, ya, yb, mult, g, yred, send, fs, field, terms):
    f, p, xc, yc, zc, dp = parts(xs)
    part = lambda n, q: got[n, pl.ds(q * NK, NK), :]
    prev = None
    for n in range(CHIPS - 1):
        dd = part(n, 4) + part(n + 1, 2)
        if n:
            m = part(n, 3)
            low = m * prev
            dd = dd - low * m
            yred[n] = low
        else:
            yred[n] = jnp.zeros_like(dd)
        prev = 1.0 / dd
        yred[CHIPS + n] = prev
        yred[2 * CHIPS + n] = part(n + 1, 3) * prev
    for n in range(1, 4):
        yred[n * CHIPS - 1] = jnp.zeros((NK, NI), F32)
    y_fluxes(
        fs,
        lambda n: part(n + 1, 0) - part(n, 1),
        lambda n: yred[n],
        lambda n: yred[CHIPS + n],
        lambda n: yred[2 * CHIPS + n],
    )
    y_finish(own_fluxes(fs, joint, inner), yc, below, yg, ya, yb, field, terms)
    lane = lanes(NJ)
    packed = jnp.zeros((NJ, NI), F32)
    group = 2
    for k0 in range(0, NK, group):
        rhs = jnp.concatenate(
            [z_terms(zc, field, k, level(f, k) + level(terms, k)) for k in range(k0, k0 + group)], axis=0
        )
        place = pl.ds(k0 * NJ, group * NJ)
        rhs = x_second_solve(rhs, lambda n: mult[pl.ds(n * ROWS + k0 * NJ, group * NJ), :])
        g[place, :] = rhs
        for k in range(k0, k0 + group):
            mine = rhs[(k - k0) * NJ : (k - k0 + 1) * NJ]
            packed = jnp.where(lane == k, column(mine, 0), packed)
            packed = jnp.where(lane == NK + k, column(mine, NI - 1), packed)
    send[...] = jnp.where(lanes(8) < 2 * NK, packed[:8], rolled(packed[8:], 2 * NK, 1))


def y_again_kernel(xs, got, g, a, b, xred, cl, yw, yinv, yg, send, fs, field, src):
    f, p, xc, yc, zc, dp = parts(xs)
    part = lambda n, q: jnp.concatenate([rolled(got[n], -NK * q, 1), rolled(got[n], -NK * (q + 2), 1)], axis=0)
    x_fluxes(
        fs,
        lambda n: part(n + 1, 0) - part(n, 1),
        [xred[n] for n in range(GX - 1)],
        [xred[GX + n] for n in range(GX - 1)],
        [xred[2 * GX + n] for n in range(GX - 1)],
    )
    fluxes = x_finish(fs, g, a, b, field)
    c_left = cl[...]
    for k in range(NK):
        src[pl.ds(k * NJ, NJ), :] = y_source(f, xc, zc, field, fluxes, c_left, k)
    block = lambda ref, j: ref[pl.ds(j * NK, NK), :]
    ys = []
    for j in range(NJ):
        rhs = across(src, j)
        if j:
            rhs = rhs + block(yw, j) * ys[-1]
        ys.append(rhs)
    value = None
    for j in range(NJ - 1, -1, -1):
        new = ys[j] * block(yinv, j)
        value = new if value is None else new + block(yw, j + 1) * value
        yg[pl.ds(j * NK, NK), :] = value
        if j == NJ - 1:
            send[pl.ds(NK, NK), :] = value
    send[pl.ds(0, NK), :] = value


def residual_kernel(xs, below, got, joint, inner, yg, ya, yb, yred, cl, fluxes, coarse, near, far, fs, terms, tmp, field):
    f, p, xc, yc, zc, dp = parts(xs)
    d = lax.axis_index("gx")
    lane = lanes(NJ)
    part = lambda n, q: got[n, pl.ds(q * NK, NK), :]
    y_fluxes(
        fs,
        lambda n: part(n + 1, 0) - part(n, 1),
        lambda n: yred[n],
        lambda n: yred[CHIPS + n],
        lambda n: yred[2 * CHIPS + n],
    )
    e = lax.axis_index("gy")
    ends = own_fluxes(fs, joint, inner)
    fluxes[0], fluxes[1] = ends
    y_finish(ends, yc, below, yg, ya, yb, field, terms)
    c_left = cl[...]
    main, rim = [], []
    for k in range(NK):
        v, x = level(field, k), level(xc, k)
        left = column(c_left, k)
        x_left = jnp.where(lane == 0, left, rolled(x, 1, 1))
        diag = z_sum(zc, k, x_left + x + y_left_of(yc, below, k) + level(yc, k) + level(dp, k))
        around = jnp.where(lane == 0, 0.0, x_left * rolled(v, 1, 1)) + jnp.where(lane == NI - 1, 0.0, x * rolled(v, -1, 1))
        main.append(level(f, k) - (diag * v - around - level(terms, k) - z_terms(zc, field, k, jnp.zeros((NJ, NI), F32))))
        last = jnp.where(d == GX - 1, 0.0, x * v)
        rim.append(jnp.where(lane == 0, left * v, jnp.where(lane == NI - 1, last, 0.0)))
    pairs = jnp.concatenate([main[2 * K] + main[2 * K + 1] for K in range(NK // 2)], axis=0)
    outer = jnp.concatenate([rim[2 * K] + rim[2 * K + 1] for K in range(NK // 2)], axis=0)
    tmp[...] = squeeze(pairs) + edges(outer)
    store_coarse(coarse, 0, tmp)
    odd = lax.rem(e, 2) == 1
    up, down = coarse[pl.ds(48, 16), :], coarse[pl.ds(0, 16), :]
    near[...] = jnp.where(odd, down, up)
    far[...] = jnp.where(odd, up, down)


def eight(ref, J):
    return ref[pl.ds(J * 8, 8), :]


def coarse_matrix_kernel(ext, got, *outs):
    e = lax.axis_index("gy")
    lane = lanes(8)
    source = lax.broadcasted_iota(jnp.int32, (NI, 4 * NI), 0)
    target = lax.broadcasted_iota(jnp.int32, (NI, 4 * NI), 1)
    device, at_column = target >> 6, target & 63
    hit = jnp.logical_and(at_column < 3, source == 10 * device + at_column)
    hit = jnp.logical_or(hit, jnp.logical_and(at_column > 60, source == 10 * device + at_column - 54))
    outs[2][...] = jnp.where(hit, 1.0, 0.0).astype(jnp.bfloat16)

    def joint(n, J):
        value = jnp.zeros((8, NI), F32)
        for d in range(GX):
            moved = rolled(got[d, pl.ds(NJ + n * 8, 8), :], 10 * (d - J), 1)
            value = jnp.where(jnp.logical_and(lane >= 10 * d, lane < 10 * d + 10), moved, value)
        return value

    own = lambda n, J: ext[pl.ds(n * 96 + J * 8, 8), :]
    first = jnp.logical_and(lax.rem(lane, 10) == 0, lane > 0)
    for out, source, width in ((outs[0], own, 64), (outs[1], joint, 10 * GX)):
        y_before = jnp.zeros((8, NI), F32)
        for J in range(12):
            x, y, z_top, rest = (source(n, J) for n in range(4))
            x_left = rolled(x, 1, 1)
            at = e * 8 + J - 2
            valid = jnp.logical_and(jnp.logical_and(at >= 0, at < 8 * GY), lane < width)
            if width != 64:
                rest = rest + jnp.where(first, x_left, 0.0)
            weight = jnp.where(valid, RELAX / jnp.where(valid, rest, 1.0), 0.0)
            couplings = (x_left, x, y_before, y, rolled(z_top, 1, 0), z_top)
            for n, value in enumerate((weight, *(weight * c for c in couplings))):
                out[n, pl.ds(J * 8, 8), :] = value
            y_before = y


def relaxed(res, matrix):
    at = lambda n, J: matrix[n, pl.ds(J * 8, 8), :]

    def around(v, J):
        return (
            at(1, J) * rolled(v[J], 1, 1)
            + at(2, J) * rolled(v[J], -1, 1)
            + at(3, J) * v[J - 1]
            + at(4, J) * v[J + 1]
            + at(5, J) * rolled(v[J], 1, 0)
            + at(6, J) * rolled(v[J], -1, 0)
        )

    first = {J: at(0, J) * res[J] for J in range(12)}
    second = {J: (2.0 - RELAX) * first[J] + around(first, J) for J in range(1, 11)}
    return [first[J] + (1.0 - RELAX) * second[J] + around(second, J) for J in range(2, 10)]


def coarse_own_kernel(order, near, far, coarse, matrix, send):
    lane = lanes(8)
    lower, upper = sorted_out(near, far, pl.ds(0, 16))
    res = [lower[:8], lower[8:], *(eight(coarse, J) for J in range(8)), upper[:8], upper[8:]]
    done = relaxed(res, matrix)
    d = lax.axis_index("gx")
    odd = lax.rem(d, 2) == 1
    for t in range(4):
        both = jnp.where(lane < 64, done[t], rolled(done[t + 4], 64, 1))
        send[pl.ds(t * 8, 8), :] = jnp.where(odd, rolled(both, 64, 1), both)
    strips = [jnp.zeros((8, NI), F32)] * 2
    for J in range(12):
        at = 16 * (J % 8)
        strip = jnp.where(jnp.logical_and(lane >= at, lane < at + 6), rolled(res[J], at + 1, 1), strips[J // 8])
        strips[J // 8] = jnp.where(jnp.logical_and(lane >= at + 6, lane < at + 12), rolled(res[J], at + 6 - 59, 1), strip)
    turn = lax.rem(10 * d + NI - 1, NI)
    send[pl.ds(32, 8), :] = pltpu.roll(strips[0], turn, 1)
    send[pl.ds(40, 8), :] = pltpu.roll(strips[1], turn, 1)


def coarse_last_kernel(got, coarse, matrix, places, res_out, cor_out, tmp, res_tmp):
    d_own = lax.axis_index("gx")
    lane = lanes(8)
    joint = []
    for J in range(12):
        value = jnp.zeros((8, NI), F32)
        at = (lane - 16 * (J % 8)) & (NI - 1)
        for d in range(GX):
            strip = got[d, pl.ds(32 + 8 * (J // 8), 8), :]
            value = value + jnp.where(jnp.logical_and(at >= 10 * d - 1, at < 10 * d + 11), strip, 0.0)
        joint.append(rolled(value, -16 * (J % 8), 1))
    done = jnp.concatenate(relaxed(joint, matrix), axis=0)
    placed = exact_dot(done, places[...])
    end = jnp.logical_or((lane & 63) < 3, (lane & 63) > 60)
    turn = lax.rem(NI - 10 * d_own, NI)
    for J in range(8):
        mine = pltpu.roll(joint[J + 2], turn, 1)
        mine = jnp.where(lane == 0, mine, jnp.where(lane == 63, rolled(mine, 54, 1), eight(coarse, J)))
        res_tmp[pl.ds(J, 8, stride=8), :] = mine
        rows = pl.ds((J % 4) * 8, 8)
        for m in range(4):
            even, odd = got[2 * m, rows, :], got[2 * m + 1, rows, :]
            if J < 4:
                value = jnp.where(lane < 64, even, odd)
            else:
                value = rolled(jnp.where(lane < 64, odd, even), 64, 1)
            right = placed[J * 8 : J * 8 + 8, m * NI : (m + 1) * NI]
            tmp[m, pl.ds(J, 8, stride=8), :] = jnp.where(end, right, value)
    for m in range(4):
        cor_out[:, pl.ds(m * NI, NI)] = tmp[m]
    res_out[...] = res_tmp[:, :64]


def field_kernel(order, fluxes, yg, ya, yb, field):
    for j in range(NJ):
        place = pl.ds(j * NK, NK)
        field[pl.ds(j, NK, stride=NJ), :] = yg[place, :] - ya[place, :] * fluxes[0] + yb[place, :] * fluxes[1]


def spread(value, axis, count):
    many = jnp.broadcast_to(value[None], (count,) + value.shape)
    return lax.all_to_all(many, axis, split_axis=0, concat_axis=0, tiled=True)


def other_core(value):
    return lax.ppermute(value, "gy", [(n, n ^ 1) for n in range(GY)])


def spread_by_core(value):
    groups = [list(range(0, GY, 2)), list(range(1, GY, 2))]
    many = jnp.broadcast_to(value[None], (CHIPS,) + value.shape)
    return lax.all_to_all(many, "gy", split_axis=0, concat_axis=0, tiled=True, axis_index_groups=groups)


def swap(near, far):
    pairs = [(n, n ^ 1) for n in range(GY)]
    others = [(n, (n + 1) % GY if n % 2 else (n - 1) % GY) for n in range(GY)]
    return lax.ppermute(near, "gy", pairs), lax.ppermute(far, "gy", others)


def body(forcing, pressure_in, x_coupling, y_coupling, z_coupling, damping):
    args = (forcing, pressure_in, x_coupling, y_coupling, z_coupling, damping)
    whole = sds(ROWS, NI)
    kept = sds((2 * len(STEPS) + 1) * ROWS, NI)
    xs, near, far, coef = call(
        first_kernel,
        [sds(6 * ROWS, NI), sds(80, NI), sds(80, NI), sds(128, NI)],
        *[v.reshape(ROWS, NI) for v in args],
        scratch=[(128, NI)],
        hbm=6,
        sems=6,
    )
    mine = near
    near, far = swap(near, far)
    g, a, b, mult, packed = call(x_first_kernel, [whole, whole, whole, kept, sds(NJ, NI)], xs, mine, flops=10**8)
    below, g, a, b, mult, send, ext = call(
        x_rim_kernel,
        [sds(NK, NI), whole, whole, whole, kept, sds(NJ + 32, NI), sds(4 * 96, NI)],
        xs, near, far, coef, packed, g, a, b, mult,
        aliases={5: 1, 6: 2, 7: 3, 8: 4},
    )
    got_coef = got = spread(send, "gx", GX)
    yg, ya, yb, yw, yinv, xred, cl, send = call(
        y_first_kernel,
        [whole] * 5 + [sds(3 * GX, NJ, NI), sds(NJ, NI), sds(5 * NK, NI)],
        xs, got, g, a, b,
        scratch=[(GX + 1, NJ, NI), (GX + 1, NJ, NI), (ROWS, NI), (ROWS, NI), (ROWS, NI)],
    )
    theirs = other_core(send)
    own, ends, places = call(
        coarse_matrix_kernel, [sds(7, 96, NI)] * 2 + [jax.ShapeDtypeStruct((NI, 4 * NI), jnp.bfloat16)], ext, got_coef, flops=10**7
    )
    send, joint, inner = call(
        join_first_kernel, [sds(5 * NK, NI), sds(5, NK, NI), sds(NK, NI)], ends, send, theirs
    )
    got = spread_by_core(send)
    g, yred, send = call(
        x_again_kernel,
        [whole, sds(3 * CHIPS, NK, NI), sds(8, NI)],
        xs, below, got, joint, inner, yg, ya, yb, mult,
        scratch=[(CHIPS + 1, NK, NI), (ROWS, NI), (ROWS, NI)],
    )
    got = spread(send, "gx", GX)
    yg, send = call(
        y_again_kernel,
        [whole, sds(2 * NK, NI)],
        xs, got, g, a, b, xred, cl, yw, yinv,
        scratch=[(GX + 1, NJ, NI), (ROWS, NI), (ROWS, NI)],
    )
    send, inner = call(join_again_kernel, [sds(2 * NK, NI), sds(NK, NI)], send, other_core(send), joint)
    got = spread_by_core(send)
    fluxes, coarse, near, far = call(
        residual_kernel,
        [sds(2, NK, NI), sds(64, NI), sds(16, NI), sds(16, NI)],
        xs, below, got, joint, inner, yg, ya, yb, yred, cl,
        scratch=[(CHIPS + 1, NK, NI), (ROWS, NI), (128, NI), (ROWS, NI)],
    )
    mine = near
    near, far = swap(near, far)
    (field,) = call(field_kernel, [whole], mine, fluxes, yg, ya, yb, flops=10**7)
    (send,) = call(coarse_own_kernel, [sds(48, NI)], field, near, far, coarse, own, hbm=1)
    got = spread(send, "gx", GX)
    res, cor = call(
        coarse_last_kernel, [sds(64, 64), sds(64, 4 * NI)], got, coarse, ends, places, scratch=[(4, 64, NI), (64, NI)]
    )
    return field.reshape(NK, NJ, NI), res.reshape(8, 8, 64), cor.reshape(8, 8, 512)


def solution(mesh):
    spec = P(None, "gy", "gx")
    return jax.shard_map(
        body, mesh=mesh, in_specs=(spec,) * 6, out_specs=(spec, spec, P(None, "gy", None)), check_vma=False
    )
```

```python
import functools

import jax
import jax.numpy as jnp
from jax import lax
from jax.experimental import pallas as pl
from jax.experimental.pallas import tpu as pltpu
from jax.sharding import PartitionSpec as P

RELAX = 0.8
NK, NJ, NI = 16, 16, 128
ROWS = NK * NJ
GX, GY = 8, 16
CHIPS = GY // 2
STEPS = (1, 2, 4, 8, 16, 32, 64)
F32 = jnp.float32


def sds(*shape):
    return jax.ShapeDtypeStruct(shape, F32)


def call(kernel, outs, *args, scratch=(), hbm=0, aliases={}, sems=0, flops=None):
    spec = pl.BlockSpec(memory_space=pltpu.VMEM)
    outside = pl.BlockSpec(memory_space=pltpu.HBM)
    args = [pltpu.with_memory_space_constraint(v, pltpu.HBM) for v in args[:hbm]] + list(args[hbm:])
    shapes = [pltpu.VMEM(v, F32) for v in scratch]
    if sems:
        shapes.append(pltpu.SemaphoreType.DMA((sems,)))
    cost = None if flops is None else pl.CostEstimate(flops=flops, bytes_accessed=1 << 20, transcendentals=0)
    return pl.pallas_call(
        kernel,
        out_shape=outs,
        in_specs=[outside] * hbm + [spec] * (len(args) - hbm),
        out_specs=[spec] * len(outs),
        scratch_shapes=shapes,
        input_output_aliases=aliases,
        cost_estimate=cost,
        compiler_params=pltpu.CompilerParams(vmem_limit_bytes=16 * 1024 * 1024),
    )(*args)


def parts(xs):
    return [xs.at[pl.ds(n * ROWS, ROWS), :] for n in range(6)]


def lanes(rows, width=NI):
    return lax.broadcasted_iota(jnp.int32, (rows, width), 1)


def rolled(value, amount, axis):
    return pltpu.roll(value, amount % value.shape[axis], axis)


def level(ref, k):
    return ref[pl.ds(k * NJ, NJ), :]


def across(ref, j, count=NK, stride=NJ):
    return ref[pl.ds(j, count, stride=stride), :]


def column(value, k):
    return jnp.broadcast_to(value[:, k : k + 1], (value.shape[0], NI))


def z_pair(zc, k):
    return (level(zc, k - 1) if k > 0 else None, level(zc, k) if k < NK - 1 else None)


def z_sum(zc, k, base):
    low, top = z_pair(zc, k)
    if low is not None:
        base = base + low
    if top is not None:
        base = base + top
    return base


def z_terms(zc, field, k, base):
    low, top = z_pair(zc, k)
    if low is not None:
        base = base + low * level(field, k - 1)
    if top is not None:
        base = base + top * level(field, k + 1)
    return base


def y_left_of(yc, halo, k):
    row = lax.broadcasted_iota(jnp.int32, (NJ, NI), 0)
    return jnp.where(row == 0, halo[pl.ds(k, 1), :], rolled(level(yc, k), 1, 0))


def exact_dot(values, matrix):
    matrix = matrix.astype(jnp.bfloat16)
    total = None
    for _ in range(3):
        piece = values.astype(jnp.bfloat16)
        values = values - piece.astype(F32)
        part = jnp.dot(piece, matrix, preferred_element_type=F32)
        total = part if total is None else total + part
    return total


def squeeze(values, scale=0.125, start=0):
    source = lax.broadcasted_iota(jnp.int32, (NI, NI), 0)
    target = lax.broadcasted_iota(jnp.int32, (NI, NI), 1)
    matrix = jnp.where(source // 2 + start == target, scale, 0.0).astype(F32)
    return exact_dot(values, matrix)


def edges(values, scale=0.125):
    source = lax.broadcasted_iota(jnp.int32, (NI, NI), 0)
    target = lax.broadcasted_iota(jnp.int32, (NI, NI), 1)
    hit = ((source == NI - 1) & (target == 64)) | ((source == 0) & (target == NI - 1))
    matrix = jnp.where(hit, scale, 0.0).astype(F32)
    return exact_dot(values, matrix)


def store_coarse(out, base, tmp):
    for J in range(NJ // 2):
        out[pl.ds(base + J * 8, 8), :] = across(tmp, 2 * J, 8) + across(tmp, 2 * J + 1, 8)


def first_kernel(fh, ph, xh, yh, zh, dh, xs, near, far, coarse, tmp, sems):
    copies = [
        pltpu.make_async_copy(ref, xs.at[pl.ds(n * ROWS, ROWS), :], sems.at[n])
        for n, ref in enumerate((fh, ph, xh, yh, zh, dh))
    ]
    for copy in copies:
        copy.start()
    for copy in copies[1:]:
        copy.wait()
    f, p, xc, yc, zc, dp = parts(xs)
    odd = lax.rem(lax.axis_index("gy"), 2) == 1
    for q, two in enumerate(((xc, yc), (zc, dp))):
        total = jnp.zeros((128, NI), F32)
        for half, ref in enumerate(two):
            pairs = jnp.concatenate([level(ref, 2 * K) + level(ref, 2 * K + 1) for K in range(NK // 2)], axis=0)
            total = total + squeeze(pairs, start=64 * half)
        tmp[...] = total
        store_coarse(coarse, q * 64, tmp)

    def put(place, up, down):
        near[place, :] = jnp.where(odd, down, up)
        far[place, :] = jnp.where(odd, up, down)

    put(pl.ds(0, NK), across(p, NJ - 1), across(p, 0))
    put(pl.ds(NK, NK), across(yc, NJ - 1), across(yc, 0))
    for q in range(2):
        put(pl.ds(2 * NK + q * 24, 24), coarse[pl.ds(q * 64 + 40, 24), :], coarse[pl.ds(q * 64, 24), :])
    copies[0].wait()


def sorted_out(near, far, place):
    e = lax.axis_index("gy")
    odd = lax.rem(e, 2) == 1
    one, two = near[place, :], far[place, :]
    return (
        jnp.where(e == 0, 0.0, jnp.where(odd, one, two)),
        jnp.where(e == GY - 1, 0.0, jnp.where(odd, two, one)),
    )


def x_matrix(x, rest):
    d = lax.axis_index("gx")
    lane = lanes(x.shape[0])
    inner = jnp.logical_or(lane < NI - 1, d == GX - 1)
    diag = jnp.where(lane == 0, 0.0, rolled(x, 1, 1)) + jnp.where(inner, x, 0.0) + rest
    return diag, jnp.where(lane == NI - 1, 0.0, -x)


def x_eliminate(diag, off, rhs, keep):
    wide = lanes(diag.shape[0])
    ends = jnp.where(jnp.logical_or(wide == 0, wide == NI - 1), 1.0, 0.0).astype(F32)
    for n, s in enumerate(STEPS):
        inv = 1.0 / diag
        low = rolled(off, s, 1)
        alpha = -low * rolled(inv, s, 1)
        beta = -off * rolled(inv, -s, 1)
        keep(2 * n, alpha)
        keep(2 * n + 1, beta)
        diag = diag + alpha * low + beta * off
        rhs = rhs + alpha * rolled(rhs, s, 1) + beta * rolled(rhs, -s, 1)
        if s < NI // 2:
            off = beta * rolled(off, -s, 1)
            ends = ends + alpha * rolled(ends, s, 1) + beta * rolled(ends, -s, 1)
    inv = 1.0 / diag
    keep(2 * len(STEPS), inv)
    other = rolled(ends, NI // 2, 1)
    left = jnp.where(wide < NI // 2, ends, alpha * other)
    right = jnp.where(wide < NI // 2, beta * other, ends)
    return rhs * inv, left * inv, right * inv


def x_picks(g, a, b, x):
    return column(g, 0), column(g, NI - 1), column(a, 0), column(b, 0), column(b, NI - 1), column(x, NI - 1)


def x_first_kernel(xs, order, g, a, b, mult, packed_out):
    f, p, xc, yc, zc, dp = parts(xs)
    lane = lanes(NJ)
    row = lax.broadcasted_iota(jnp.int32, (NJ, NI), 0)
    packed = jnp.zeros((NJ, NI), F32)
    group = 8
    for k0 in range(0, NK, group):
        diag, off, rhs = [], [], []
        for k in range(k0, k0 + group):
            y, v = level(yc, k), level(p, k)
            y_left = jnp.where(row == 0, 0.0, rolled(y, 1, 0))
            matrix = x_matrix(level(xc, k), z_sum(zc, k, y_left + y + level(dp, k)))
            diag.append(matrix[0])
            off.append(matrix[1])
            after = jnp.where(row == NJ - 1, 0.0, rolled(v, -1, 0))
            rhs.append(z_terms(zc, p, k, level(f, k) + y_left * rolled(v, 1, 0) + y * after))
        diag, off, rhs = (jnp.concatenate(v, axis=0) for v in (diag, off, rhs))
        place = pl.ds(k0 * NJ, group * NJ)

        def keep(n, value):
            mult[pl.ds(n * ROWS + k0 * NJ, group * NJ), :] = value

        rhs, left, right = x_eliminate(diag, off, rhs, keep)
        g[place, :], a[place, :], b[place, :] = rhs, left, right
        for k in range(k0, k0 + group):
            part = slice((k - k0) * NJ, (k - k0 + 1) * NJ)
            for q, pick in enumerate(x_picks(rhs[part], left[part], right[part], level(xc, k))):
                packed = jnp.where(lane == q * NK + k, pick, packed)
    packed_out[...] = packed


def x_rim_kernel(xs, near, far, coarse, packed, g_in, a_in, b_in, mult_in, below, g, a, b, mult, send, near_out, far_out, coarse_out):
    f, p, xc, yc, zc, dp = parts(xs)
    lane = lanes(NK)
    row = lax.broadcasted_iota(jnp.int32, (NK, NI), 0)

    def lifted(j):
        z, v = across(zc, j), across(p, j)
        top = jnp.where(row == NK - 1, 0.0, z)
        low = rolled(top, 1, 0)
        return low, top, low * rolled(v, 1, 0) + top * rolled(v, -1, 0)

    near_out[...] = near[pl.ds(2 * NK, 48), :]
    far_out[...] = far[pl.ds(2 * NK, 48), :]
    coarse_out[...] = coarse[...]
    p_below, p_above = sorted_out(near, far, pl.ds(0, NK))
    y_left, _ = sorted_out(near, far, pl.ds(NK, NK))
    below[...] = y_left
    low, top, z_part = lifted(0)
    y = across(yc, 0)
    diag, off = x_matrix(across(xc, 0), low + top + y + y_left + across(dp, 0))
    rhs = across(f, 0) + y_left * p_below + y * across(p, 1) + z_part

    def keep(n, value):
        mult[pl.ds(n * ROWS, NK, stride=NJ), :] = value

    rhs, left, right = x_eliminate(diag, off, rhs, keep)
    first = pl.ds(0, NK, stride=NJ)
    g[first, :], a[first, :], b[first, :] = rhs, left, right
    line = jnp.zeros((NK, NI), F32)
    for q, pick in enumerate(x_picks(rhs, left, right, across(xc, 0))):
        line = line + jnp.where(lane == q * NK + row, pick, 0.0)
    line = jnp.sum(line, axis=0, keepdims=True)

    j = NJ - 1
    _, _, z_part = lifted(j)
    y = across(yc, j)
    rhs = across(f, j) + across(yc, j - 1) * across(p, j - 1) + y * p_above + z_part
    rhs = x_second_solve(rhs, lambda n: mult_in[pl.ds(n * ROWS + j, NK, stride=NJ), :])
    g[pl.ds(j, NK, stride=NJ), :] = rhs
    last = jnp.where(lane == row, column(rhs, 0), 0.0) + jnp.where(lane == NK + row, column(rhs, NI - 1), 0.0)
    last = jnp.sum(last, axis=0, keepdims=True)
    was = packed[...]
    was = jnp.where(row == 0, line, was)
    send[pl.ds(0, NJ), :] = jnp.where(jnp.logical_and(row == NJ - 1, lane < 2 * NK), last, was)


def coarse_share_kernel(near, far, coarse, send, ext):
    wide = lanes(8)
    level_k = lax.broadcasted_iota(jnp.int32, (8, NI), 0)
    fields = [[], [], [], []]
    for q in range(2):
        lower, upper = sorted_out(near, far, pl.ds(q * 24, 24))
        rows = [lower[n * 8 : n * 8 + 8] for n in range(3)]
        rows += [coarse[pl.ds(q * 64 + n * 8, 8), :] for n in range(8)]
        rows += [upper[n * 8 : n * 8 + 8] for n in range(2)]
        for row in rows:
            fields[2 * q].append(jnp.where(wide < 64, row, 0.0))
            fields[2 * q + 1].append(jnp.where(wide < 64, rolled(row, 64, 1), 0.0))
    xs_, ys_, zs_, damps = fields
    shares = [jnp.zeros((8, NI), F32)] * 4
    for J in range(12):
        top = jnp.where(level_k == 7, 0.0, zs_[J + 1])
        rest = damps[J + 1] + ys_[J + 1] + ys_[J] + top + rolled(top, 1, 0) + xs_[J + 1] + rolled(xs_[J + 1], 1, 1)
        for n, value in enumerate((xs_[J + 1], ys_[J + 1], top, rest)):
            ext[pl.ds(n * 96 + J * 8, 8), :] = value
            at = 10 * J
            first, last = rolled(value, at, 1), rolled(value, at + 5 - 59, 1)
            share = jnp.where(jnp.logical_and(wide >= at, wide < at + 5), first, shares[n])
            shares[n] = jnp.where(jnp.logical_and(wide >= at + 5, wide < at + 10), last, share)
    for n in range(4):
        send[pl.ds(n * 8, 8), :] = shares[n]


def x_second_solve(rhs, kept):
    for n, s in enumerate(STEPS):
        rhs = rhs + kept(2 * n) * rolled(rhs, s, 1) + kept(2 * n + 1) * rolled(rhs, -s, 1)
    return rhs * kept(2 * len(STEPS))


def x_fluxes(fs, source, low, inv, up):
    zero = jnp.zeros((NJ, NI), F32)
    fs[0], fs[GX] = zero, zero
    forward = [source(0)]
    for d in range(1, GX - 1):
        forward.append(source(d) + low[d] * forward[-1])
    value = forward[-1] * inv[GX - 2]
    fs[GX - 1] = value
    for d in range(GX - 3, -1, -1):
        value = forward[d] * inv[d] + up[d] * value
        fs[1 + d] = value


def x_finish(fs, g, a, b, field):
    d = lax.axis_index("gx")
    flux_left, flux_right = fs[d], fs[d + 1]
    for k in range(NK):
        field[pl.ds(k * NJ, NJ), :] = (
            level(g, k) - level(a, k) * column(flux_left, k) + level(b, k) * column(flux_right, k)
        )
    return flux_left, flux_right


def y_source(f, xc, zc, field, fluxes, c_left, k):
    d = lax.axis_index("gx")
    lane = lanes(NJ)
    flux_left, flux_right = fluxes
    v, x = level(field, k), level(xc, k)
    before = jnp.where(lane == 0, column(c_left, k) * v - column(flux_left, k), rolled(x * v, 1, 1))
    last = jnp.where(d == GX - 1, 0.0, x * v + column(flux_right, k))
    after = jnp.where(lane == NI - 1, last, x * rolled(v, -1, 1))
    return z_terms(zc, field, k, level(f, k) + before + after)


def y_first_kernel(xs, got, g, a, b, yg, ya, yb, yw, yinv, xred, cl, send, fs, cs, field, src, base):
    f, p, xc, yc, zc, dp = parts(xs)
    d = lax.axis_index("gx")
    e = lax.axis_index("gy")
    lane = lanes(NJ)
    part = lambda n, q: rolled(got[n, pl.ds(0, NJ), :], -NK * q, 1)
    m = [part(n, 3) for n in range(GX)]
    low, inv, up = [None], [], []
    for n in range(GX - 1):
        dd = part(n, 4) + 1.0 / part(n, 5) + part(n + 1, 2)
        if n:
            low.append(m[n] * inv[-1])
            dd = dd - low[n] * m[n]
        inv.append(1.0 / dd)
        up.append(m[n + 1] * inv[n])
        xred[n], xred[GX + n], xred[2 * GX + n] = (low[n] if n else jnp.zeros_like(dd)), inv[n], up[n]
    x_fluxes(fs, lambda n: part(n + 1, 0) - part(n, 1), low, inv, up)
    cs[0] = jnp.zeros((NJ, NI), F32)
    for n in range(GX):
        cs[n + 1] = part(n, 5)
    c_left = cs[d]
    cl[...] = c_left
    fluxes = x_finish(fs, g, a, b, field)
    for k in range(NK):
        src[pl.ds(k * NJ, NJ), :] = y_source(f, xc, zc, field, fluxes, c_left, k)
        x = level(xc, k)
        x_left = jnp.where(lane == 0, column(c_left, k), rolled(x, 1, 1))
        base[pl.ds(k * NJ, NJ), :] = z_sum(zc, k, x_left + x + level(dp, k))
    ys, ws, invs, spike = [], [None], [], []
    for j in range(NJ):
        y = across(yc, j)
        diag = across(base, j)
        if j < NJ - 1:
            diag = diag + y
        else:
            diag = diag + jnp.where(e == GY - 1, y, 0.0)
        rhs = across(src, j)
        if j:
            y_before = across(yc, j - 1)
            w = y_before * invs[-1]
            ws.append(w)
            diag = diag + y_before - w * y_before
            rhs = rhs + w * ys[-1]
            spike.append(w * spike[-1])
            yw[pl.ds(j * NK, NK), :] = w
        else:
            spike.append(jnp.ones((NK, NI), F32))
            yw[pl.ds(0, NK), :] = jnp.zeros((NK, NI), F32)
        ys.append(rhs)
        invs.append(1.0 / diag)
        yinv[pl.ds(j * NK, NK), :] = invs[-1]
    for j in range(NJ - 1, -1, -1):
        if j == NJ - 1:
            gv, av, bv = ys[j] * invs[j], spike[j] * invs[j], invs[j]
            send[pl.ds(NK, NK), :] = gv
            send[pl.ds(4 * NK, NK), :] = bv + 1.0 / across(yc, j)
        else:
            w = ws[j + 1]
            gv, av, bv = ys[j] * invs[j] + w * gv, spike[j] * invs[j] + w * av, w * bv
        place = pl.ds(j * NK, NK)
        yg[place, :], ya[place, :], yb[place, :] = gv, av, bv
    send[pl.ds(0, NK), :] = gv
    send[pl.ds(2 * NK, NK), :] = av
    send[pl.ds(3 * NK, NK), :] = bv


def y_fluxes(fs, source, low, inv, up):
    zero = jnp.zeros((NK, NI), F32)
    fs[0], fs[CHIPS] = zero, zero
    forward = [source(0)]
    for n in range(1, CHIPS - 1):
        forward.append(source(n) + low(n) * forward[-1])
    value = forward[-1] * inv(CHIPS - 2)
    fs[CHIPS - 1] = value
    for n in range(CHIPS - 3, -1, -1):
        value = forward[n] * inv(n) + up(n) * value
        fs[1 + n] = value


def own_fluxes(fs, joint, inner):
    e = lax.axis_index("gy")
    outer_left, outer_right = fs[e // 2], fs[e // 2 + 1]
    between = inner[...] + joint[1] * outer_left + joint[2] * outer_right
    odd = lax.rem(e, 2) == 1
    return jnp.where(odd, between, outer_left), jnp.where(odd, outer_right, between)


def join_first_kernel(order, mine, theirs, send, joint, inner):
    odd = lax.rem(lax.axis_index("gy"), 2) == 1
    block = lambda ref, q: ref[pl.ds(q * NK, NK), :]
    low = [jnp.where(odd, block(theirs, q), block(mine, q)) for q in range(5)]
    high = [jnp.where(odd, block(mine, q), block(theirs, q)) for q in range(5)]
    inv = 1.0 / (low[4] + high[2])
    from_low, from_high = low[3] * inv, high[3] * inv
    base = (high[0] - low[1]) * inv
    values = (
        low[0] + low[3] * base,
        high[1] - high[3] * base,
        low[2] - low[3] * from_low,
        low[3] * from_high,
        high[4] - high[3] * from_high,
    )
    for q, value in enumerate(values):
        send[pl.ds(q * NK, NK), :] = value
    for n, value in enumerate((inv, from_low, from_high, low[3], high[3])):
        joint[n] = value
    inner[...] = base


def join_again_kernel(order, mine, theirs, joint, send, inner):
    odd = lax.rem(lax.axis_index("gy"), 2) == 1
    block = lambda ref, q: ref[pl.ds(q * NK, NK), :]
    low = [jnp.where(odd, block(theirs, q), block(mine, q)) for q in range(2)]
    high = [jnp.where(odd, block(mine, q), block(theirs, q)) for q in range(2)]
    base = (high[0] - low[1]) * joint[0]
    send[pl.ds(0, NK), :] = low[0] + joint[3] * base
    send[pl.ds(NK, NK), :] = high[1] - joint[4] * base
    inner[...] = base


def y_finish(fluxes, yc, below, yg, ya, yb, field, terms):
    e = lax.axis_index("gy")
    flux_left, flux_right = fluxes
    block = lambda ref, j: ref[pl.ds(j * NK, NK), :]
    p = [block(yg, j) - block(ya, j) * flux_left + block(yb, j) * flux_right for j in range(NJ)]
    for j in range(NJ):
        y = across(yc, j)
        if j:
            before = across(yc, j - 1) * p[j - 1]
        else:
            before = below[pl.ds(0, NK), :] * p[0] - flux_left
        if j < NJ - 1:
            after = y * p[j + 1]
        else:
            after = jnp.where(e == GY - 1, 0.0, y * p[j] + flux_right)
        field[pl.ds(j, NK, stride=NJ), :] = p[j]
        terms[pl.ds(j, NK, stride=NJ), :] = before + after


def x_again_kernel(xs, below, got, joint, inner, share, yg, ya, yb, mult, g, yred, send, fs, field, terms):
    f, p, xc, yc, zc, dp = parts(xs)
    part = lambda n, q: got[n, pl.ds(q * NK, NK), :]
    prev = None
    for n in range(CHIPS - 1):
        dd = part(n, 4) + part(n + 1, 2)
        if n:
            m = part(n, 3)
            low = m * prev
            dd = dd - low * m
            yred[n] = low
        else:
            yred[n] = jnp.zeros_like(dd)
        prev = 1.0 / dd
        yred[CHIPS + n] = prev
        yred[2 * CHIPS + n] = part(n + 1, 3) * prev
    for n in range(1, 4):
        yred[n * CHIPS - 1] = jnp.zeros((NK, NI), F32)
    y_fluxes(
        fs,
        lambda n: part(n + 1, 0) - part(n, 1),
        lambda n: yred[n],
        lambda n: yred[CHIPS + n],
        lambda n: yred[2 * CHIPS + n],
    )
    y_finish(own_fluxes(fs, joint, inner), yc, below, yg, ya, yb, field, terms)
    lane = lanes(NJ)
    packed = jnp.zeros((NJ, NI), F32)
    group = 2
    for k0 in range(0, NK, group):
        rhs = jnp.concatenate(
            [z_terms(zc, field, k, level(f, k) + level(terms, k)) for k in range(k0, k0 + group)], axis=0
        )
        place = pl.ds(k0 * NJ, group * NJ)
        rhs = x_second_solve(rhs, lambda n: mult[pl.ds(n * ROWS + k0 * NJ, group * NJ), :])
        g[place, :] = rhs
        for k in range(k0, k0 + group):
            mine = rhs[(k - k0) * NJ : (k - k0 + 1) * NJ]
            packed = jnp.where(lane == k, column(mine, 0), packed)
            packed = jnp.where(lane == NK + k, column(mine, NI - 1), packed)
    send[pl.ds(0, 8), :] = jnp.where(lanes(8) < 2 * NK, packed[:8], rolled(packed[8:], 2 * NK, 1))
    send[pl.ds(8, 32), :] = share[...]


def y_again_kernel(xs, got, g, a, b, xred, cl, yw, yinv, yg, send, fs, field, src):
    f, p, xc, yc, zc, dp = parts(xs)
    part = lambda n, q: jnp.concatenate(
        [rolled(got[n, pl.ds(0, 8), :], -NK * q, 1), rolled(got[n, pl.ds(0, 8), :], -NK * (q + 2), 1)], axis=0
    )
    x_fluxes(
        fs,
        lambda n: part(n + 1, 0) - part(n, 1),
        [xred[n] for n in range(GX - 1)],
        [xred[GX + n] for n in range(GX - 1)],
        [xred[2 * GX + n] for n in range(GX - 1)],
    )
    fluxes = x_finish(fs, g, a, b, field)
    c_left = cl[...]
    for k in range(NK):
        src[pl.ds(k * NJ, NJ), :] = y_source(f, xc, zc, field, fluxes, c_left, k)
    block = lambda ref, j: ref[pl.ds(j * NK, NK), :]
    ys = []
    for j in range(NJ):
        rhs = across(src, j)
        if j:
            rhs = rhs + block(yw, j) * ys[-1]
        ys.append(rhs)
    value = None
    for j in range(NJ - 1, -1, -1):
        new = ys[j] * block(yinv, j)
        value = new if value is None else new + block(yw, j + 1) * value
        yg[pl.ds(j * NK, NK), :] = value
        if j == NJ - 1:
            send[pl.ds(NK, NK), :] = value
    send[pl.ds(0, NK), :] = value


def residual_kernel(xs, below, got, joint, inner, yg, ya, yb, yred, cl, fluxes, coarse, near, far, fs, terms, tmp, field):
    f, p, xc, yc, zc, dp = parts(xs)
    d = lax.axis_index("gx")
    lane = lanes(NJ)
    part = lambda n, q: got[n, pl.ds(q * NK, NK), :]
    y_fluxes(
        fs,
        lambda n: part(n + 1, 0) - part(n, 1),
        lambda n: yred[n],
        lambda n: yred[CHIPS + n],
        lambda n: yred[2 * CHIPS + n],
    )
    e = lax.axis_index("gy")
    ends = own_fluxes(fs, joint, inner)
    fluxes[0], fluxes[1] = ends
    y_finish(ends, yc, below, yg, ya, yb, field, terms)
    c_left = cl[...]
    main, rim = [], []
    for k in range(NK):
        v, x = level(field, k), level(xc, k)
        left = column(c_left, k)
        x_left = jnp.where(lane == 0, left, rolled(x, 1, 1))
        diag = z_sum(zc, k, x_left + x + y_left_of(yc, below, k) + level(yc, k) + level(dp, k))
        around = jnp.where(lane == 0, 0.0, x_left * rolled(v, 1, 1)) + jnp.where(lane == NI - 1, 0.0, x * rolled(v, -1, 1))
        main.append(level(f, k) - (diag * v - around - level(terms, k) - z_terms(zc, field, k, jnp.zeros((NJ, NI), F32))))
        last = jnp.where(d == GX - 1, 0.0, x * v)
        rim.append(jnp.where(lane == 0, left * v, jnp.where(lane == NI - 1, last, 0.0)))
    pairs = jnp.concatenate([main[2 * K] + main[2 * K + 1] for K in range(NK // 2)], axis=0)
    outer = jnp.concatenate([rim[2 * K] + rim[2 * K + 1] for K in range(NK // 2)], axis=0)
    tmp[...] = squeeze(pairs) + edges(outer)
    store_coarse(coarse, 0, tmp)
    odd = lax.rem(e, 2) == 1
    up, down = coarse[pl.ds(48, 16), :], coarse[pl.ds(0, 16), :]
    near[...] = jnp.where(odd, down, up)
    far[...] = jnp.where(odd, up, down)


def eight(ref, J):
    return ref[pl.ds(J * 8, 8), :]


def coarse_matrix_kernel(ext, got, *outs):
    e = lax.axis_index("gy")
    lane = lanes(8)
    source = lax.broadcasted_iota(jnp.int32, (NI, 4 * NI), 0)
    target = lax.broadcasted_iota(jnp.int32, (NI, 4 * NI), 1)
    device, at_column = target >> 6, target & 63
    hit = jnp.logical_and(at_column < 3, source == 10 * device + at_column)
    hit = jnp.logical_or(hit, jnp.logical_and(at_column > 60, source == 10 * device + at_column - 54))
    outs[2][...] = jnp.where(hit, 1.0, 0.0).astype(jnp.bfloat16)

    def joint(n, J):
        value = jnp.zeros((8, NI), F32)
        for d in range(GX):
            moved = rolled(got[d, pl.ds(8 + n * 8, 8), :], 10 * (d - J), 1)
            value = jnp.where(jnp.logical_and(lane >= 10 * d, lane < 10 * d + 10), moved, value)
        return value

    own = lambda n, J: ext[pl.ds(n * 96 + J * 8, 8), :]
    first = jnp.logical_and(lax.rem(lane, 10) == 0, lane > 0)
    for out, source, width in ((outs[0], own, 64), (outs[1], joint, 10 * GX)):
        y_before = jnp.zeros((8, NI), F32)
        for J in range(12):
            x, y, z_top, rest = (source(n, J) for n in range(4))
            x_left = rolled(x, 1, 1)
            at = e * 8 + J - 2
            valid = jnp.logical_and(jnp.logical_and(at >= 0, at < 8 * GY), lane < width)
            if width != 64:
                rest = rest + jnp.where(first, x_left, 0.0)
            weight = jnp.where(valid, RELAX / jnp.where(valid, rest, 1.0), 0.0)
            couplings = (x_left, x, y_before, y, rolled(z_top, 1, 0), z_top)
            for n, value in enumerate((weight, *(weight * c for c in couplings))):
                out[n, pl.ds(J * 8, 8), :] = value
            y_before = y


def relaxed(res, matrix):
    at = lambda n, J: matrix[n, pl.ds(J * 8, 8), :]

    def around(v, J):
        return (
            at(1, J) * rolled(v[J], 1, 1)
            + at(2, J) * rolled(v[J], -1, 1)
            + at(3, J) * v[J - 1]
            + at(4, J) * v[J + 1]
            + at(5, J) * rolled(v[J], 1, 0)
            + at(6, J) * rolled(v[J], -1, 0)
        )

    first = {J: at(0, J) * res[J] for J in range(12)}
    second = {J: (2.0 - RELAX) * first[J] + around(first, J) for J in range(1, 11)}
    return [first[J] + (1.0 - RELAX) * second[J] + around(second, J) for J in range(2, 10)]


def coarse_own_kernel(order, near, far, coarse, matrix, send):
    lane = lanes(8)
    lower, upper = sorted_out(near, far, pl.ds(0, 16))
    res = [lower[:8], lower[8:], *(eight(coarse, J) for J in range(8)), upper[:8], upper[8:]]
    done = relaxed(res, matrix)
    d = lax.axis_index("gx")
    odd = lax.rem(d, 2) == 1
    for t in range(4):
        both = jnp.where(lane < 64, done[t], rolled(done[t + 4], 64, 1))
        send[pl.ds(t * 8, 8), :] = jnp.where(odd, rolled(both, 64, 1), both)
    strips = [jnp.zeros((8, NI), F32)] * 2
    for J in range(12):
        at = 16 * (J % 8)
        strip = jnp.where(jnp.logical_and(lane >= at, lane < at + 6), rolled(res[J], at + 1, 1), strips[J // 8])
        strips[J // 8] = jnp.where(jnp.logical_and(lane >= at + 6, lane < at + 12), rolled(res[J], at + 6 - 59, 1), strip)
    turn = lax.rem(10 * d + NI - 1, NI)
    send[pl.ds(32, 8), :] = pltpu.roll(strips[0], turn, 1)
    send[pl.ds(40, 8), :] = pltpu.roll(strips[1], turn, 1)


def coarse_last_kernel(got, coarse, matrix, places, res_out, cor_out, tmp, res_tmp):
    d_own = lax.axis_index("gx")
    lane = lanes(8)
    joint = []
    for J in range(12):
        value = jnp.zeros((8, NI), F32)
        at = (lane - 16 * (J % 8)) & (NI - 1)
        for d in range(GX):
            strip = got[d, pl.ds(32 + 8 * (J // 8), 8), :]
            value = value + jnp.where(jnp.logical_and(at >= 10 * d - 1, at < 10 * d + 11), strip, 0.0)
        joint.append(rolled(value, -16 * (J % 8), 1))
    done = jnp.concatenate(relaxed(joint, matrix), axis=0)
    placed = exact_dot(done, places[...])
    end = jnp.logical_or((lane & 63) < 3, (lane & 63) > 60)
    turn = lax.rem(NI - 10 * d_own, NI)
    for J in range(8):
        mine = pltpu.roll(joint[J + 2], turn, 1)
        mine = jnp.where(lane == 0, mine, jnp.where(lane == 63, rolled(mine, 54, 1), eight(coarse, J)))
        res_tmp[pl.ds(J, 8, stride=8), :] = mine
        rows = pl.ds((J % 4) * 8, 8)
        for m in range(4):
            even, odd = got[2 * m, rows, :], got[2 * m + 1, rows, :]
            if J < 4:
                value = jnp.where(lane < 64, even, odd)
            else:
                value = rolled(jnp.where(lane < 64, odd, even), 64, 1)
            right = placed[J * 8 : J * 8 + 8, m * NI : (m + 1) * NI]
            tmp[m, pl.ds(J, 8, stride=8), :] = jnp.where(end, right, value)
    for m in range(4):
        cor_out[:, pl.ds(m * NI, NI)] = tmp[m]
    res_out[...] = res_tmp[:, :64]


def field_kernel(order, fluxes, yg, ya, yb, field):
    for j in range(NJ):
        place = pl.ds(j * NK, NK)
        field[pl.ds(j, NK, stride=NJ), :] = yg[place, :] - ya[place, :] * fluxes[0] + yb[place, :] * fluxes[1]


def spread(value, axis, count):
    many = jnp.broadcast_to(value[None], (count,) + value.shape)
    return lax.all_to_all(many, axis, split_axis=0, concat_axis=0, tiled=True)


def other_core(value):
    return lax.ppermute(value, "gy", [(n, n ^ 1) for n in range(GY)])


def spread_by_core(value):
    groups = [list(range(0, GY, 2)), list(range(1, GY, 2))]
    many = jnp.broadcast_to(value[None], (CHIPS,) + value.shape)
    return lax.all_to_all(many, "gy", split_axis=0, concat_axis=0, tiled=True, axis_index_groups=groups)


def swap(near, far):
    pairs = [(n, n ^ 1) for n in range(GY)]
    others = [(n, (n + 1) % GY if n % 2 else (n - 1) % GY) for n in range(GY)]
    return lax.ppermute(near, "gy", pairs), lax.ppermute(far, "gy", others)


def body(forcing, pressure_in, x_coupling, y_coupling, z_coupling, damping):
    args = (forcing, pressure_in, x_coupling, y_coupling, z_coupling, damping)
    whole = sds(ROWS, NI)
    kept = sds((2 * len(STEPS) + 1) * ROWS, NI)
    xs, near, far, coef = call(
        first_kernel,
        [sds(6 * ROWS, NI), sds(80, NI), sds(80, NI), sds(128, NI)],
        *[v.reshape(ROWS, NI) for v in args],
        scratch=[(128, NI)],
        hbm=6,
        sems=6,
    )
    mine = near
    near, far = swap(near, far)
    g, a, b, mult, packed = call(x_first_kernel, [whole, whole, whole, kept, sds(NJ, NI)], xs, mine, flops=10**8)
    below, g, a, b, mult, send, *sides = call(
        x_rim_kernel,
        [sds(NK, NI), whole, whole, whole, kept, sds(NJ, NI), sds(48, NI), sds(48, NI), sds(128, NI)],
        xs, near, far, coef, packed, g, a, b, mult,
        aliases={5: 1, 6: 2, 7: 3, 8: 4},
    )
    got = spread(send, "gx", GX)
    yg, ya, yb, yw, yinv, xred, cl, send = call(
        y_first_kernel,
        [whole] * 5 + [sds(3 * GX, NJ, NI), sds(NJ, NI), sds(5 * NK, NI)],
        xs, got, g, a, b,
        scratch=[(GX + 1, NJ, NI), (GX + 1, NJ, NI), (ROWS, NI), (ROWS, NI), (ROWS, NI)],
    )
    theirs = other_core(send)
    share, ext = call(coarse_share_kernel, [sds(32, NI), sds(4 * 96, NI)], *sides, flops=10**7)
    send, joint, inner = call(
        join_first_kernel, [sds(5 * NK, NI), sds(5, NK, NI), sds(NK, NI)], share, send, theirs
    )
    got = spread_by_core(send)
    g, yred, send = call(
        x_again_kernel,
        [whole, sds(3 * CHIPS, NK, NI), sds(40, NI)],
        xs, below, got, joint, inner, share, yg, ya, yb, mult,
        scratch=[(CHIPS + 1, NK, NI), (ROWS, NI), (ROWS, NI)],
    )
    got = spread(send, "gx", GX)
    yg, send = call(
        y_again_kernel,
        [whole, sds(2 * NK, NI)],
        xs, got, g, a, b, xred, cl, yw, yinv,
        scratch=[(GX + 1, NJ, NI), (ROWS, NI), (ROWS, NI)],
    )
    theirs = other_core(send)
    own, ends, places = call(
        coarse_matrix_kernel, [sds(7, 96, NI)] * 2 + [jax.ShapeDtypeStruct((NI, 4 * NI), jnp.bfloat16)], ext, got, flops=10**7
    )
    send, inner = call(join_again_kernel, [sds(2 * NK, NI), sds(NK, NI)], ends, send, theirs, joint)
    got = spread_by_core(send)
    fluxes, coarse, near, far = call(
        residual_kernel,
        [sds(2, NK, NI), sds(64, NI), sds(16, NI), sds(16, NI)],
        xs, below, got, joint, inner, yg, ya, yb, yred, cl,
        scratch=[(CHIPS + 1, NK, NI), (ROWS, NI), (128, NI), (ROWS, NI)],
    )
    mine = near
    near, far = swap(near, far)
    (field,) = call(field_kernel, [whole], mine, fluxes, yg, ya, yb, flops=10**7)
    (send,) = call(coarse_own_kernel, [sds(48, NI)], field, near, far, coarse, own, hbm=1)
    got = spread(send, "gx", GX)
    res, cor = call(
        coarse_last_kernel, [sds(64, 64), sds(64, 4 * NI)], got, coarse, ends, places, scratch=[(4, 64, NI), (64, NI)]
    )
    return field.reshape(NK, NJ, NI), res.reshape(8, 8, 64), cor.reshape(8, 8, 512)


def solution(mesh):
    spec = P(None, "gy", "gx")
    return jax.shard_map(
        body, mesh=mesh, in_specs=(spec,) * 6, out_specs=(spec, spec, P(None, "gy", None)), check_vma=False
    )
```

```python
import functools

import jax
import jax.numpy as jnp
from jax import lax
from jax.experimental import pallas as pl
from jax.experimental.pallas import tpu as pltpu
from jax.sharding import PartitionSpec as P

RELAX = 0.8
NK, NJ, NI = 16, 16, 128
ROWS = NK * NJ
GX, GY = 8, 16
CHIPS = GY // 2
STEPS = (1, 2, 4, 8, 16, 32, 64)
F32 = jnp.float32


def sds(*shape):
    return jax.ShapeDtypeStruct(shape, F32)


def call(kernel, outs, *args, scratch=(), hbm=0, aliases={}, sems=0, flops=None):
    spec = pl.BlockSpec(memory_space=pltpu.VMEM)
    outside = pl.BlockSpec(memory_space=pltpu.HBM)
    args = [pltpu.with_memory_space_constraint(v, pltpu.HBM) for v in args[:hbm]] + list(args[hbm:])
    shapes = [pltpu.VMEM(v, F32) for v in scratch]
    if sems:
        shapes.append(pltpu.SemaphoreType.DMA((sems,)))
    cost = None if flops is None else pl.CostEstimate(flops=flops, bytes_accessed=1 << 20, transcendentals=0)
    return pl.pallas_call(
        kernel,
        out_shape=outs,
        in_specs=[outside] * hbm + [spec] * (len(args) - hbm),
        out_specs=[spec] * len(outs),
        scratch_shapes=shapes,
        input_output_aliases=aliases,
        cost_estimate=cost,
        compiler_params=pltpu.CompilerParams(vmem_limit_bytes=16 * 1024 * 1024),
    )(*args)


def parts(xs):
    return [xs.at[pl.ds(n * ROWS, ROWS), :] for n in range(6)]


def lanes(rows, width=NI):
    return lax.broadcasted_iota(jnp.int32, (rows, width), 1)


def rolled(value, amount, axis):
    return pltpu.roll(value, amount % value.shape[axis], axis)


def level(ref, k):
    return ref[pl.ds(k * NJ, NJ), :]


def across(ref, j, count=NK, stride=NJ):
    return ref[pl.ds(j, count, stride=stride), :]


def column(value, k):
    return jnp.broadcast_to(value[:, k : k + 1], (value.shape[0], NI))


def z_pair(zc, k):
    return (level(zc, k - 1) if k > 0 else None, level(zc, k) if k < NK - 1 else None)


def z_sum(zc, k, base):
    low, top = z_pair(zc, k)
    if low is not None:
        base = base + low
    if top is not None:
        base = base + top
    return base


def z_terms(zc, field, k, base):
    low, top = z_pair(zc, k)
    if low is not None:
        base = base + low * level(field, k - 1)
    if top is not None:
        base = base + top * level(field, k + 1)
    return base


def y_left_of(yc, halo, k):
    row = lax.broadcasted_iota(jnp.int32, (NJ, NI), 0)
    return jnp.where(row == 0, halo[pl.ds(k, 1), :], rolled(level(yc, k), 1, 0))


def exact_dot(values, matrix):
    matrix = matrix.astype(jnp.bfloat16)
    total = None
    for _ in range(3):
        piece = values.astype(jnp.bfloat16)
        values = values - piece.astype(F32)
        part = jnp.dot(piece, matrix, preferred_element_type=F32)
        total = part if total is None else total + part
    return total


def squeeze(values, scale=0.125, start=0):
    source = lax.broadcasted_iota(jnp.int32, (NI, NI), 0)
    target = lax.broadcasted_iota(jnp.int32, (NI, NI), 1)
    matrix = jnp.where(source // 2 + start == target, scale, 0.0).astype(F32)
    return exact_dot(values, matrix)


def edges(values, scale=0.125):
    source = lax.broadcasted_iota(jnp.int32, (NI, NI), 0)
    target = lax.broadcasted_iota(jnp.int32, (NI, NI), 1)
    hit = ((source == NI - 1) & (target == 64)) | ((source == 0) & (target == NI - 1))
    matrix = jnp.where(hit, scale, 0.0).astype(F32)
    return exact_dot(values, matrix)


def store_coarse(out, base, tmp):
    for J in range(NJ // 2):
        out[pl.ds(base + J * 8, 8), :] = across(tmp, 2 * J, 8) + across(tmp, 2 * J + 1, 8)


def first_kernel(fh, ph, xh, yh, zh, dh, xs, near, far, coarse, tmp, sems):
    copies = [
        pltpu.make_async_copy(ref, xs.at[pl.ds(n * ROWS, ROWS), :], sems.at[n])
        for n, ref in enumerate((fh, ph, xh, yh, zh, dh))
    ]
    for copy in copies:
        copy.start()
    for copy in copies[1:]:
        copy.wait()
    f, p, xc, yc, zc, dp = parts(xs)
    odd = lax.rem(lax.axis_index("gy"), 2) == 1
    for q, two in enumerate(((xc, yc), (zc, dp))):
        total = jnp.zeros((128, NI), F32)
        for half, ref in enumerate(two):
            pairs = jnp.concatenate([level(ref, 2 * K) + level(ref, 2 * K + 1) for K in range(NK // 2)], axis=0)
            total = total + squeeze(pairs, start=64 * half)
        tmp[...] = total
        store_coarse(coarse, q * 64, tmp)

    def put(place, up, down):
        near[place, :] = jnp.where(odd, down, up)
        far[place, :] = jnp.where(odd, up, down)

    put(pl.ds(0, NK), across(p, NJ - 1), across(p, 0))
    put(pl.ds(NK, NK), across(yc, NJ - 1), across(yc, 0))
    for q in range(2):
        put(pl.ds(2 * NK + q * 24, 24), coarse[pl.ds(q * 64 + 40, 24), :], coarse[pl.ds(q * 64, 24), :])
    copies[0].wait()


def sorted_out(near, far, place):
    e = lax.axis_index("gy")
    odd = lax.rem(e, 2) == 1
    one, two = near[place, :], far[place, :]
    return (
        jnp.where(e == 0, 0.0, jnp.where(odd, one, two)),
        jnp.where(e == GY - 1, 0.0, jnp.where(odd, two, one)),
    )


def x_matrix(x, rest):
    d = lax.axis_index("gx")
    lane = lanes(x.shape[0])
    inner = jnp.logical_or(lane < NI - 1, d == GX - 1)
    diag = jnp.where(lane == 0, 0.0, rolled(x, 1, 1)) + jnp.where(inner, x, 0.0) + rest
    return diag, jnp.where(lane == NI - 1, 0.0, -x)


def x_eliminate(diag, off, rhs, keep):
    wide = lanes(diag.shape[0])
    ends = jnp.where(jnp.logical_or(wide == 0, wide == NI - 1), 1.0, 0.0).astype(F32)
    for n, s in enumerate(STEPS):
        inv = 1.0 / diag
        low = rolled(off, s, 1)
        alpha = -low * rolled(inv, s, 1)
        beta = -off * rolled(inv, -s, 1)
        if s < NI // 2:
            keep(2 * n, alpha)
            keep(2 * n + 1, beta)
        else:
            keep(2 * n, alpha + beta)
        diag = diag + alpha * low + beta * off
        rhs = rhs + alpha * rolled(rhs, s, 1) + beta * rolled(rhs, -s, 1)
        if s < NI // 2:
            off = beta * rolled(off, -s, 1)
            ends = ends + alpha * rolled(ends, s, 1) + beta * rolled(ends, -s, 1)
    inv = 1.0 / diag
    keep(2 * len(STEPS), inv)
    other = rolled(ends, NI // 2, 1)
    left = jnp.where(wide < NI // 2, ends, alpha * other)
    right = jnp.where(wide < NI // 2, beta * other, ends)
    return rhs * inv, left * inv, right * inv


def x_picks(g, a, b, x):
    return column(g, 0), column(g, NI - 1), column(a, 0), column(b, 0), column(b, NI - 1), column(x, NI - 1)


def x_first_kernel(xs, order, g, a, b, mult, packed_out):
    f, p, xc, yc, zc, dp = parts(xs)
    lane = lanes(NJ)
    row = lax.broadcasted_iota(jnp.int32, (NJ, NI), 0)
    packed = jnp.zeros((NJ, NI), F32)
    group = 8
    for k0 in range(0, NK, group):
        diag, off, rhs = [], [], []
        for k in range(k0, k0 + group):
            y, v = level(yc, k), level(p, k)
            y_left = jnp.where(row == 0, 0.0, rolled(y, 1, 0))
            matrix = x_matrix(level(xc, k), z_sum(zc, k, y_left + y + level(dp, k)))
            diag.append(matrix[0])
            off.append(matrix[1])
            after = jnp.where(row == NJ - 1, 0.0, rolled(v, -1, 0))
            rhs.append(z_terms(zc, p, k, level(f, k) + y_left * rolled(v, 1, 0) + y * after))
        diag, off, rhs = (jnp.concatenate(v, axis=0) for v in (diag, off, rhs))
        place = pl.ds(k0 * NJ, group * NJ)

        def keep(n, value):
            mult[pl.ds(n * ROWS + k0 * NJ, group * NJ), :] = value

        rhs, left, right = x_eliminate(diag, off, rhs, keep)
        g[place, :], a[place, :], b[place, :] = rhs, left, right
        for k in range(k0, k0 + group):
            part = slice((k - k0) * NJ, (k - k0 + 1) * NJ)
            for q, pick in enumerate(x_picks(rhs[part], left[part], right[part], level(xc, k))):
                packed = jnp.where(lane == q * NK + k, pick, packed)
    packed_out[...] = packed


def x_rim_kernel(xs, near, far, coarse, packed, g_in, a_in, b_in, mult_in, below, g, a, b, mult, send, near_out, far_out, coarse_out):
    f, p, xc, yc, zc, dp = parts(xs)
    lane = lanes(NK)
    row = lax.broadcasted_iota(jnp.int32, (NK, NI), 0)

    def lifted(j):
        z, v = across(zc, j), across(p, j)
        top = jnp.where(row == NK - 1, 0.0, z)
        low = rolled(top, 1, 0)
        return low, top, low * rolled(v, 1, 0) + top * rolled(v, -1, 0)

    near_out[...] = near[pl.ds(2 * NK, 48), :]
    far_out[...] = far[pl.ds(2 * NK, 48), :]
    coarse_out[...] = coarse[...]
    p_below, p_above = sorted_out(near, far, pl.ds(0, NK))
    y_left, _ = sorted_out(near, far, pl.ds(NK, NK))
    below[...] = y_left
    low, top, z_part = lifted(0)
    y = across(yc, 0)
    diag, off = x_matrix(across(xc, 0), low + top + y + y_left + across(dp, 0))
    rhs = across(f, 0) + y_left * p_below + y * across(p, 1) + z_part

    def keep(n, value):
        mult[pl.ds(n * ROWS, NK, stride=NJ), :] = value

    rhs, left, right = x_eliminate(diag, off, rhs, keep)
    first = pl.ds(0, NK, stride=NJ)
    g[first, :], a[first, :], b[first, :] = rhs, left, right
    line = jnp.zeros((NK, NI), F32)
    for q, pick in enumerate(x_picks(rhs, left, right, across(xc, 0))):
        line = line + jnp.where(lane == q * NK + row, pick, 0.0)
    line = jnp.sum(line, axis=0, keepdims=True)

    j = NJ - 1
    _, _, z_part = lifted(j)
    y = across(yc, j)
    rhs = across(f, j) + across(yc, j - 1) * across(p, j - 1) + y * p_above + z_part
    rhs = x_second_solve(rhs, lambda n: mult_in[pl.ds(n * ROWS + j, NK, stride=NJ), :])
    g[pl.ds(j, NK, stride=NJ), :] = rhs
    last = jnp.where(lane == row, column(rhs, 0), 0.0) + jnp.where(lane == NK + row, column(rhs, NI - 1), 0.0)
    last = jnp.sum(last, axis=0, keepdims=True)
    was = packed[...]
    was = jnp.where(row == 0, line, was)
    send[pl.ds(0, NJ), :] = jnp.where(jnp.logical_and(row == NJ - 1, lane < 2 * NK), last, was)


def coarse_share_kernel(near, far, coarse, send, ext):
    wide = lanes(8)
    level_k = lax.broadcasted_iota(jnp.int32, (8, NI), 0)
    fields = [[], [], [], []]
    for q in range(2):
        lower, upper = sorted_out(near, far, pl.ds(q * 24, 24))
        rows = [lower[n * 8 : n * 8 + 8] for n in range(3)]
        rows += [coarse[pl.ds(q * 64 + n * 8, 8), :] for n in range(8)]
        rows += [upper[n * 8 : n * 8 + 8] for n in range(2)]
        for row in rows:
            fields[2 * q].append(jnp.where(wide < 64, row, 0.0))
            fields[2 * q + 1].append(jnp.where(wide < 64, rolled(row, 64, 1), 0.0))
    xs_, ys_, zs_, damps = fields
    shares = [jnp.zeros((8, NI), F32)] * 4
    for J in range(12):
        top = jnp.where(level_k == 7, 0.0, zs_[J + 1])
        rest = damps[J + 1] + ys_[J + 1] + ys_[J] + top + rolled(top, 1, 0) + xs_[J + 1] + rolled(xs_[J + 1], 1, 1)
        for n, value in enumerate((xs_[J + 1], ys_[J + 1], top, rest)):
            ext[pl.ds(n * 96 + J * 8, 8), :] = value
            at = 10 * J
            first, last = rolled(value, at, 1), rolled(value, at + 5 - 59, 1)
            share = jnp.where(jnp.logical_and(wide >= at, wide < at + 5), first, shares[n])
            shares[n] = jnp.where(jnp.logical_and(wide >= at + 5, wide < at + 10), last, share)
    for n in range(4):
        send[pl.ds(n * 8, 8), :] = shares[n]


def x_second_solve(rhs, kept):
    for n, s in enumerate(STEPS[:-1]):
        rhs = rhs + kept(2 * n) * rolled(rhs, s, 1) + kept(2 * n + 1) * rolled(rhs, -s, 1)
    rhs = rhs + kept(2 * len(STEPS) - 2) * rolled(rhs, NI // 2, 1)
    return rhs * kept(2 * len(STEPS))


def x_fluxes(fs, source, low, inv, up):
    zero = jnp.zeros((NJ, NI), F32)
    fs[0], fs[GX] = zero, zero
    forward = [source(0)]
    for d in range(1, GX - 1):
        forward.append(source(d) + low[d] * forward[-1])
    value = forward[-1] * inv[GX - 2]
    fs[GX - 1] = value
    for d in range(GX - 3, -1, -1):
        value = forward[d] * inv[d] + up[d] * value
        fs[1 + d] = value


def x_finish(fs, g, a, b, field):
    d = lax.axis_index("gx")
    flux_left, flux_right = fs[d], fs[d + 1]
    for k in range(NK):
        field[pl.ds(k * NJ, NJ), :] = (
            level(g, k) - level(a, k) * column(flux_left, k) + level(b, k) * column(flux_right, k)
        )
    return flux_left, flux_right


def y_source(f, xc, zc, field, fluxes, c_left, k):
    d = lax.axis_index("gx")
    lane = lanes(NJ)
    flux_left, flux_right = fluxes
    v, x = level(field, k), level(xc, k)
    before = jnp.where(lane == 0, column(c_left, k) * v - column(flux_left, k), rolled(x * v, 1, 1))
    last = jnp.where(d == GX - 1, 0.0, x * v + column(flux_right, k))
    after = jnp.where(lane == NI - 1, last, x * rolled(v, -1, 1))
    return z_terms(zc, field, k, level(f, k) + before + after)


def y_first_kernel(xs, got, g, a, b, yg, ya, yb, yw, yinv, xred, cl, send, fs, cs, field, src, base):
    f, p, xc, yc, zc, dp = parts(xs)
    d = lax.axis_index("gx")
    e = lax.axis_index("gy")
    lane = lanes(NJ)
    part = lambda n, q: rolled(got[n, pl.ds(0, NJ), :], -NK * q, 1)
    m = [part(n, 3) for n in range(GX)]
    low, inv, up = [None], [], []
    for n in range(GX - 1):
        dd = part(n, 4) + 1.0 / part(n, 5) + part(n + 1, 2)
        if n:
            low.append(m[n] * inv[-1])
            dd = dd - low[n] * m[n]
        inv.append(1.0 / dd)
        up.append(m[n + 1] * inv[n])
        xred[n], xred[GX + n], xred[2 * GX + n] = (low[n] if n else jnp.zeros_like(dd)), inv[n], up[n]
    x_fluxes(fs, lambda n: part(n + 1, 0) - part(n, 1), low, inv, up)
    cs[0] = jnp.zeros((NJ, NI), F32)
    for n in range(GX):
        cs[n + 1] = part(n, 5)
    c_left = cs[d]
    cl[...] = c_left
    fluxes = x_finish(fs, g, a, b, field)
    for k in range(NK):
        src[pl.ds(k * NJ, NJ), :] = y_source(f, xc, zc, field, fluxes, c_left, k)
        x = level(xc, k)
        x_left = jnp.where(lane == 0, column(c_left, k), rolled(x, 1, 1))
        base[pl.ds(k * NJ, NJ), :] = z_sum(zc, k, x_left + x + level(dp, k))
    ys, ws, invs, spike = [], [None], [], []
    for j in range(NJ):
        y = across(yc, j)
        diag = across(base, j)
        if j < NJ - 1:
            diag = diag + y
        else:
            diag = diag + jnp.where(e == GY - 1, y, 0.0)
        rhs = across(src, j)
        if j:
            y_before = across(yc, j - 1)
            w = y_before * invs[-1]
            ws.append(w)
            diag = diag + y_before - w * y_before
            rhs = rhs + w * ys[-1]
            spike.append(w * spike[-1])
            yw[pl.ds(j * NK, NK), :] = w
        else:
            spike.append(jnp.ones((NK, NI), F32))
            yw[pl.ds(0, NK), :] = jnp.zeros((NK, NI), F32)
        ys.append(rhs)
        invs.append(1.0 / diag)
        yinv[pl.ds(j * NK, NK), :] = invs[-1]
    for j in range(NJ - 1, -1, -1):
        if j == NJ - 1:
            gv, av, bv = ys[j] * invs[j], spike[j] * invs[j], invs[j]
            send[pl.ds(NK, NK), :] = gv
            send[pl.ds(4 * NK, NK), :] = bv + 1.0 / across(yc, j)
        else:
            w = ws[j + 1]
            gv, av, bv = ys[j] * invs[j] + w * gv, spike[j] * invs[j] + w * av, w * bv
        place = pl.ds(j * NK, NK)
        yg[place, :], ya[place, :], yb[place, :] = gv, av, bv
    send[pl.ds(0, NK), :] = gv
    send[pl.ds(2 * NK, NK), :] = av
    send[pl.ds(3 * NK, NK), :] = bv


def y_fluxes(fs, source, low, inv, up):
    zero = jnp.zeros((NK, NI), F32)
    fs[0], fs[CHIPS] = zero, zero
    forward = [source(0)]
    for n in range(1, CHIPS - 1):
        forward.append(source(n) + low(n) * forward[-1])
    value = forward[-1] * inv(CHIPS - 2)
    fs[CHIPS - 1] = value
    for n in range(CHIPS - 3, -1, -1):
        value = forward[n] * inv(n) + up(n) * value
        fs[1 + n] = value


def own_fluxes(fs, joint, inner):
    e = lax.axis_index("gy")
    outer_left, outer_right = fs[e // 2], fs[e // 2 + 1]
    between = inner[...] + joint[1] * outer_left + joint[2] * outer_right
    odd = lax.rem(e, 2) == 1
    return jnp.where(odd, between, outer_left), jnp.where(odd, outer_right, between)


def join_first_kernel(order, mine, theirs, send, joint, inner):
    odd = lax.rem(lax.axis_index("gy"), 2) == 1
    block = lambda ref, q: ref[pl.ds(q * NK, NK), :]
    low = [jnp.where(odd, block(theirs, q), block(mine, q)) for q in range(5)]
    high = [jnp.where(odd, block(mine, q), block(theirs, q)) for q in range(5)]
    inv = 1.0 / (low[4] + high[2])
    from_low, from_high = low[3] * inv, high[3] * inv
    base = (high[0] - low[1]) * inv
    values = (
        low[0] + low[3] * base,
        high[1] - high[3] * base,
        low[2] - low[3] * from_low,
        low[3] * from_high,
        high[4] - high[3] * from_high,
    )
    for q, value in enumerate(values):
        send[pl.ds(q * NK, NK), :] = value
    for n, value in enumerate((inv, from_low, from_high, low[3], high[3])):
        joint[n] = value
    inner[...] = base


def join_again_kernel(order, mine, theirs, joint, send, inner):
    odd = lax.rem(lax.axis_index("gy"), 2) == 1
    block = lambda ref, q: ref[pl.ds(q * NK, NK), :]
    low = [jnp.where(odd, block(theirs, q), block(mine, q)) for q in range(2)]
    high = [jnp.where(odd, block(mine, q), block(theirs, q)) for q in range(2)]
    base = (high[0] - low[1]) * joint[0]
    send[pl.ds(0, NK), :] = low[0] + joint[3] * base
    send[pl.ds(NK, NK), :] = high[1] - joint[4] * base
    inner[...] = base


def y_finish(fluxes, yc, below, yg, ya, yb, field, terms):
    e = lax.axis_index("gy")
    flux_left, flux_right = fluxes
    block = lambda ref, j: ref[pl.ds(j * NK, NK), :]
    p = [block(yg, j) - block(ya, j) * flux_left + block(yb, j) * flux_right for j in range(NJ)]
    for j in range(NJ):
        y = across(yc, j)
        if j:
            before = across(yc, j - 1) * p[j - 1]
        else:
            before = below[pl.ds(0, NK), :] * p[0] - flux_left
        if j < NJ - 1:
            after = y * p[j + 1]
        else:
            after = jnp.where(e == GY - 1, 0.0, y * p[j] + flux_right)
        field[pl.ds(j, NK, stride=NJ), :] = p[j]
        terms[pl.ds(j, NK, stride=NJ), :] = before + after


def x_again_kernel(xs, below, got, joint, inner, share, yg, ya, yb, mult, g, yred, send, fs, field, terms):
    f, p, xc, yc, zc, dp = parts(xs)
    part = lambda n, q: got[n, pl.ds(q * NK, NK), :]
    prev = None
    for n in range(CHIPS - 1):
        dd = part(n, 4) + part(n + 1, 2)
        if n:
            m = part(n, 3)
            low = m * prev
            dd = dd - low * m
            yred[n] = low
        else:
            yred[n] = jnp.zeros_like(dd)
        prev = 1.0 / dd
        yred[CHIPS + n] = prev
        yred[2 * CHIPS + n] = part(n + 1, 3) * prev
    for n in range(1, 4):
        yred[n * CHIPS - 1] = jnp.zeros((NK, NI), F32)
    y_fluxes(
        fs,
        lambda n: part(n + 1, 0) - part(n, 1),
        lambda n: yred[n],
        lambda n: yred[CHIPS + n],
        lambda n: yred[2 * CHIPS + n],
    )
    y_finish(own_fluxes(fs, joint, inner), yc, below, yg, ya, yb, field, terms)
    lane = lanes(NJ)
    packed = jnp.zeros((NJ, NI), F32)
    group = 2
    for k0 in range(0, NK, group):
        rhs = jnp.concatenate(
            [z_terms(zc, field, k, level(f, k) + level(terms, k)) for k in range(k0, k0 + group)], axis=0
        )
        place = pl.ds(k0 * NJ, group * NJ)
        rhs = x_second_solve(rhs, lambda n: mult[pl.ds(n * ROWS + k0 * NJ, group * NJ), :])
        g[place, :] = rhs
        for k in range(k0, k0 + group):
            mine = rhs[(k - k0) * NJ : (k - k0 + 1) * NJ]
            packed = jnp.where(lane == k, column(mine, 0), packed)
            packed = jnp.where(lane == NK + k, column(mine, NI - 1), packed)
    send[pl.ds(0, 8), :] = jnp.where(lanes(8) < 2 * NK, packed[:8], rolled(packed[8:], 2 * NK, 1))
    send[pl.ds(8, 32), :] = share[...]


def y_again_kernel(xs, got, g, a, b, xred, cl, yw, yinv, yg, send, fs, field, src):
    f, p, xc, yc, zc, dp = parts(xs)
    part = lambda n, q: jnp.concatenate(
        [rolled(got[n, pl.ds(0, 8), :], -NK * q, 1), rolled(got[n, pl.ds(0, 8), :], -NK * (q + 2), 1)], axis=0
    )
    x_fluxes(
        fs,
        lambda n: part(n + 1, 0) - part(n, 1),
        [xred[n] for n in range(GX - 1)],
        [xred[GX + n] for n in range(GX - 1)],
        [xred[2 * GX + n] for n in range(GX - 1)],
    )
    fluxes = x_finish(fs, g, a, b, field)
    c_left = cl[...]
    for k in range(NK):
        src[pl.ds(k * NJ, NJ), :] = y_source(f, xc, zc, field, fluxes, c_left, k)
    block = lambda ref, j: ref[pl.ds(j * NK, NK), :]
    ys = []
    for j in range(NJ):
        rhs = across(src, j)
        if j:
            rhs = rhs + block(yw, j) * ys[-1]
        ys.append(rhs)
    value = None
    for j in range(NJ - 1, -1, -1):
        new = ys[j] * block(yinv, j)
        value = new if value is None else new + block(yw, j + 1) * value
        yg[pl.ds(j * NK, NK), :] = value
        if j == NJ - 1:
            send[pl.ds(NK, NK), :] = value
    send[pl.ds(0, NK), :] = value


def residual_kernel(xs, below, got, joint, inner, yg, ya, yb, yred, cl, fluxes, coarse, near, far, fs, terms, tmp, field):
    f, p, xc, yc, zc, dp = parts(xs)
    d = lax.axis_index("gx")
    lane = lanes(NJ)
    part = lambda n, q: got[n, pl.ds(q * NK, NK), :]
    y_fluxes(
        fs,
        lambda n: part(n + 1, 0) - part(n, 1),
        lambda n: yred[n],
        lambda n: yred[CHIPS + n],
        lambda n: yred[2 * CHIPS + n],
    )
    e = lax.axis_index("gy")
    ends = own_fluxes(fs, joint, inner)
    fluxes[0], fluxes[1] = ends
    y_finish(ends, yc, below, yg, ya, yb, field, terms)
    c_left = cl[...]
    main, rim = [], []
    for k in range(NK):
        v, x = level(field, k), level(xc, k)
        left = column(c_left, k)
        x_left = jnp.where(lane == 0, left, rolled(x, 1, 1))
        diag = z_sum(zc, k, x_left + x + y_left_of(yc, below, k) + level(yc, k) + level(dp, k))
        around = jnp.where(lane == 0, 0.0, x_left * rolled(v, 1, 1)) + jnp.where(lane == NI - 1, 0.0, x * rolled(v, -1, 1))
        main.append(level(f, k) - (diag * v - around - level(terms, k) - z_terms(zc, field, k, jnp.zeros((NJ, NI), F32))))
        last = jnp.where(d == GX - 1, 0.0, x * v)
        rim.append(jnp.where(lane == 0, left * v, jnp.where(lane == NI - 1, last, 0.0)))
    pairs = jnp.concatenate([main[2 * K] + main[2 * K + 1] for K in range(NK // 2)], axis=0)
    outer = jnp.concatenate([rim[2 * K] + rim[2 * K + 1] for K in range(NK // 2)], axis=0)
    tmp[...] = squeeze(pairs) + edges(outer)
    store_coarse(coarse, 0, tmp)
    odd = lax.rem(e, 2) == 1
    up, down = coarse[pl.ds(48, 16), :], coarse[pl.ds(0, 16), :]
    near[...] = jnp.where(odd, down, up)
    far[...] = jnp.where(odd, up, down)


def eight(ref, J):
    return ref[pl.ds(J * 8, 8), :]


def coarse_matrix_kernel(ext, got, *outs):
    e = lax.axis_index("gy")
    lane = lanes(8)
    source = lax.broadcasted_iota(jnp.int32, (NI, 4 * NI), 0)
    target = lax.broadcasted_iota(jnp.int32, (NI, 4 * NI), 1)
    device, at_column = target >> 6, target & 63
    hit = jnp.logical_and(at_column < 3, source == 10 * device + at_column)
    hit = jnp.logical_or(hit, jnp.logical_and(at_column > 60, source == 10 * device + at_column - 54))
    outs[2][...] = jnp.where(hit, 1.0, 0.0).astype(jnp.bfloat16)

    def joint(n, J):
        value = jnp.zeros((8, NI), F32)
        for d in range(GX):
            moved = rolled(got[d, pl.ds(8 + n * 8, 8), :], 10 * (d - J), 1)
            value = jnp.where(jnp.logical_and(lane >= 10 * d, lane < 10 * d + 10), moved, value)
        return value

    own = lambda n, J: ext[pl.ds(n * 96 + J * 8, 8), :]
    first = jnp.logical_and(lax.rem(lane, 10) == 0, lane > 0)
    for out, source, width in ((outs[0], own, 64), (outs[1], joint, 10 * GX)):
        y_before = jnp.zeros((8, NI), F32)
        for J in range(12):
            x, y, z_top, rest = (source(n, J) for n in range(4))
            x_left = rolled(x, 1, 1)
            at = e * 8 + J - 2
            valid = jnp.logical_and(jnp.logical_and(at >= 0, at < 8 * GY), lane < width)
            if width != 64:
                rest = rest + jnp.where(first, x_left, 0.0)
            weight = jnp.where(valid, RELAX / jnp.where(valid, rest, 1.0), 0.0)
            couplings = (x_left, x, y_before, y, rolled(z_top, 1, 0), z_top)
            for n, value in enumerate((weight, *(weight * c for c in couplings))):
                out[n, pl.ds(J * 8, 8), :] = value
            y_before = y


def relaxed(res, matrix):
    at = lambda n, J: matrix[n, pl.ds(J * 8, 8), :]

    def around(v, J):
        return (
            at(1, J) * rolled(v[J], 1, 1)
            + at(2, J) * rolled(v[J], -1, 1)
            + at(3, J) * v[J - 1]
            + at(4, J) * v[J + 1]
            + at(5, J) * rolled(v[J], 1, 0)
            + at(6, J) * rolled(v[J], -1, 0)
        )

    first = {J: at(0, J) * res[J] for J in range(12)}
    second = {J: (2.0 - RELAX) * first[J] + around(first, J) for J in range(1, 11)}
    return [first[J] + (1.0 - RELAX) * second[J] + around(second, J) for J in range(2, 10)]


def coarse_own_kernel(order, near, far, coarse, matrix, send):
    lane = lanes(8)
    lower, upper = sorted_out(near, far, pl.ds(0, 16))
    res = [lower[:8], lower[8:], *(eight(coarse, J) for J in range(8)), upper[:8], upper[8:]]
    done = relaxed(res, matrix)
    d = lax.axis_index("gx")
    odd = lax.rem(d, 2) == 1
    for t in range(4):
        both = jnp.where(lane < 64, done[t], rolled(done[t + 4], 64, 1))
        send[pl.ds(t * 8, 8), :] = jnp.where(odd, rolled(both, 64, 1), both)
    strips = [jnp.zeros((8, NI), F32)] * 2
    for J in range(12):
        at = 16 * (J % 8)
        strip = jnp.where(jnp.logical_and(lane >= at, lane < at + 6), rolled(res[J], at + 1, 1), strips[J // 8])
        strips[J // 8] = jnp.where(jnp.logical_and(lane >= at + 6, lane < at + 12), rolled(res[J], at + 6 - 59, 1), strip)
    turn = lax.rem(10 * d + NI - 1, NI)
    send[pl.ds(32, 8), :] = pltpu.roll(strips[0], turn, 1)
    send[pl.ds(40, 8), :] = pltpu.roll(strips[1], turn, 1)


def coarse_last_kernel(got, coarse, matrix, places, res_out, cor_out, tmp, res_tmp):
    d_own = lax.axis_index("gx")
    lane = lanes(8)
    joint = []
    for J in range(12):
        value = jnp.zeros((8, NI), F32)
        at = (lane - 16 * (J % 8)) & (NI - 1)
        for d in range(GX):
            strip = got[d, pl.ds(32 + 8 * (J // 8), 8), :]
            value = value + jnp.where(jnp.logical_and(at >= 10 * d - 1, at < 10 * d + 11), strip, 0.0)
        joint.append(rolled(value, -16 * (J % 8), 1))
    done = jnp.concatenate(relaxed(joint, matrix), axis=0)
    placed = exact_dot(done, places[...])
    end = jnp.logical_or((lane & 63) < 3, (lane & 63) > 60)
    turn = lax.rem(NI - 10 * d_own, NI)
    for J in range(8):
        mine = pltpu.roll(joint[J + 2], turn, 1)
        mine = jnp.where(lane == 0, mine, jnp.where(lane == 63, rolled(mine, 54, 1), eight(coarse, J)))
        res_tmp[pl.ds(J, 8, stride=8), :] = mine
        rows = pl.ds((J % 4) * 8, 8)
        for m in range(4):
            even, odd = got[2 * m, rows, :], got[2 * m + 1, rows, :]
            if J < 4:
                value = jnp.where(lane < 64, even, odd)
            else:
                value = rolled(jnp.where(lane < 64, odd, even), 64, 1)
            right = placed[J * 8 : J * 8 + 8, m * NI : (m + 1) * NI]
            tmp[m, pl.ds(J, 8, stride=8), :] = jnp.where(end, right, value)
    for m in range(4):
        cor_out[:, pl.ds(m * NI, NI)] = tmp[m]
    res_out[...] = res_tmp[:, :64]


def field_kernel(order, fluxes, yg, ya, yb, field):
    for j in range(NJ):
        place = pl.ds(j * NK, NK)
        field[pl.ds(j, NK, stride=NJ), :] = yg[place, :] - ya[place, :] * fluxes[0] + yb[place, :] * fluxes[1]


def spread(value, axis, count):
    many = jnp.broadcast_to(value[None], (count,) + value.shape)
    return lax.all_to_all(many, axis, split_axis=0, concat_axis=0, tiled=True)


def other_core(value):
    return lax.ppermute(value, "gy", [(n, n ^ 1) for n in range(GY)])


def spread_by_core(value):
    groups = [list(range(0, GY, 2)), list(range(1, GY, 2))]
    many = jnp.broadcast_to(value[None], (CHIPS,) + value.shape)
    return lax.all_to_all(many, "gy", split_axis=0, concat_axis=0, tiled=True, axis_index_groups=groups)


def swap(near, far):
    pairs = [(n, n ^ 1) for n in range(GY)]
    others = [(n, (n + 1) % GY if n % 2 else (n - 1) % GY) for n in range(GY)]
    return lax.ppermute(near, "gy", pairs), lax.ppermute(far, "gy", others)


def body(forcing, pressure_in, x_coupling, y_coupling, z_coupling, damping):
    args = (forcing, pressure_in, x_coupling, y_coupling, z_coupling, damping)
    whole = sds(ROWS, NI)
    kept = sds((2 * len(STEPS) + 1) * ROWS, NI)
    xs, near, far, coef = call(
        first_kernel,
        [sds(6 * ROWS, NI), sds(80, NI), sds(80, NI), sds(128, NI)],
        *[v.reshape(ROWS, NI) for v in args],
        scratch=[(128, NI)],
        hbm=6,
        sems=6,
    )
    mine = near
    near, far = swap(near, far)
    g, a, b, mult, packed = call(x_first_kernel, [whole, whole, whole, kept, sds(NJ, NI)], xs, mine, flops=10**8)
    below, g, a, b, mult, send, *sides = call(
        x_rim_kernel,
        [sds(NK, NI), whole, whole, whole, kept, sds(NJ, NI), sds(48, NI), sds(48, NI), sds(128, NI)],
        xs, near, far, coef, packed, g, a, b, mult,
        aliases={5: 1, 6: 2, 7: 3, 8: 4},
    )
    got = spread(send, "gx", GX)
    yg, ya, yb, yw, yinv, xred, cl, send = call(
        y_first_kernel,
        [whole] * 5 + [sds(3 * GX, NJ, NI), sds(NJ, NI), sds(5 * NK, NI)],
        xs, got, g, a, b,
        scratch=[(GX + 1, NJ, NI), (GX + 1, NJ, NI), (ROWS, NI), (ROWS, NI), (ROWS, NI)],
    )
    theirs = other_core(send)
    share, ext = call(coarse_share_kernel, [sds(32, NI), sds(4 * 96, NI)], *sides, flops=10**7)
    send, joint, inner = call(
        join_first_kernel, [sds(5 * NK, NI), sds(5, NK, NI), sds(NK, NI)], share, send, theirs
    )
    got = spread_by_core(send)
    g, yred, send = call(
        x_again_kernel,
        [whole, sds(3 * CHIPS, NK, NI), sds(40, NI)],
        xs, below, got, joint, inner, share, yg, ya, yb, mult,
        scratch=[(CHIPS + 1, NK, NI), (ROWS, NI), (ROWS, NI)],
    )
    got = spread(send, "gx", GX)
    yg, send = call(
        y_again_kernel,
        [whole, sds(2 * NK, NI)],
        xs, got, g, a, b, xred, cl, yw, yinv,
        scratch=[(GX + 1, NJ, NI), (ROWS, NI), (ROWS, NI)],
    )
    theirs = other_core(send)
    own, ends, places = call(
        coarse_matrix_kernel, [sds(7, 96, NI)] * 2 + [jax.ShapeDtypeStruct((NI, 4 * NI), jnp.bfloat16)], ext, got, flops=10**7
    )
    send, inner = call(join_again_kernel, [sds(2 * NK, NI), sds(NK, NI)], ends, send, theirs, joint)
    got = spread_by_core(send)
    fluxes, coarse, near, far = call(
        residual_kernel,
        [sds(2, NK, NI), sds(64, NI), sds(16, NI), sds(16, NI)],
        xs, below, got, joint, inner, yg, ya, yb, yred, cl,
        scratch=[(CHIPS + 1, NK, NI), (ROWS, NI), (128, NI), (ROWS, NI)],
    )
    mine = near
    near, far = swap(near, far)
    (field,) = call(field_kernel, [whole], mine, fluxes, yg, ya, yb, flops=10**7)
    (send,) = call(coarse_own_kernel, [sds(48, NI)], field, near, far, coarse, own, hbm=1)
    got = spread(send, "gx", GX)
    res, cor = call(
        coarse_last_kernel, [sds(64, 64), sds(64, 4 * NI)], got, coarse, ends, places, scratch=[(4, 64, NI), (64, NI)]
    )
    return field.reshape(NK, NJ, NI), res.reshape(8, 8, 64), cor.reshape(8, 8, 512)


def solution(mesh):
    spec = P(None, "gy", "gx")
    return jax.shard_map(
        body, mesh=mesh, in_specs=(spec,) * 6, out_specs=(spec, spec, P(None, "gy", None)), check_vma=False
    )
```
